128 devices in a mesh: dp: 4 (over y), region: 32 (over z, x, core).
Axes of the slice: x: 4, y: 4, z: 4, core: 2. Of those that a mesh axis runs over, the one named last changes fastest.
Arguments:
- features: bfloat16 [4, 32, 16, 16, 16, 128], P('dp', 'region'), may hold values from -6 to 6
- conv_weight: bfloat16 [3, 3, 3, 128, 128], replicated, may hold values from -0.109375 to 0.109375
- down_weight: bfloat16 [2, 2, 2, 128, 128], replicated, may hold values from -0.1875 to 0.1875
- coarse_cotangent: bfloat16 [4, 32, 16, 16, 16, 128], P('dp', 'region'), may hold values from -6 to 6
- brick_coords: int32 [4, 32, 3], P('dp', 'region'), may hold values from 0 to 31, as said below
- neighbours: int32 [4, 32, 26], P('dp', 'region'), may hold values from -1 to 31, as said below
- parents: int32 [4, 32], P('dp', 'region'), may hold values from 0 to 31, as said below
Outputs:
- coarse_features: bfloat16 [4, 32, 16, 16, 16, 128], P('dp', 'region')
- input_grad: bfloat16 [4, 32, 16, 16, 16, 128], P('dp', 'region')
- conv_grad: float32 [3, 3, 3, 128, 128], replicated
- down_grad: float32 [2, 2, 2, 128, 128], replicated
The draws below stay inside these ranges and needn't reach their ends.
Inputs may be any that keep to these rules, and one draw needn't show every extreme that they name: `brick_coords`: slot s lies on region index s; its first coordinate is s, the second below 4, the third below 2; the coordinates of one scene's slots are distinct. `neighbours`: entry d names the slot whose coordinates are the brick's own plus offset d, or -1 where no slot has them; named slots lie on the same or an adjacent region index, and the relation is symmetric. `parents`: the parent is 2 (x // 2) + (y // 2) of the brick's coordinates; coarse brick c lies on region index c.
All inputs are finite; a program needn't handle non-finite values.
Results may differ from the reference program's by a relative error of at most 0.005.
Values may be sent and summed in bfloat16 or wider, within the bound.
No kernel may reach another device: no remote copies, remote signals or barrier semaphores. Data moves between devices by JAX's collectives and lax.ppermute only.
A program may use at most 192 MiB of HBM per device.

```python
import jax
import jax.numpy as jnp
import numpy as np
from jax import lax

CHANNELS = 128
BRICK = 16
BRICK_DEV = 1
GRID_Y = 4
GRID_Z = 2
SCENES = 4
TOTAL_BRICKS = 32
COARSE = 32
N_REGION = 32


OFFSET_TABLE = np.array([(a, b, c) for a in (-1, 0, 1) for b in (-1, 0, 1) for c in (-1, 0, 1) if (a, b, c) != (0, 0, 0)], dtype=np.int32)


def brick_layout(key):
    keys = jax.random.split(jax.random.fold_in(key, 7), SCENES * N_REGION)
    places = jax.vmap(lambda single: jax.random.permutation(single, GRID_Y * GRID_Z))(keys)[:, :BRICK_DEV]
    places = places.reshape(SCENES, TOTAL_BRICKS).astype(jnp.int32)
    first = jnp.broadcast_to((jnp.arange(TOTAL_BRICKS, dtype=jnp.int32) // BRICK_DEV)[None, :], (SCENES, TOTAL_BRICKS))
    return jnp.stack([first, places // GRID_Z, places % GRID_Z], axis=-1).astype(jnp.int32)


def draw_brick_coords(key, part):
    return brick_layout(key)


def draw_neighbours(key, part):
    coords = brick_layout(key)
    wanted = coords[:, :, None, :] + jnp.asarray(OFFSET_TABLE)[None, None, :, :]
    matches = jnp.all(wanted[:, :, :, None, :] == coords[:, None, None, :, :], axis=-1).astype(jnp.int32)
    labels = jnp.arange(1, TOTAL_BRICKS + 1, dtype=jnp.int32)
    return (jnp.sum(matches * labels, axis=-1) - 1).astype(jnp.int32)


def draw_parents(key, part):
    coords = brick_layout(key)
    return (2 * (coords[:, :, 0] // 2) + coords[:, :, 1] // 2).astype(jnp.int32)


def block_levels(key, extent, cuts, least, high):
    factor_of, own = 1.0, jax.random.fold_in(key, 6)
    for position, shards_of in cuts:
        heights = jnp.exp(jax.random.uniform(jax.random.fold_in(own, position), (shards_of,), jnp.float32, least / len(cuts), high / len(cuts)))
        factor_of = factor_of * jnp.repeat(heights, extent[position] // shards_of).reshape([-1 if axis == position else 1 for axis in range(len(extent))])
    return factor_of


def centred(own_key, shape, deviation, reach, cuts=(), held_as=jnp.bfloat16):
    values = jax.random.normal(own_key, shape, jnp.float32) * deviation
    if len(cuts) > 0:
        values = block_levels(own_key, shape, cuts, -0.22, 0.18) * values
    return jnp.clip(values, min=-reach, max=reach).astype(held_as)


def setup_inputs(seed: int = 0) -> dict:
    key_of = jax.random.split(jax.random.key(seed), 8)
    return {
        "features": centred(key_of[0], (SCENES, TOTAL_BRICKS, BRICK, BRICK, BRICK, CHANNELS), 1.0, 6.0, ((0, 4), (1, 32))),
        "conv_weight": centred(key_of[1], (3, 3, 3, CHANNELS, CHANNELS), (27 * CHANNELS) ** -0.5, 0.109375),
        "down_weight": centred(key_of[2], (2, 2, 2, CHANNELS, CHANNELS), (8 * CHANNELS) ** -0.5, 0.1875),
        "coarse_cotangent": centred(key_of[3], (SCENES, COARSE, BRICK, BRICK, BRICK, CHANNELS), 1.0, 6.0, ((0, 4), (1, 32))),
        "brick_coords": draw_brick_coords(jax.random.fold_in(key_of[7], 71), 0),
        "neighbours": draw_neighbours(jax.random.fold_in(key_of[7], 71), 0),
        "parents": draw_parents(jax.random.fold_in(key_of[7], 71), 0),
    }


OFFSETS = [(a, b, c) for a in (-1, 0, 1) for b in (-1, 0, 1) for c in (-1, 0, 1) if (a, b, c) != (0, 0, 0)]
loss_scale = 1024.0


def source_cut(offset, brick_edge):
    if offset < 0:
        return slice(brick_edge - 1, brick_edge)
    if offset == 0:
        return slice(0, brick_edge)
    return slice(0, 1)


def pad_bricks(center, fetcher, present):
    pieces = {}
    for number, (a, b, c) in enumerate(OFFSETS):
        section = fetcher(number, a, b, c)
        keeper = present[:, number].reshape(-1, 1, 1, 1, 1)
        pieces[(a, b, c)] = jnp.where(keeper, section, jnp.zeros_like(section))
    pieces[(0, 0, 0)] = center
    slabs = []
    for a in (-1, 0, 1):
        rows = []
        for b in (-1, 0, 1):
            rows.append(jnp.concatenate([pieces[(a, b, c)] for c in (-1, 0, 1)], axis=3))
        slabs.append(jnp.concatenate(rows, axis=2))
    return jnp.concatenate(slabs, axis=1)


def tap_windows(padded, a):
    brick_edge, channels = padded.shape[1] - 2, padded.shape[-1]
    parts = [padded[:, a:a + brick_edge, b:b + brick_edge, c:c + brick_edge] for b in range(3) for c in range(3)]
    return jnp.concatenate(parts, axis=-1).reshape(-1, 9 * channels)


def conv_bricks(padded, kernel):
    brick_count, brick_edge, channels = padded.shape[0], padded.shape[1] - 2, padded.shape[-1]
    summed = jnp.zeros((brick_count * brick_edge ** 3, kernel.shape[-1]), jnp.float32)
    for a in range(3):
        window = tap_windows(padded, a)
        summed = summed + jnp.dot(window, kernel[a].reshape(9 * channels, -1), preferred_element_type=jnp.float32)
    return summed.reshape(brick_count, brick_edge, brick_edge, brick_edge, -1)


def kernel_grads(padded, grads):
    channels = padded.shape[-1]
    flat_grads = grads.reshape(-1, grads.shape[-1])
    result = []
    for a in range(3):
        window = tap_windows(padded, a)
        result.append(lax.dot_general(window, flat_grads, (((0,), (0,)), ((), ())), preferred_element_type=jnp.float32).reshape(3, 3, channels, -1))
    return jnp.stack(result)


def padded_scene(field, neighbours):
    brick_edge = field.shape[1]
    present = neighbours >= 0
    indices = jnp.where(present, neighbours, 0).astype(jnp.int32)

    def fetcher(number, a, b, c):
        return field[:, source_cut(a, brick_edge), source_cut(b, brick_edge), source_cut(c, brick_edge)][indices[:, number]]

    return pad_bricks(field, fetcher, present)


def reference(features, conv_weight, down_weight, coarse_cotangent, brick_coords, neighbours, parents):
    brick_edge, channels = features.shape[2], features.shape[-1]
    half_edge = brick_edge // 2
    brick_count = features.shape[1]
    coarse_count = coarse_cotangent.shape[1]
    flipped = jnp.swapaxes(jnp.flip(conv_weight, (0, 1, 2)), 3, 4)
    conv_total = jnp.zeros((3, 3, 3, channels, channels), jnp.float32)
    down_total = jnp.zeros((2, 2, 2, channels, channels), jnp.float32)
    coarse_list = []
    grad_list = []
    for scene in range(features.shape[0]):
        field = features[scene]
        padded = padded_scene(field, neighbours[scene])
        outputs = (conv_bricks(padded, conv_weight) + field.astype(jnp.float32)).astype(jnp.bfloat16)
        fine_split = outputs.reshape(brick_count, half_edge, 2, half_edge, 2, half_edge, 2, channels).astype(jnp.float32)
        blocks = jnp.einsum("bixjykzc,xyzcd->bijkd", fine_split, down_weight.astype(jnp.float32)).astype(jnp.bfloat16)
        coords = brick_coords[scene]
        octant = (coords[:, 0] % 2) * 4 + (coords[:, 1] % 2) * 2 + coords[:, 2] % 2
        targets = (parents[scene] * 8 + octant).astype(jnp.int32)
        coarse = jnp.zeros((coarse_count * 8, half_edge, half_edge, half_edge, channels), jnp.float32)
        coarse = coarse.at[targets].add(blocks.astype(jnp.float32))
        coarse = coarse.reshape(coarse_count, 2, 2, 2, half_edge, half_edge, half_edge, channels)
        coarse = coarse.transpose(0, 1, 4, 2, 5, 3, 6, 7).reshape(coarse_count, brick_edge, brick_edge, brick_edge, channels)
        coarse_list.append(coarse.astype(jnp.bfloat16))
        cotangent = coarse_cotangent[scene].reshape(coarse_count, 2, half_edge, 2, half_edge, 2, half_edge, channels)
        cotangent = cotangent.transpose(0, 1, 3, 5, 2, 4, 6, 7).reshape(coarse_count * 8, half_edge, half_edge, half_edge, channels)
        chosen = cotangent[targets]
        grad_outputs = jnp.einsum("bijkd,xyzcd->bixjykzc", chosen.astype(jnp.float32), down_weight.astype(jnp.float32))
        grad_outputs = grad_outputs.reshape(brick_count, brick_edge, brick_edge, brick_edge, channels).astype(jnp.bfloat16)
        down_total = down_total + jnp.einsum("bixjykzc,bijkd->xyzcd", fine_split, chosen.astype(jnp.float32))
        padded_back = padded_scene(grad_outputs, neighbours[scene])
        input_grad = grad_outputs.astype(jnp.float32) + conv_bricks(padded_back, flipped)
        grad_list.append(input_grad.astype(jnp.bfloat16))
        conv_total = conv_total + kernel_grads(padded, grad_outputs)
    return (jnp.stack(coarse_list), jnp.stack(grad_list), conv_total / loss_scale, down_total / loss_scale)
```

```python
import functools
import jax
import jax.numpy as jnp
from jax import lax
from jax.experimental import pallas as pl
from jax.experimental.pallas import tpu as pltpu
from jax.sharding import PartitionSpec as P

BF, F32 = jnp.bfloat16, jnp.float32
SMEM = pl.BlockSpec(memory_space=pltpu.SMEM)
VMEM = pl.BlockSpec(memory_space=pltpu.VMEM)
NN = (((1,), (0,)), ((), ()))
NT = (((1,), (1,)), ((), ()))
TN = (((0,), (0,)), ((), ()))


def dot(lhs, rhs, dims):
    return lax.dot_general(lhs, rhs, dims, preferred_element_type=F32)


def z_index(rows):
    return lax.broadcasted_iota(jnp.int32, (rows, 128), 0) % 16


def lay_interior(field_ref, shifts_ref):
    z = z_index(256)

    @pl.loop(0, 16)
    def _(x):
        plain = field_ref[x].reshape(256, 128)
        wide = plain.astype(F32)
        lower = jnp.where(z == 0, 0.0, pltpu.roll(wide, 1, 0)).astype(BF)
        upper = jnp.where(z == 15, 0.0, pltpu.roll(wide, 255, 0)).astype(BF)
        for c, value in enumerate((lower, plain, upper)):
            rows = value.reshape(8, 2, 16, 128)
            shifts_ref[c, x + 1, 0:8, 1] = rows[:, 0]
            shifts_ref[c, x + 1, 1:9, 0] = rows[:, 1]
            shifts_ref[c, x + 1, 0, 0] = jnp.zeros((16, 128), BF)
            shifts_ref[c, x + 1, 8, 1] = jnp.zeros((16, 128), BF)


def lay_slab(layer, flag, shifts_ref, place):
    def three(value, b):
        rows = value.shape[0] * 16
        wide = value.astype(F32).reshape(rows, 128)
        z = z_index(rows)
        below, same, above = (flag(b, c) for c in (-1, 0, 1))
        lower = jnp.where(
            z == 0, pltpu.roll(wide, rows - 15, 0) * below, pltpu.roll(wide, 1, 0) * same
        )
        upper = jnp.where(
            z == 15, pltpu.roll(wide, 15, 0) * above, pltpu.roll(wide, rows - 1, 0) * same
        )
        return [v.astype(BF) for v in (lower, wide * same, upper)]

    for c, value in enumerate(three(layer, 0)):
        rows = value.reshape(8, 2, 16, 128)
        shifts_ref[c, place, 0:8, 1] = rows[:, 0]
        shifts_ref[c, place, 1:9, 0] = rows[:, 1]
    for c, value in enumerate(three(layer[15:16], -1)):
        shifts_ref[c, place, 0, 0] = value
    for c, value in enumerate(three(layer[0:1], 1)):
        shifts_ref[c, place, 8, 1] = value


def lay_field(field_ref, low_ref, high_ref, near_ref, shifts_ref):
    def flag(first):
        return lambda b, c: (near_ref[first + 3 * (b + 1) + c + 1] >= 0).astype(F32)

    lay_slab(low_ref[...], flag(0), shifts_ref, 0)
    lay_slab(high_ref[...], flag(17), shifts_ref, 17)
    lay_interior(field_ref, shifts_ref)


def window(shifts_ref, c, x, count):
    return jnp.concatenate(
        [
            shifts_ref[c, pl.ds(x, count), t // 2 : t // 2 + 8, t % 2].reshape(count * 128, 128)
            for t in range(4)
        ],
        axis=1,
    )


def grad_kernel(coords_ref, parent_ref, own_ref, other_ref, down_ref, grads_ref, spread_ref, wide_ref):
    x, y, z = coords_ref[0], coords_ref[1], coords_ref[2]
    oy, oz = y % 2, z % 2
    is_own = parent_ref[0] == x
    wide_ref[...] = jnp.zeros_like(wide_ref)
    for i in range(8):
        mine = own_ref[8 * (x % 2) + i, pl.ds(8 * oy, 8)].astype(F32)
        theirs = other_ref[i, pl.ds(8 * oy, 8)].astype(F32)
        both = jnp.where(is_own, mine, theirs)
        part = jnp.where(oz == 0, both[:, 0:8], both[:, 8:16]).reshape(64, 128)
        wide_ref[i, pl.ds(0, 64, stride=2), :] = part
    weights = jnp.concatenate(
        [
            jnp.concatenate([down_ref[p, q, r] for r in range(2)], axis=1)
            for p in range(2)
            for q in range(2)
        ],
        axis=0,
    )
    for i in range(8):
        even = wide_ref[i]
        spread = jnp.concatenate([even, pltpu.roll(even, 1, 0)], axis=1).astype(BF)
        spread_ref[i] = spread
        grads = dot(spread, weights, NT).astype(BF)
        for p in range(2):
            for q in range(2):
                at = (2 * p + q) * 128
                grads_ref[2 * i + p, :, q] = grads[:, at : at + 128].reshape(8, 16, 128)


def main_kernel(
    coords_ref, parent_ref, near_ref, field_ref, low_ref, high_ref, conv_ref, down_ref, grads_ref,
    spread_ref, keep_ref, send_ref, kept_rows_ref, sent_rows_ref,
    shifts_ref, weights_ref, outputs_ref, sums_ref, *, tile=4,
):
    x, y, z = coords_ref[0], coords_ref[1], coords_ref[2]
    first_core = x % 2 == 0

    def part_rows(tap, rows):
        kept_rows_ref[tap] = jnp.where(first_core, rows[0:64], rows[64:128])
        sent_rows_ref[tap] = jnp.where(first_core, rows[64:128], rows[0:64]).astype(BF)

    kept_rows_ref[35] = jnp.zeros((64, 128), F32)
    sent_rows_ref[35] = jnp.zeros((64, 128), BF)
    lay_field(field_ref, low_ref, high_ref, near_ref, shifts_ref)
    zero = jnp.zeros((128, 128), BF)
    for a in range(3):
        for c in range(3):
            for t in range(4):
                for s in range(2):
                    weights_ref[a, c, t * 128 : t * 128 + 128, s * 128 : s * 128 + 128] = (
                        conv_ref[a, t - s, c] if 0 <= t - s <= 2 else zero
                    )
    down = jnp.concatenate(
        [
            jnp.concatenate([down_ref[p, q, r] for r in range(2)], axis=1)
            for p in range(2)
            for q in range(2)
        ],
        axis=0,
    )
    if True:
        keep_ref[...] = jnp.zeros_like(keep_ref)
        send_ref[...] = jnp.zeros_like(send_ref)
        kept = (parent_ref[0] == x).astype(F32)
        oy, oz = y % 2, z % 2

        @pl.loop(0, 16 // tile)
        def _(step):
            first = step * tile
            acc = None
            for a in range(3):
                for c in range(3):
                    part = dot(window(shifts_ref, c, first + a, tile), weights_ref[a, c], NN)
                    acc = part if acc is None else acc + part
            for s in range(2):
                field = field_ref[pl.ds(first, tile), :, s].astype(F32)
                outputs_ref[pl.ds(first, tile), :, s] = (
                    acc[:, s * 128 : s * 128 + 128].reshape(tile, 8, 16, 128) + field
                ).astype(BF)
            half = tile // 2
            corners = jnp.concatenate(
                [
                    jnp.concatenate(
                        [outputs_ref[first + 2 * i + p, :, q].reshape(128, 128) for i in range(half)], axis=0
                    )
                    for p in range(2)
                    for q in range(2)
                ],
                axis=1,
            )
            sums = dot(corners, down, NN)
            sums_ref[0] = sums[:, 0:128]
            sums_ref[1] = sums[:, 128:256]
            rows = half * 64
            block = sums_ref[0, pl.ds(0, rows, stride=2), :] + sums_ref[1, pl.ds(1, rows, stride=2), :]
            block = block.reshape(half * 8, 8, 128)
            none = jnp.zeros_like(block)
            low = jnp.where(oz == 0, block, none)
            high = jnp.where(oz == 0, none, block)
            placed = jnp.concatenate([low, high], axis=1).reshape(half, 8, 16, 128)
            keep_ref[pl.ds(step * half, half), pl.ds(8 * oy, 8)] = (placed * kept).astype(BF)
            send_ref[pl.ds(step * half, half), pl.ds(8 * oy, 8)] = (placed * (1 - kept)).astype(BF)

    if True:
        spread = spread_ref[...].reshape(1024, 256)
        for p in range(2):
            for q in range(2):
                corner = jnp.concatenate(
                    [outputs_ref[2 * i + p, :, q].reshape(128, 128) for i in range(8)], axis=0
                )
                result = dot(corner, spread, TN) * (1.0 / 1024)
                part_rows(27 + 4 * p + 2 * q, result[:, 0:128])
                part_rows(28 + 4 * p + 2 * q, result[:, 128:256])

    if True:
        pair = jnp.concatenate([grads_ref[:, :, s].reshape(2048, 128) for s in range(2)], axis=1)
        for c in range(3):
            @pl.loop(0, 3)
            def _(a):
                result = dot(window(shifts_ref, c, a, 16), pair, TN) * (1.0 / 1024)
                for b in range(3):
                    part_rows(
                        9 * a + 3 * b + c,
                        result[b * 128 : b * 128 + 128, 0:128]
                        + result[b * 128 + 128 : b * 128 + 256, 128:256],
                    )


def input_kernel(near_ref, field_ref, low_ref, high_ref, conv_ref, result_ref, shifts_ref, weights_ref, *, tile=4):
    lay_field(field_ref, low_ref, high_ref, near_ref, shifts_ref)
    zero = jnp.zeros((128, 128), BF)
    for a in range(3):
        for c in range(3):
            for t in range(4):
                for s in range(2):
                    weights_ref[a, c, s * 128 : s * 128 + 128, t * 128 : t * 128 + 128] = (
                        conv_ref[2 - a, 2 - t + s, 2 - c] if 0 <= t - s <= 2 else zero
                    )

    @pl.loop(0, 16 // tile)
    def _(step):
        first = step * tile
        acc = None
        for a in range(3):
            for c in range(3):
                part = dot(window(shifts_ref, c, first + a, tile), weights_ref[a, c], NT)
                acc = part if acc is None else acc + part
        for s in range(2):
            field = field_ref[pl.ds(first, tile), :, s].astype(F32)
            result_ref[pl.ds(first, tile), :, s] = (
                acc[:, s * 128 : s * 128 + 128].reshape(tile, 8, 16, 128) + field
            ).astype(BF)


def coarse_kernel(coords_ref, keep_ref, got_ref, coarse_ref):
    upper = coords_ref[0] % 2
    coarse_ref[pl.ds(8 * upper, 8)] = keep_ref[...]
    coarse_ref[pl.ds(8 * (1 - upper), 8)] = got_ref[...]


PARAMS = dict(compiler_params=pltpu.CompilerParams(vmem_limit_bytes=60 * 2**20))
sds = jax.ShapeDtypeStruct


def call(kernel, ins, outs, scratch=(), flops=0, moved=4 << 20):
    return pl.pallas_call(
        kernel,
        in_specs=ins,
        out_specs=[VMEM] * len(outs),
        out_shape=outs,
        scratch_shapes=list(scratch),
        cost_estimate=pl.CostEstimate(flops=flops, bytes_accessed=moved, transcendentals=0),
        **PARAMS,
    )


def grad_call(coords, parent, own, other, down):
    return call(
        grad_kernel, [SMEM] * 2 + [VMEM] * 3,
        [sds((16, 8, 2, 16, 128), BF), sds((8, 128, 256), BF)],
        [pltpu.VMEM((8, 128, 128), F32)], flops=2 * 2**27,
    )(coords, parent, own, other, down)


def main_call(coords, parent, near, field, low, high, conv, down, grads, spread, **kw):
    tile = kw.get("tile", 4)
    return call(
        functools.partial(main_kernel, **kw), [SMEM] * 3 + [VMEM] * 7,
        [sds((8, 16, 16, 128), BF)] * 2 + [sds((36, 64, 128), F32), sds((36, 64, 128), BF)],
        [pltpu.VMEM((3, 18, 9, 2, 16, 128), BF), pltpu.VMEM((3, 3, 512, 256), BF),
         pltpu.VMEM((16, 8, 2, 16, 128), BF), pltpu.VMEM((2, 64 * tile, 128), F32)], flops=2 * 9 * 2048 * 512 * 256 * 2,
    )(coords, parent, near, field, low, high, conv, down, grads, spread)


def input_call(near, field, low, high, conv, **kw):
    return call(
        functools.partial(input_kernel, **kw), [SMEM] + [VMEM] * 4, [sds((16, 8, 2, 16, 128), BF)],
        [pltpu.VMEM((3, 18, 9, 2, 16, 128), BF), pltpu.VMEM((3, 3, 256, 512), BF)], flops=2 * 9 * 2048 * 512 * 256,
    )(near, field, low, high, conv)[0]


def coarse_call(coords, keep, got):
    return call(coarse_kernel, [SMEM] + [VMEM] * 2, [sds((16, 16, 16, 128), BF)])(coords, keep, got)[0]


def spread_rows(coords_ref, y_ref, kept_ref, got_ref, own_ref, *send_refs):
    for k, ref in enumerate((own_ref, *send_refs)):
        at = pl.multiple_of(16 * ((y_ref[0] + k) % 4), 16)
        rows = kept_ref[:, pl.ds(at, 16)] + got_ref[:, pl.ds(at, 16)].astype(F32)
        ref[...] = rows.astype(ref.dtype)


def spread_taps(coords_ref, y_ref, kept_ref, *refs):
    got_refs, out_refs = refs[:3], refs[3:]
    x = (coords_ref[0] // 2) % 4
    for k, ref in enumerate(out_refs):
        taps = pl.ds(9 * ((x + k) % 4), 9)
        total = kept_ref[taps]
        for got_ref in got_refs:
            total = total + got_ref[taps].astype(F32)
        ref[...] = total.astype(ref.dtype)


def add_up(coords_ref, y_ref, kept_ref, first_ref, second_ref, third_ref, total_ref):
    total_ref[...] = kept_ref[...] + first_ref[...] + second_ref[...] + third_ref[...]


def add_in_order(coords_ref, y_ref, own_ref, *refs):
    z = coords_ref[0] // 8
    slots_ref, total_ref = refs[4], refs[3]
    for k, ref in enumerate((own_ref, *refs[:3])):
        slots_ref[(z - k + 4) % 4] = ref[...]
    total_ref[...] = ((slots_ref[0] + slots_ref[1]) + (slots_ref[2] + slots_ref[3])).astype(BF)


def join_taps(coords_ref, y_ref, own_ref, *refs):
    x = (coords_ref[0] // 2) % 4
    for k, ref in enumerate((own_ref, *refs[:3])):
        refs[3][pl.ds(9 * ((x - k + 4) % 4), 9)] = ref[...]


def join_rows(coords_ref, y_ref, own_ref, *refs):
    for k, ref in enumerate((own_ref, *refs[:3])):
        at = pl.multiple_of(16 * ((y_ref[0] - k + 4) % 4), 16)
        refs[3][:, pl.ds(at, 16)] = ref[...]


def finish(coords_ref, y_ref, own_ref, got_ref, conv_ref, down_ref):
    core = coords_ref[0] % 2
    mine = pl.ds(pl.multiple_of(64 * core, 64), 64)
    theirs = pl.ds(pl.multiple_of(64 * (1 - core), 64), 64)
    conv_ref[:, mine] = own_ref[0:27].astype(F32)
    conv_ref[:, theirs] = got_ref[0:27].astype(F32)
    down_ref[:, mine] = own_ref[27:35].astype(F32)
    down_ref[:, theirs] = got_ref[27:35].astype(F32)


def ring(size, step, by):
    return [(i, i - i // step % size * step + (i // step + by) % size * step) for i in range(32)]


def over_core(value):
    return lax.ppermute(value, "region", [(i, i ^ 1) for i in range(32)])


def over_x(value, by):
    return lax.ppermute(value, "region", ring(4, 2, by))


def over_z(value, by):
    return lax.ppermute(value, "region", ring(4, 8, by))


def over_y(value, by):
    return lax.ppermute(value, "dp", [(i, (i + by) % 4) for i in range(4)])


def summed(kept, sent, coords, y):
    def run(kernel, values, outs, scratch=()):
        return call(kernel, [SMEM] * 2 + [VMEM] * len(values), outs, scratch)(coords, y, *values)

    got = over_core(sent)
    own, *sends = run(
        spread_rows, (kept, got), [sds((36, 16, 128), F32)] + [sds((36, 16, 128), BF)] * 3
    )
    gots = [over_y(v, k + 1) for k, v in enumerate(sends)]
    own, *sends = run(spread_taps, (own, *gots), [sds((9, 16, 128), F32)] * 4)
    gots = [over_x(v, k + 1) for k, v in enumerate(sends)]
    own = run(add_up, (own, *gots), [sds((9, 16, 128), F32)])[0]
    gots = [over_z(own, k) for k in (1, 2, 3)]
    own = run(
        add_in_order, (own, *gots), [sds((9, 16, 128), BF)], [pltpu.VMEM((4, 9, 16, 128), F32)]
    )[0]
    gots = [over_x(own, k) for k in (1, 2, 3)]
    own = run(join_taps, (own, *gots), [sds((36, 16, 128), BF)])[0]
    gots = [over_y(own, k) for k in (1, 2, 3)]
    own = run(join_rows, (own, *gots), [sds((36, 64, 128), BF)])[0]
    got = over_core(own)
    return run(finish, (own, got), [sds((27, 128, 128), F32), sds((8, 128, 128), F32)])


def halo(field):
    low = lax.ppermute(field[15], "region", [(i, i + 1) for i in range(31)])
    high = lax.ppermute(field[0], "region", [(i + 1, i) for i in range(31)])
    return low, high


def local(features, conv_weight, down_weight, coarse_cotangent, brick_coords, neighbours, parents):
    coords, near, parent = brick_coords.reshape(3), neighbours.reshape(26), parents.reshape(1)
    y = lax.axis_index("dp").reshape(1).astype(jnp.int32)
    core = lax.axis_index("region") % 2
    cotangent = coarse_cotangent.reshape(16, 16, 16, 128)
    theirs = over_core(lax.dynamic_slice_in_dim(cotangent, 8 * (1 - core), 8))
    field = features.reshape(16, 8, 2, 16, 128)
    low, high = halo(features.reshape(16, 16, 16, 128))
    grads, spread = grad_call(coords, parent, cotangent, theirs, down_weight)
    grads_low, grads_high = halo(grads.reshape(16, 16, 16, 128))
    keep, send, kept, sent = main_call(
        coords, parent, near, field, low, high, conv_weight, down_weight, grads, spread
    )
    conv_grad, down_grad = summed(kept, sent, coords, y)
    got = over_core(send)
    input_grad = input_call(near, grads, grads_low, grads_high, conv_weight)
    coarse = coarse_call(coords, keep, got)
    whole = (1, 1, 16, 16, 16, 128)
    return (
        coarse.reshape(whole),
        input_grad.reshape(whole),
        conv_grad.reshape(3, 3, 3, 128, 128),
        down_grad.reshape(2, 2, 2, 128, 128),
    )


def solution(mesh):
    bricks = P("dp", "region", None, None, None, None)
    return jax.shard_map(
        local,
        mesh=mesh,
        in_specs=(bricks, P(), P(), bricks, P("dp", "region", None), P("dp", "region", None), P("dp", "region")),
        out_specs=(bricks, bricks, P(), P()),
        check_vma=False,
    )
```

```python
import functools
import jax
import jax.numpy as jnp
from jax import lax
from jax.experimental import pallas as pl
from jax.experimental.pallas import tpu as pltpu
from jax.sharding import PartitionSpec as P

BF, F32 = jnp.bfloat16, jnp.float32
SMEM = pl.BlockSpec(memory_space=pltpu.SMEM)
VMEM = pl.BlockSpec(memory_space=pltpu.VMEM)
NN = (((1,), (0,)), ((), ()))
NT = (((1,), (1,)), ((), ()))
TN = (((0,), (0,)), ((), ()))


def dot(lhs, rhs, dims):
    return lax.dot_general(lhs, rhs, dims, preferred_element_type=F32)


def z_index(rows):
    return lax.broadcasted_iota(jnp.int32, (rows, 128), 0) % 16


def lay_interior(field_ref, shifts_ref, start=0, stop=16, base=1):
    z = z_index(256)

    @pl.loop(start, stop)
    def _(x):
        plain = field_ref[x].reshape(256, 128)
        wide = plain.astype(F32)
        lower = jnp.where(z == 0, 0.0, pltpu.roll(wide, 1, 0)).astype(BF)
        upper = jnp.where(z == 15, 0.0, pltpu.roll(wide, 255, 0)).astype(BF)
        for c, value in enumerate((lower, plain, upper)):
            rows = value.reshape(8, 2, 16, 128)
            shifts_ref[c, x + base, 0:8, 1] = rows[:, 0]
            shifts_ref[c, x + base, 1:9, 0] = rows[:, 1]
            shifts_ref[c, x + base, 0, 0] = jnp.zeros((16, 128), BF)
            shifts_ref[c, x + base, 8, 1] = jnp.zeros((16, 128), BF)


def lay_slab(layer, flag, slab_ref):
    def three(value, b):
        rows = value.shape[0] * 16
        wide = value.astype(F32).reshape(rows, 128)
        z = z_index(rows)
        below, same, above = (flag(b, c) for c in (-1, 0, 1))
        lower = jnp.where(
            z == 0, pltpu.roll(wide, rows - 15, 0) * below, pltpu.roll(wide, 1, 0) * same
        )
        upper = jnp.where(
            z == 15, pltpu.roll(wide, 15, 0) * above, pltpu.roll(wide, rows - 1, 0) * same
        )
        return [v.astype(BF) for v in (lower, wide * same, upper)]

    for c, value in enumerate(three(layer, 0)):
        rows = value.reshape(8, 2, 16, 128)
        slab_ref[c, 0:8, 1] = rows[:, 0]
        slab_ref[c, 1:9, 0] = rows[:, 1]
    for c, value in enumerate(three(layer[15:16], -1)):
        slab_ref[c, 0, 0] = value.reshape(16, 128)
    for c, value in enumerate(three(layer[0:1], 1)):
        slab_ref[c, 8, 1] = value.reshape(16, 128)


def near_flag(near_ref, first):
    return lambda b, c: (near_ref[first + 3 * (b + 1) + c + 1] >= 0).astype(F32)


def window(shifts_ref, c, x, count):
    return jnp.concatenate(
        [
            shifts_ref[c, pl.ds(x, count), t // 2 : t // 2 + 8, t % 2].reshape(count * 128, 128)
            for t in range(4)
        ],
        axis=1,
    )


def joined_down(down_ref):
    return jnp.concatenate(
        [
            jnp.concatenate([down_ref[p, q, r] for r in range(2)], axis=1)
            for p in range(2)
            for q in range(2)
        ],
        axis=0,
    )


def grad_kernel(
    coords_ref, parent_ref, own_ref, other_ref, down_ref, field_ref,
    grads_ref, spread_ref, up_ref, back_ref, wide_ref, sems,
):
    last = pltpu.make_async_copy(field_ref.at[15], up_ref.at[0], sems.at[0])
    first = pltpu.make_async_copy(field_ref.at[0], back_ref.at[0], sems.at[1])
    last.start()
    first.start()
    x, oy, oz = coords_ref[0], coords_ref[1] % 2, coords_ref[2] % 2
    is_own = parent_ref[0] == x
    down = joined_down(down_ref)
    wide_ref[...] = jnp.zeros_like(wide_ref)
    for i in range(8):
        mine = own_ref[8 * (x % 2) + i, pl.ds(8 * oy, 8)].astype(F32)
        theirs = other_ref[i, pl.ds(8 * oy, 8)].astype(F32)
        both = jnp.where(is_own, mine, theirs)
        part = jnp.where(oz == 0, both[:, 0:8], both[:, 8:16]).reshape(64, 128)
        wide_ref[i, pl.ds(0, 64, stride=2), :] = part
    for i in range(8):
        even = wide_ref[i]
        spread = jnp.concatenate([even, pltpu.roll(even, 1, 0)], axis=1).astype(BF)
        spread_ref[i] = spread
        grads = dot(spread, down, NT).astype(BF)
        for p in range(2):
            for q in range(2):
                at = (2 * p + q) * 128
                part = grads[:, at : at + 128].reshape(8, 16, 128)
                grads_ref[2 * i + p, :, q] = part
                if 2 * i + p == 15:
                    up_ref[1, :, q] = part
                if 2 * i + p == 0:
                    back_ref[1, :, q] = part
    last.wait()
    first.wait()


def lay_weights(conv_ref, weights_ref):
    zero = jnp.zeros((128, 128), BF)
    for a in range(3):
        for c in range(3):
            for t in range(4):
                for s in range(2):
                    weights_ref[a, c, t * 128 : t * 128 + 128, s * 128 : s * 128 + 128] = (
                        conv_ref[a, t - s, c] if 0 <= t - s <= 2 else zero
                    )


def inner_kernel(field_ref, conv_ref, shifts_ref, weights_ref, outputs_ref):
    lay_interior(field_ref, shifts_ref, 0, 16, 0)
    lay_weights(conv_ref, weights_ref)
    for first, count in ((1, 7), (8, 7)):
        acc = None
        for a in range(3):
            for c in range(3):
                part = dot(window(shifts_ref, c, first + a - 1, count), weights_ref[a, c], NN)
                acc = part if acc is None else acc + part
        for s in range(2):
            field = field_ref[first : first + count, :, s].astype(F32)
            outputs_ref[first : first + count, :, s] = (
                acc[:, s * 128 : s * 128 + 128].reshape(count, 8, 16, 128) + field
            ).astype(BF)


def taps(rows):
    return jnp.concatenate(
        [rows[t // 2 : t // 2 + 8, t % 2].reshape(128, 128) for t in range(4)], axis=1
    )


def main_kernel(
    coords_ref, parent_ref, near_ref, field_ref, low_ref, high_ref, shifts_ref, weights_ref,
    inner_ref, down_ref, grads_ref, spread_ref,
    kept_rows_ref, sent_ref, keep_ref, low_shifts_ref, high_shifts_ref, edges_ref, sums_ref,
):
    x, oy, oz = coords_ref[0], coords_ref[1] % 2, coords_ref[2] % 2
    first_core = x % 2 == 0
    kept = (parent_ref[0] == x).astype(F32)

    def part_rows(tap, rows):
        kept_rows_ref[tap] = jnp.where(first_core, rows[0:64], rows[64:128])
        sent_ref[tap] = jnp.where(first_core, rows[64:128], rows[0:64]).astype(BF)

    kept_rows_ref[35] = jnp.zeros((64, 128), F32)
    sent_ref[35] = jnp.zeros((64, 128), BF)
    sent_ref[52] = jnp.full((64, 128), oy, jnp.int32).astype(F32).astype(BF)
    lay_slab(low_ref[0].reshape(16, 16, 128), near_flag(near_ref, 0), low_shifts_ref)
    lay_slab(high_ref[0].reshape(16, 16, 128), near_flag(near_ref, 17), high_shifts_ref)

    acc = None
    for a in range(3):
        for c in range(3):
            below = taps(low_shifts_ref[c] if a == 0 else shifts_ref[c, a - 1])
            above = taps(high_shifts_ref[c] if a == 2 else shifts_ref[c, 14 + a])
            part = dot(jnp.concatenate([below, above], axis=0), weights_ref[a, c], NN)
            acc = part if acc is None else acc + part
    for s in range(2):
        for k in range(2):
            value = acc[128 * k : 128 * k + 128, s * 128 : s * 128 + 128].reshape(8, 16, 128)
            edges_ref[k, :, s] = (value + field_ref[15 * k, :, s].astype(F32)).astype(BF)

    down = joined_down(down_ref)

    def corner(i, p, q):
        at = 2 * i + p
        rows = edges_ref[at // 15, :, q] if at in (0, 15) else inner_ref[at, :, q]
        return rows.reshape(128, 128)

    for i in range(8):
        corners = jnp.concatenate([corner(i, p, q) for p in range(2) for q in range(2)], axis=1)
        sums = dot(corners, down, NN)
        sums_ref[i, 0] = sums[:, 0:128]
        sums_ref[i, 1] = sums[:, 128:256]
        block = sums_ref[i, 0, pl.ds(0, 64, stride=2), :] + sums_ref[i, 1, pl.ds(1, 64, stride=2), :]
        block = block.reshape(8, 8, 128)
        none = jnp.zeros_like(block)
        low = jnp.where(oz == 0, block, none)
        high = jnp.where(oz == 0, none, block)
        placed = jnp.concatenate([low, high], axis=1).reshape(128, 128)
        keep_ref[i] = (placed * kept).astype(BF).reshape(8, 16, 128)
        away = (placed * (1 - kept)).astype(BF)
        sent_ref[36 + 2 * i] = away[0:64]
        sent_ref[37 + 2 * i] = away[64:128]

    spread = spread_ref[...].reshape(1024, 256)
    for p in range(2):
        for q in range(2):
            rows = jnp.concatenate([corner(i, p, q) for i in range(8)], axis=0)
            result = dot(rows, spread, TN) * (1.0 / 1024)
            part_rows(27 + 4 * p + 2 * q, result[:, 0:128])
            part_rows(28 + 4 * p + 2 * q, result[:, 128:256])

    pair = jnp.concatenate([grads_ref[:, :, s].reshape(2048, 128) for s in range(2)], axis=1)
    for a in range(3):
        for c in range(3):
            if a == 0:
                rows = jnp.concatenate(
                    [taps(low_shifts_ref[c]), window(shifts_ref, c, 0, 15)], axis=0
                )
            elif a == 1:
                rows = window(shifts_ref, c, 0, 16)
            else:
                rows = jnp.concatenate(
                    [window(shifts_ref, c, 1, 15), taps(high_shifts_ref[c])], axis=0
                )
            result = dot(rows, pair, TN) * (1.0 / 1024)
            for b in range(3):
                part_rows(
                    9 * a + 3 * b + c,
                    result[b * 128 : b * 128 + 128, 0:128]
                    + result[b * 128 + 128 : b * 128 + 256, 128:256],
                )


def input_kernel(near_ref, field_ref, layer_ref, conv_ref, *refs, half, tile=4):
    result_ref, token_ref, shifts_ref, weights_ref, held_ref, sems = refs[-6:]
    token_ref[...] = jnp.zeros_like(token_ref)
    if half == 0:
        lay_slab(layer_ref[1].reshape(16, 16, 128), near_flag(near_ref, 0), shifts_ref.at[:, 0])
        lay_interior(field_ref, shifts_ref, 0, 9, 1)
    else:
        lay_interior(field_ref, shifts_ref, 7, 16, -7)
        lay_slab(layer_ref[1].reshape(16, 16, 128), near_flag(near_ref, 17), shifts_ref.at[:, 9])
    zero = jnp.zeros((128, 128), BF)
    for a in range(3):
        for c in range(3):
            for t in range(4):
                for s in range(2):
                    weights_ref[a, c, s * 128 : s * 128 + 128, t * 128 : t * 128 + 128] = (
                        conv_ref[2 - a, 2 - t + s, 2 - c] if 0 <= t - s <= 2 else zero
                    )
    copies = []
    for step in range(8 // tile):
        first = step * tile
        acc = None
        for a in range(3):
            for c in range(3):
                part = dot(window(shifts_ref, c, first + a, tile), weights_ref[a, c], NT)
                acc = part if acc is None else acc + part
        here = 8 * half + first
        for s in range(2):
            field = field_ref[here : here + tile, :, s].astype(F32)
            held_ref[first : first + tile, :, s] = (
                acc[:, s * 128 : s * 128 + 128].reshape(tile, 8, 16, 128) + field
            ).astype(BF)
        copy = pltpu.make_async_copy(
            held_ref.at[pl.ds(first, tile)], result_ref.at[pl.ds(here, tile)], sems.at[step]
        )
        copy.start()
        copies.append(copy)
    for copy in copies:
        copy.wait()


def coarse_kernel(coords_ref, keep_ref, got_ref, coarse_ref, token_ref, held_ref, sems):
    token_ref[...] = jnp.zeros_like(token_ref)
    upper, oy = coords_ref[0] % 2, coords_ref[1] % 2
    there = got_ref[52, 0:16].astype(F32)
    none = jnp.zeros((8, 16, 128), BF)
    for i in range(8):
        rows = jnp.concatenate([got_ref[36 + 2 * i], got_ref[37 + 2 * i]], axis=0)
        rows = rows.reshape(8, 16, 128).astype(F32)
        held_ref[0, i, pl.ds(8 * oy, 8)] = keep_ref[i]
        held_ref[0, i, pl.ds(8 - 8 * oy, 8)] = none
        held_ref[1, i, 0:8] = jnp.where(there == 0, rows, 0.0).astype(BF)
        held_ref[1, i, 8:16] = jnp.where(there == 1, rows, 0.0).astype(BF)
    keep = pltpu.make_async_copy(held_ref.at[0], coarse_ref.at[pl.ds(8 * upper, 8)], sems.at[0])
    got = pltpu.make_async_copy(held_ref.at[1], coarse_ref.at[pl.ds(8 - 8 * upper, 8)], sems.at[1])
    keep.start()
    got.start()
    keep.wait()
    got.wait()


ANY = pl.BlockSpec(memory_space=pl.ANY)
TOKEN = jax.ShapeDtypeStruct((8, 128), F32)
sds = jax.ShapeDtypeStruct


def call(kernel, ins, outs, scratch=(), flops=0, moved=1 << 20, limit=8, out=VMEM, **kw):
    return pl.pallas_call(
        kernel,
        in_specs=ins,
        out_specs=[VMEM if shape is TOKEN else out for shape in outs],
        out_shape=outs,
        scratch_shapes=list(scratch),
        cost_estimate=pl.CostEstimate(flops=flops, bytes_accessed=moved, transcendentals=0),
        compiler_params=pltpu.CompilerParams(vmem_limit_bytes=limit << 20),
        **kw,
    )


def grad_call(coords, parent, own, other, down, field):
    layers = sds((2, 8, 2, 16, 128), BF)
    return call(
        grad_kernel, [SMEM] * 2 + [VMEM] * 3 + [ANY],
        [sds((16, 8, 2, 16, 128), BF), sds((8, 128, 256), BF), layers, layers],
        [pltpu.VMEM((8, 128, 128), F32), pltpu.SemaphoreType.DMA((2,))],
        flops=2 * 2**27, moved=4 << 20,
    )(coords, parent, own, other, down, field)


def inner_call(field, conv):
    return call(
        inner_kernel, [VMEM] * 2,
        [sds((3, 16, 9, 2, 16, 128), BF), sds((3, 3, 512, 256), BF), sds((16, 8, 2, 16, 128), BF)],
        flops=2 * 9 * 2048 * 512 * 256, moved=2 << 20, limit=16,
    )(field, conv)


def main_call(coords, parent, near, field, low, high, inner, down, grads, spread):
    slab = pltpu.VMEM((3, 9, 2, 16, 128), BF)
    return call(
        main_kernel, [SMEM] * 3 + [VMEM] * 9,
        [sds((36, 64, 128), F32), sds((53, 64, 128), BF), sds((8, 8, 16, 128), BF)],
        [slab, slab, pltpu.VMEM((2, 8, 2, 16, 128), BF), pltpu.VMEM((8, 2, 128, 128), F32)],
        flops=2 * 9 * 2048 * 512 * 256, limit=24,
    )(coords, parent, near, field, low, high, *inner, down, grads, spread)


def input_call(near, field, layer, conv, after, half, base=None):
    ins, values = [SMEM] + [VMEM] * 3 + [ANY], [near, field, layer, conv, after]
    aliases = {}
    if base is not None:
        ins, values, aliases = ins + [ANY], values + [base], {5: 0}
    return call(
        functools.partial(input_kernel, half=half), ins, [sds((16, 8, 2, 16, 128), BF), TOKEN],
        [pltpu.VMEM((3, 10, 9, 2, 16, 128), BF), pltpu.VMEM((3, 3, 256, 512), BF),
         pltpu.VMEM((8, 8, 2, 16, 128), BF), pltpu.SemaphoreType.DMA((2,))],
        flops=9 * 2048 * 512 * 256, limit=24, out=ANY, input_output_aliases=aliases,
    )(*values)


def coarse_call(coords, keep, got, after):
    def kernel(coords_ref, keep_ref, got_ref, after_ref, *refs):
        coarse_kernel(coords_ref, keep_ref, got_ref, *refs)

    return call(
        kernel, [SMEM] + [VMEM] * 2 + [ANY], [sds((16, 16, 16, 128), BF), TOKEN],
        [pltpu.VMEM((2, 8, 16, 16, 128), BF), pltpu.SemaphoreType.DMA((2,))], out=ANY,
    )(coords, keep, got, after)


def places(coords_ref, y_ref):
    core, x = coords_ref[0] % 2, (coords_ref[0] // 2) % 4
    return jnp.where(core == 0, y_ref[0], x), jnp.where(core == 0, x, y_ref[0])


def spread_rows(coords_ref, y_ref, kept_ref, got_ref, own_ref, *send_refs):
    place = places(coords_ref, y_ref)[0]
    for k, ref in enumerate((own_ref, *send_refs)):
        at = pl.multiple_of(16 * ((place + k) % 4), 16)
        rows = kept_ref[:, pl.ds(at, 16)] + got_ref[0:36, pl.ds(at, 16)].astype(F32)
        ref[...] = rows.astype(ref.dtype)


def spread_taps(coords_ref, y_ref, kept_ref, *refs):
    got_refs, out_refs = refs[:3], refs[-4:]
    x = places(coords_ref, y_ref)[1]
    for k, ref in enumerate(out_refs):
        taps = pl.ds(9 * ((x + k) % 4), 9)
        total = kept_ref[taps]
        for got_ref in got_refs:
            total = total + got_ref[taps].astype(F32)
        ref[...] = total.astype(ref.dtype)


def add_up(coords_ref, y_ref, kept_ref, first_ref, second_ref, third_ref, *refs):
    refs[-1][...] = kept_ref[...] + first_ref[...] + second_ref[...] + third_ref[...]


def add_pair(coords_ref, y_ref, own_ref, got_ref, *refs):
    refs[-1][...] = (own_ref[...] + got_ref[...]).astype(refs[-1].dtype)


def join_taps(coords_ref, y_ref, own_ref, *refs):
    x = places(coords_ref, y_ref)[1]
    for k, ref in enumerate((own_ref, *refs[:3])):
        refs[-1][pl.ds(9 * ((x - k + 4) % 4), 9)] = ref[...]


def join_rows(coords_ref, y_ref, own_ref, *refs):
    place = places(coords_ref, y_ref)[0]
    for k, ref in enumerate((own_ref, *refs[:3])):
        at = pl.multiple_of(16 * ((place - k + 4) % 4), 16)
        refs[-1][:, pl.ds(at, 16)] = ref[...]


def finish(coords_ref, y_ref, own_ref, got_ref, conv_ref, down_ref):
    core = coords_ref[0] % 2
    mine = pl.ds(pl.multiple_of(64 * core, 64), 64)
    theirs = pl.ds(pl.multiple_of(64 * (1 - core), 64), 64)
    conv_ref[:, mine] = own_ref[0:27].astype(F32)
    conv_ref[:, theirs] = got_ref[0:27].astype(F32)
    down_ref[:, mine] = own_ref[27:35].astype(F32)
    down_ref[:, theirs] = got_ref[27:35].astype(F32)


def ring(size, step, by):
    return [(i, i - i // step % size * step + (i // step + by) % size * step) for i in range(32)]


def over_core(value):
    return lax.ppermute(value, "region", [(i, i ^ 1) for i in range(32)])


def over_z(value, mask):
    return lax.ppermute(value, "region", [(i, i ^ (8 * mask)) for i in range(32)])


def over_plane(value, by, second):
    along_x, route = ring(4, 2, by), []
    for y in range(4):
        for region, target in along_x:
            if region % 2 == second:
                route.append((32 * y + region, 32 * ((y + by) % 4) + region))
            else:
                route.append((32 * y + region, 32 * y + target))
    return lax.ppermute(value, ("dp", "region"), route)


def stage(kernel, coords, y, values, outs, after=(), scratch=()):
    ins = [SMEM] * 2 + [VMEM] * len(values) + [ANY] * len(after)
    return call(kernel, ins, outs, scratch)(coords, y, *values, *after)


def next_region(value):
    return lax.ppermute(value, "region", [(i, i + 1) for i in range(31)])


def previous_region(value):
    return lax.ppermute(value, "region", [(i + 1, i) for i in range(31)])


def local(features, conv_weight, down_weight, coarse_cotangent, brick_coords, neighbours, parents):
    coords, near, parent = brick_coords.reshape(3), neighbours.reshape(26), parents.reshape(1)
    y = lax.axis_index("dp").reshape(1).astype(jnp.int32)
    core = lax.axis_index("region") % 2
    cotangent = coarse_cotangent.reshape(16, 16, 16, 128)
    theirs = over_core(lax.dynamic_slice_in_dim(cotangent, 8 * (1 - core), 8))
    field = features.reshape(16, 8, 2, 16, 128)
    grads, spread, up, back = grad_call(coords, parent, cotangent, theirs, down_weight, field)
    low, high = next_region(up), previous_region(back)
    inner = inner_call(field, conv_weight)
    kept, sent, keep = main_call(
        coords, parent, near, field, low, high, inner, down_weight, grads, spread
    )
    run = functools.partial(stage, coords=coords, y=y)

    got = over_core(sent)
    own, *sends = run(
        spread_rows, values=(kept, got), outs=[sds((36, 16, 128), F32)] + [sds((36, 16, 128), BF)] * 3
    )
    gots = [over_plane(v, k + 1, 0) for k, v in enumerate(sends)]
    partial_grad, token = input_call(near, grads, low, conv_weight, own, 0)
    own, *sends = run(
        spread_taps, values=(own, *gots), outs=[sds((9, 16, 128), F32)] * 4, after=(token,)
    )
    gots = [over_plane(v, k + 1, 1) for k, v in enumerate(sends)]
    coarse, token = coarse_call(coords, keep, got, own)
    own = run(add_up, values=(own, *gots), outs=[sds((9, 16, 128), F32)], after=(token,))[0]
    own = run(add_pair, values=(own, over_z(own, 1)), outs=[sds((9, 16, 128), F32)])[0]
    own = run(add_pair, values=(own, over_z(own, 3)), outs=[sds((9, 16, 128), BF)])[0]

    gots = [over_plane(own, k, 1) for k in (1, 2, 3)]
    own = run(join_taps, values=(own, *gots), outs=[sds((36, 16, 128), BF)])[0]
    gots = [over_plane(own, k, 0) for k in (1, 2, 3)]
    input_grad, token = input_call(near, grads, high, conv_weight, own, 1, partial_grad)
    own = run(join_rows, values=(own, *gots), outs=[sds((36, 64, 128), BF)], after=(token,))[0]
    got = over_core(own)
    conv_grad, down_grad = run(
        finish, values=(own, got), outs=[sds((27, 128, 128), F32), sds((8, 128, 128), F32)]
    )
    whole = (1, 1, 16, 16, 16, 128)
    return (
        coarse.reshape(whole),
        input_grad.reshape(whole),
        conv_grad.reshape(3, 3, 3, 128, 128),
        down_grad.reshape(2, 2, 2, 128, 128),
    )


def solution(mesh):
    bricks = P("dp", "region", None, None, None, None)
    return jax.shard_map(
        local,
        mesh=mesh,
        in_specs=(bricks, P(), P(), bricks, P("dp", "region", None), P("dp", "region", None), P("dp", "region")),
        out_specs=(bricks, bricks, P(), P()),
        check_vma=False,
    )
```

```python
import functools
import jax
import jax.numpy as jnp
from jax import lax
from jax.experimental import pallas as pl
from jax.experimental.pallas import tpu as pltpu
from jax.sharding import PartitionSpec as P

BF, F32 = jnp.bfloat16, jnp.float32
SMEM = pl.BlockSpec(memory_space=pltpu.SMEM)
VMEM = pl.BlockSpec(memory_space=pltpu.VMEM)
NN = (((1,), (0,)), ((), ()))
NT = (((1,), (1,)), ((), ()))
TN = (((0,), (0,)), ((), ()))


def dot(lhs, rhs, dims):
    return lax.dot_general(lhs, rhs, dims, preferred_element_type=F32)


def z_index(rows):
    return lax.broadcasted_iota(jnp.int32, (rows, 128), 0) % 16


def lay_interior(field_ref, shifts_ref, start=0, stop=16, base=1):
    z = z_index(256)

    @pl.loop(start, stop)
    def _(x):
        plain = field_ref[x].reshape(256, 128)
        wide = plain.astype(F32)
        lower = jnp.where(z == 0, 0.0, pltpu.roll(wide, 1, 0)).astype(BF)
        upper = jnp.where(z == 15, 0.0, pltpu.roll(wide, 255, 0)).astype(BF)
        for c, value in enumerate((lower, plain, upper)):
            rows = value.reshape(8, 2, 16, 128)
            shifts_ref[c, x + base, 0:8, 1] = rows[:, 0]
            shifts_ref[c, x + base, 1:9, 0] = rows[:, 1]
            shifts_ref[c, x + base, 0, 0] = jnp.zeros((16, 128), BF)
            shifts_ref[c, x + base, 8, 1] = jnp.zeros((16, 128), BF)


def lay_slab(layer, flag, slab_ref):
    def three(value, b):
        rows = value.shape[0] * 16
        wide = value.astype(F32).reshape(rows, 128)
        z = z_index(rows)
        below, same, above = (flag(b, c) for c in (-1, 0, 1))
        lower = jnp.where(
            z == 0, pltpu.roll(wide, rows - 15, 0) * below, pltpu.roll(wide, 1, 0) * same
        )
        upper = jnp.where(
            z == 15, pltpu.roll(wide, 15, 0) * above, pltpu.roll(wide, rows - 1, 0) * same
        )
        return [v.astype(BF) for v in (lower, wide * same, upper)]

    for c, value in enumerate(three(layer, 0)):
        rows = value.reshape(8, 2, 16, 128)
        slab_ref[c, 0:8, 1] = rows[:, 0]
        slab_ref[c, 1:9, 0] = rows[:, 1]
    for c, value in enumerate(three(layer[15:16], -1)):
        slab_ref[c, 0, 0] = value.reshape(16, 128)
    for c, value in enumerate(three(layer[0:1], 1)):
        slab_ref[c, 8, 1] = value.reshape(16, 128)


def near_flag(near_ref, first):
    return lambda b, c: (near_ref[first + 3 * (b + 1) + c + 1] >= 0).astype(F32)


def window(shifts_ref, c, x, count):
    return jnp.concatenate(
        [
            shifts_ref[c, pl.ds(x, count), t // 2 : t // 2 + 8, t % 2].reshape(count * 128, 128)
            for t in range(4)
        ],
        axis=1,
    )


def joined_down(down_ref):
    return jnp.concatenate(
        [
            jnp.concatenate([down_ref[p, q, r] for r in range(2)], axis=1)
            for p in range(2)
            for q in range(2)
        ],
        axis=0,
    )


def grad_kernel(
    coords_ref, parent_ref, own_hbm, other_ref, down_hbm, field_hbm,
    grads_ref, spread_ref, up_ref, back_ref, wide_ref, own_ref, down_ref, sems,
):
    x, oy, oz = coords_ref[0], coords_ref[1] % 2, coords_ref[2] % 2
    copies = [
        pltpu.make_async_copy(
            own_hbm.at[pl.ds(8 * (x % 2), 8), pl.ds(8 * oy, 8)], own_ref, sems.at[0]
        ),
        pltpu.make_async_copy(down_hbm, down_ref, sems.at[1]),
        pltpu.make_async_copy(field_hbm.at[15], up_ref.at[0], sems.at[2]),
        pltpu.make_async_copy(field_hbm.at[0], back_ref.at[0], sems.at[3]),
    ]
    for copy in copies:
        copy.start()
    is_own = parent_ref[0] == x
    copies[0].wait()
    copies[1].wait()
    down = joined_down(down_ref)
    wide_ref[...] = jnp.zeros_like(wide_ref)
    for i in range(8):
        mine = own_ref[i].astype(F32)
        theirs = other_ref[i, pl.ds(8 * oy, 8)].astype(F32)
        both = jnp.where(is_own, mine, theirs)
        part = jnp.where(oz == 0, both[:, 0:8], both[:, 8:16]).reshape(64, 128)
        wide_ref[i, pl.ds(0, 64, stride=2), :] = part
    for i in range(8):
        even = wide_ref[i]
        spread = jnp.concatenate([even, pltpu.roll(even, 1, 0)], axis=1).astype(BF)
        spread_ref[i] = spread
        grads = dot(spread, down, NT).astype(BF)
        for p in range(2):
            for q in range(2):
                at = (2 * p + q) * 128
                part = grads[:, at : at + 128].reshape(8, 16, 128)
                grads_ref[2 * i + p, :, q] = part
                if 2 * i + p == 15:
                    up_ref[1, :, q] = part
                if 2 * i + p == 0:
                    back_ref[1, :, q] = part
    copies[2].wait()
    copies[3].wait()


def lay_weights(conv_ref, weights_ref):
    zero = jnp.zeros((128, 128), BF)
    for a in range(3):
        for c in range(3):
            for t in range(4):
                for s in range(2):
                    weights_ref[a, c, t * 128 : t * 128 + 128, s * 128 : s * 128 + 128] = (
                        conv_ref[a, t - s, c] if 0 <= t - s <= 2 else zero
                    )


def inner_kernel(field_ref, conv_ref, shifts_ref, weights_ref, outputs_ref):
    lay_interior(field_ref, shifts_ref, 0, 16, 0)
    lay_weights(conv_ref, weights_ref)
    for first, count in ((1, 7), (8, 7)):
        acc = None
        for a in range(3):
            for c in range(3):
                part = dot(window(shifts_ref, c, first + a - 1, count), weights_ref[a, c], NN)
                acc = part if acc is None else acc + part
        for s in range(2):
            field = field_ref[first : first + count, :, s].astype(F32)
            outputs_ref[first : first + count, :, s] = (
                acc[:, s * 128 : s * 128 + 128].reshape(count, 8, 16, 128) + field
            ).astype(BF)


def taps(rows):
    return jnp.concatenate(
        [rows[t // 2 : t // 2 + 8, t % 2].reshape(128, 128) for t in range(4)], axis=1
    )


def main_kernel(
    coords_ref, parent_ref, near_ref, field_ref, low_ref, high_ref, shifts_ref, weights_ref,
    inner_ref, down_ref, grads_ref, spread_ref,
    kept_rows_ref, sent_ref, keep_ref, low_shifts_ref, high_shifts_ref, edges_ref, sums_ref,
):
    x, oy, oz = coords_ref[0], coords_ref[1] % 2, coords_ref[2] % 2
    first_core = x % 2 == 0
    kept = (parent_ref[0] == x).astype(F32)

    def part_rows(tap, rows):
        kept_rows_ref[tap] = jnp.where(first_core, rows[0:64], rows[64:128])
        sent_ref[tap] = jnp.where(first_core, rows[64:128], rows[0:64]).astype(BF)

    kept_rows_ref[35] = jnp.zeros((64, 128), F32)
    sent_ref[35] = jnp.zeros((64, 128), BF)
    sent_ref[52] = jnp.full((64, 128), oy, jnp.int32).astype(F32).astype(BF)
    lay_slab(low_ref[0].reshape(16, 16, 128), near_flag(near_ref, 0), low_shifts_ref)
    lay_slab(high_ref[0].reshape(16, 16, 128), near_flag(near_ref, 17), high_shifts_ref)

    acc = None
    for a in range(3):
        for c in range(3):
            below = taps(low_shifts_ref[c] if a == 0 else shifts_ref[c, a - 1])
            above = taps(high_shifts_ref[c] if a == 2 else shifts_ref[c, 14 + a])
            part = dot(jnp.concatenate([below, above], axis=0), weights_ref[a, c], NN)
            acc = part if acc is None else acc + part
    for s in range(2):
        for k in range(2):
            value = acc[128 * k : 128 * k + 128, s * 128 : s * 128 + 128].reshape(8, 16, 128)
            edges_ref[k, :, s] = (value + field_ref[15 * k, :, s].astype(F32)).astype(BF)

    down = joined_down(down_ref)

    def corner(i, p, q):
        at = 2 * i + p
        rows = edges_ref[at // 15, :, q] if at in (0, 15) else inner_ref[at, :, q]
        return rows.reshape(128, 128)

    for i in range(8):
        corners = jnp.concatenate([corner(i, p, q) for p in range(2) for q in range(2)], axis=1)
        sums = dot(corners, down, NN)
        sums_ref[i, 0] = sums[:, 0:128]
        sums_ref[i, 1] = sums[:, 128:256]
        block = sums_ref[i, 0, pl.ds(0, 64, stride=2), :] + sums_ref[i, 1, pl.ds(1, 64, stride=2), :]
        block = block.reshape(8, 8, 128)
        none = jnp.zeros_like(block)
        low = jnp.where(oz == 0, block, none)
        high = jnp.where(oz == 0, none, block)
        placed = jnp.concatenate([low, high], axis=1).reshape(128, 128)
        keep_ref[i] = (placed * kept).astype(BF).reshape(8, 16, 128)
        away = (placed * (1 - kept)).astype(BF)
        sent_ref[36 + 2 * i] = away[0:64]
        sent_ref[37 + 2 * i] = away[64:128]

    spread = spread_ref[...].reshape(1024, 256)
    for p in range(2):
        for q in range(2):
            rows = jnp.concatenate([corner(i, p, q) for i in range(8)], axis=0)
            result = dot(rows, spread, TN) * (1.0 / 1024)
            part_rows(27 + 4 * p + 2 * q, result[:, 0:128])
            part_rows(28 + 4 * p + 2 * q, result[:, 128:256])

    pair = jnp.concatenate([grads_ref[:, :, s].reshape(2048, 128) for s in range(2)], axis=1)
    for a in range(3):
        for c in range(3):
            if a == 0:
                rows = jnp.concatenate(
                    [taps(low_shifts_ref[c]), window(shifts_ref, c, 0, 15)], axis=0
                )
            elif a == 1:
                rows = window(shifts_ref, c, 0, 16)
            else:
                rows = jnp.concatenate(
                    [window(shifts_ref, c, 1, 15), taps(high_shifts_ref[c])], axis=0
                )
            result = dot(rows, pair, TN) * (1.0 / 1024)
            for b in range(3):
                part_rows(
                    9 * a + 3 * b + c,
                    result[b * 128 : b * 128 + 128, 0:128]
                    + result[b * 128 + 128 : b * 128 + 256, 128:256],
                )


def input_kernel(near_ref, field_hbm, layer_hbm, conv_hbm, *refs, half, tile=4):
    (result_ref, token_ref, shifts_ref, weights_ref, held_ref, field_ref, layer_ref, conv_ref,
     sems) = refs[-9:]
    token_ref[...] = jnp.zeros_like(token_ref)
    first_layer = 7 * half
    fetches = [
        pltpu.make_async_copy(
            field_hbm.at[pl.ds(first_layer + 3 * k, 3)], field_ref.at[pl.ds(3 * k, 3)], sems.at[2 + k]
        )
        for k in range(3)
    ]
    layer_copy = pltpu.make_async_copy(layer_hbm.at[1], layer_ref, sems.at[5])
    conv_copies = [
        pltpu.make_async_copy(conv_hbm.at[a], conv_ref.at[a], sems.at[6 + a]) for a in range(3)
    ]
    for copy in (*fetches, layer_copy, *conv_copies):
        copy.start()
    for k in range(3):
        fetches[k].wait()
        lay_interior(field_ref, shifts_ref, 3 * k, 3 * k + 3, 1 - half)
    layer_copy.wait()
    lay_slab(
        layer_ref[...].reshape(16, 16, 128), near_flag(near_ref, 17 * half), shifts_ref.at[:, 9 * half]
    )
    zero = jnp.zeros((128, 128), BF)
    for a in (2, 1, 0):
        conv_copies[2 - a].wait()
        for c in range(3):
            for t in range(4):
                for s in range(2):
                    weights_ref[a, c, s * 128 : s * 128 + 128, t * 128 : t * 128 + 128] = (
                        conv_ref[2 - a, 2 - t + s, 2 - c] if 0 <= t - s <= 2 else zero
                    )
    copies = []
    for step in range(8 // tile):
        first = step * tile
        acc = None
        for a in range(3):
            for c in range(3):
                part = dot(window(shifts_ref, c, first + a, tile), weights_ref[a, c], NT)
                acc = part if acc is None else acc + part
        here = 8 * half + first
        for s in range(2):
            field = field_ref[first + half : first + half + tile, :, s].astype(F32)
            held_ref[first : first + tile, :, s] = (
                acc[:, s * 128 : s * 128 + 128].reshape(tile, 8, 16, 128) + field
            ).astype(BF)
        copy = pltpu.make_async_copy(
            held_ref.at[pl.ds(first, tile)], result_ref.at[pl.ds(here, tile)], sems.at[step]
        )
        copy.start()
        copies.append(copy)
    for copy in copies:
        copy.wait()


def coarse_kernel(coords_ref, keep_ref, got_ref, coarse_ref, token_ref, held_ref, sems):
    token_ref[...] = jnp.zeros_like(token_ref)
    upper, oy = coords_ref[0] % 2, coords_ref[1] % 2
    there = got_ref[52, 0:16].astype(F32)
    none = jnp.zeros((8, 16, 128), BF)
    for i in range(8):
        rows = jnp.concatenate([got_ref[36 + 2 * i], got_ref[37 + 2 * i]], axis=0)
        rows = rows.reshape(8, 16, 128).astype(F32)
        held_ref[0, i, pl.ds(8 * oy, 8)] = keep_ref[i]
        held_ref[0, i, pl.ds(8 - 8 * oy, 8)] = none
        held_ref[1, i, 0:8] = jnp.where(there == 0, rows, 0.0).astype(BF)
        held_ref[1, i, 8:16] = jnp.where(there == 1, rows, 0.0).astype(BF)
    keep = pltpu.make_async_copy(held_ref.at[0], coarse_ref.at[pl.ds(8 * upper, 8)], sems.at[0])
    got = pltpu.make_async_copy(held_ref.at[1], coarse_ref.at[pl.ds(8 - 8 * upper, 8)], sems.at[1])
    keep.start()
    got.start()
    keep.wait()
    got.wait()


ANY = pl.BlockSpec(memory_space=pl.ANY)
HBM = pl.BlockSpec(memory_space=pltpu.HBM)
TOKEN = jax.ShapeDtypeStruct((8, 128), F32)
sds = jax.ShapeDtypeStruct


def call(kernel, ins, outs, scratch=(), flops=0, moved=1 << 20, limit=8, out=VMEM, **kw):
    return pl.pallas_call(
        kernel,
        in_specs=ins,
        out_specs=[VMEM if shape is TOKEN else out for shape in outs],
        out_shape=outs,
        scratch_shapes=list(scratch),
        cost_estimate=pl.CostEstimate(flops=flops, bytes_accessed=moved, transcendentals=0),
        compiler_params=pltpu.CompilerParams(vmem_limit_bytes=limit << 20),
        **kw,
    )


def grad_call(coords, parent, own, other, down, field):
    layers = sds((2, 8, 2, 16, 128), BF)
    return call(
        grad_kernel, [SMEM] * 2 + [HBM, VMEM, HBM, HBM],
        [sds((16, 8, 2, 16, 128), BF), sds((8, 128, 256), BF), layers, layers],
        [pltpu.VMEM((8, 128, 128), F32), pltpu.VMEM((8, 8, 16, 128), BF),
         pltpu.VMEM((2, 2, 2, 128, 128), BF), pltpu.SemaphoreType.DMA((4,))],
        flops=2 * 2**27, moved=4 << 20,
    )(coords, parent, own, other, down, field)


def inner_call(field, conv):
    return call(
        inner_kernel, [VMEM] * 2,
        [sds((3, 16, 9, 2, 16, 128), BF), sds((3, 3, 512, 256), BF), sds((16, 8, 2, 16, 128), BF)],
        flops=2 * 9 * 2048 * 512 * 256, moved=2 << 20, limit=16,
    )(field, conv)


def main_call(coords, parent, near, field, low, high, inner, down, grads, spread):
    slab = pltpu.VMEM((3, 9, 2, 16, 128), BF)
    return call(
        main_kernel, [SMEM] * 3 + [VMEM] * 9,
        [sds((36, 64, 128), F32), sds((53, 64, 128), BF), sds((8, 8, 16, 128), BF)],
        [slab, slab, pltpu.VMEM((2, 8, 2, 16, 128), BF), pltpu.VMEM((8, 2, 128, 128), F32)],
        flops=2 * 9 * 2048 * 512 * 256, limit=24,
    )(coords, parent, near, field, low, high, *inner, down, grads, spread)


def input_call(near, field, layer, conv, after, half, base=None):
    ins, values = [SMEM] + [HBM] * 3 + [ANY], [near, field, layer, conv, after]
    aliases = {}
    if base is not None:
        ins, values, aliases = ins + [ANY], values + [base], {5: 0}
    return call(
        functools.partial(input_kernel, half=half), ins, [sds((16, 8, 2, 16, 128), BF), TOKEN],
        [pltpu.VMEM((3, 10, 9, 2, 16, 128), BF), pltpu.VMEM((3, 3, 256, 512), BF),
         pltpu.VMEM((8, 8, 2, 16, 128), BF), pltpu.VMEM((9, 8, 2, 16, 128), BF),
         pltpu.VMEM((8, 2, 16, 128), BF), pltpu.VMEM((3, 3, 3, 128, 128), BF),
         pltpu.SemaphoreType.DMA((9,))],
        flops=9 * 2048 * 512 * 256, limit=24, out=ANY, input_output_aliases=aliases,
    )(*values)


def coarse_call(coords, keep, got, after):
    def kernel(coords_ref, keep_ref, got_ref, after_ref, *refs):
        coarse_kernel(coords_ref, keep_ref, got_ref, *refs)

    return call(
        kernel, [SMEM] + [VMEM] * 2 + [ANY], [sds((16, 16, 16, 128), BF), TOKEN],
        [pltpu.VMEM((2, 8, 16, 16, 128), BF), pltpu.SemaphoreType.DMA((2,))], out=ANY,
    )(coords, keep, got, after)


def add_halves(kept_ref, got_ref, total_ref):
    total_ref[...] = (kept_ref[...] + got_ref[0:36].astype(F32)).astype(BF)


def add_sixteen(got_ref, *refs):
    total = got_ref[0].astype(F32)
    for k in range(1, 16):
        total = total + got_ref[k].astype(F32)
    refs[-1][...] = total


def add_in_order(own_ref, *refs):
    y = lax.axis_index("dp")
    total_ref, slots_ref = refs[-2:]
    for k, ref in enumerate((own_ref, *refs[:3])):
        slots_ref[(y - k + 4) % 4] = ref[...]
    total = ((slots_ref[0] + slots_ref[1]) + (slots_ref[2] + slots_ref[3])).astype(BF)
    for k in range(16):
        total_ref[k] = total


def finish(own_ref, got_ref, *refs):
    conv_ref, down_ref = refs[-2:]
    core = lax.axis_index("core")
    mine = pl.ds(pl.multiple_of(64 * core, 64), 64)
    theirs = pl.ds(pl.multiple_of(64 * (1 - core), 64), 64)
    conv_ref[:, mine] = own_ref[0:27].astype(F32)
    conv_ref[:, theirs] = got_ref[0:27].astype(F32)
    down_ref[:, mine] = own_ref[27:35].astype(F32)
    down_ref[:, theirs] = got_ref[27:35].astype(F32)


def over_core(value):
    return lax.ppermute(value, "core", [(0, 1), (1, 0)])


def over_y(value, by):
    return lax.ppermute(value, "dp", [(i, (i + by) % 4) for i in range(4)])


def over_plane(value):
    return lax.all_to_all(value, ("z", "x"), 0, 0, tiled=True)


def stage(kernel, values, outs, after=(), scratch=()):
    return call(kernel, [VMEM] * len(values) + [ANY] * len(after), outs, scratch)(*values, *after)


def next_region(value):
    return lax.ppermute(value, ("z", "x", "core"), [(i, i + 1) for i in range(31)])


def previous_region(value):
    return lax.ppermute(value, ("z", "x", "core"), [(i + 1, i) for i in range(31)])


def local(features, conv_weight, down_weight, coarse_cotangent, brick_coords, neighbours, parents):
    coords, near, parent = brick_coords.reshape(3), neighbours.reshape(26), parents.reshape(1)
    core = lax.axis_index("core")
    cotangent = coarse_cotangent.reshape(16, 16, 16, 128)
    theirs = over_core(lax.dynamic_slice_in_dim(cotangent, 8 * (1 - core), 8))
    field = features.reshape(16, 8, 2, 16, 128)
    far = functools.partial(pltpu.with_memory_space_constraint, memory_space=pltpu.HBM)
    grads, spread, up, back = grad_call(
        coords, parent, far(cotangent), theirs, far(down_weight), far(field)
    )
    low, high = next_region(up), previous_region(back)
    inner = inner_call(field, conv_weight)
    kept, sent, keep = main_call(
        coords, parent, near, field, low, high, inner, down_weight, grads, spread
    )

    got = over_core(sent)
    own = stage(add_halves, (kept, got), [sds((36, 64, 128), BF)])[0]
    gots = over_plane(own.reshape(16, 144, 128))
    partial_grad, token = input_call(near, grads, low, far(conv_weight), own, 0)
    coarse, token = coarse_call(coords, keep, got, token)
    own = stage(add_sixteen, (gots,), [sds((144, 128), F32)], (token,))[0]
    gots = [over_y(own, k) for k in (1, 2, 3)]
    shares = stage(
        add_in_order, (own, *gots), [sds((16, 144, 128), BF)],
        scratch=[pltpu.VMEM((4, 144, 128), F32)],
    )[0]

    own = over_plane(shares).reshape(36, 64, 128)
    input_grad, token = input_call(near, grads, high, far(conv_weight), shares, 1, partial_grad)
    own, token = lax.optimization_barrier((own, token))
    got = over_core(own)
    conv_grad, down_grad = stage(
        finish, (own, got), [sds((27, 128, 128), F32), sds((8, 128, 128), F32)], (token,)
    )
    whole = (1, 1, 16, 16, 16, 128)
    return (
        coarse.reshape(whole),
        input_grad.reshape(whole),
        conv_grad.reshape(3, 3, 3, 128, 128),
        down_grad.reshape(2, 2, 2, 128, 128),
    )


def solution(mesh):
    sizes = (mesh.devices.shape[0], 4, 4, 2)
    mesh = jax.sharding.Mesh(mesh.devices.reshape(sizes), ("dp", "z", "x", "core"))
    region = ("z", "x", "core")
    bricks = P("dp", region, None, None, None, None)
    rows = P("dp", region, None)
    return jax.shard_map(
        local,
        mesh=mesh,
        in_specs=(bricks, P(), P(), bricks, rows, rows, P("dp", region)),
        out_specs=(bricks, bricks, P(), P()),
        check_vma=False,
    )
```

```python
import functools
import jax
import jax.numpy as jnp
from jax import lax
from jax.experimental import pallas as pl
from jax.experimental.pallas import tpu as pltpu
from jax.sharding import PartitionSpec as P

BF, F32 = jnp.bfloat16, jnp.float32
SMEM = pl.BlockSpec(memory_space=pltpu.SMEM)
VMEM = pl.BlockSpec(memory_space=pltpu.VMEM)
NN = (((1,), (0,)), ((), ()))
NT = (((1,), (1,)), ((), ()))
TN = (((0,), (0,)), ((), ()))


def dot(lhs, rhs, dims):
    return lax.dot_general(lhs, rhs, dims, preferred_element_type=F32)


def z_index(rows):
    return lax.broadcasted_iota(jnp.int32, (rows, 128), 0) % 16


def lay_interior(field_ref, shifts_ref, start=0, stop=16, base=1):
    z = z_index(256)

    @pl.loop(start, stop)
    def _(x):
        plain = field_ref[x].reshape(256, 128)
        wide = plain.astype(F32)
        lower = jnp.where(z == 0, 0.0, pltpu.roll(wide, 1, 0)).astype(BF)
        upper = jnp.where(z == 15, 0.0, pltpu.roll(wide, 255, 0)).astype(BF)
        for c, value in enumerate((lower, plain, upper)):
            rows = value.reshape(8, 2, 16, 128)
            shifts_ref[c, x + base, 0:8, 1] = rows[:, 0]
            shifts_ref[c, x + base, 1:9, 0] = rows[:, 1]
            shifts_ref[c, x + base, 0, 0] = jnp.zeros((16, 128), BF)
            shifts_ref[c, x + base, 8, 1] = jnp.zeros((16, 128), BF)


def lay_slab(layer, flag, slab_ref):
    def three(value, b):
        rows = value.shape[0] * 16
        wide = value.astype(F32).reshape(rows, 128)
        z = z_index(rows)
        below, same, above = (flag(b, c) for c in (-1, 0, 1))
        lower = jnp.where(
            z == 0, pltpu.roll(wide, rows - 15, 0) * below, pltpu.roll(wide, 1, 0) * same
        )
        upper = jnp.where(
            z == 15, pltpu.roll(wide, 15, 0) * above, pltpu.roll(wide, rows - 1, 0) * same
        )
        return [v.astype(BF) for v in (lower, wide * same, upper)]

    for c, value in enumerate(three(layer, 0)):
        rows = value.reshape(8, 2, 16, 128)
        slab_ref[c, 0:8, 1] = rows[:, 0]
        slab_ref[c, 1:9, 0] = rows[:, 1]
    for c, value in enumerate(three(layer[15:16], -1)):
        slab_ref[c, 0, 0] = value.reshape(16, 128)
    for c, value in enumerate(three(layer[0:1], 1)):
        slab_ref[c, 8, 1] = value.reshape(16, 128)


def near_flag(near_ref, first):
    return lambda b, c: (near_ref[first + 3 * (b + 1) + c + 1] >= 0).astype(F32)


def window(shifts_ref, c, x, count):
    return jnp.concatenate(
        [
            shifts_ref[c, pl.ds(x, count), t // 2 : t // 2 + 8, t % 2].reshape(count * 128, 128)
            for t in range(4)
        ],
        axis=1,
    )


def joined_down(down_ref):
    return jnp.concatenate(
        [
            jnp.concatenate([down_ref[p, q, r] for r in range(2)], axis=1)
            for p in range(2)
            for q in range(2)
        ],
        axis=0,
    )


def prepare_kernel(
    coords_ref, cotangent_hbm, down_hbm, field_hbm, after_ref,
    mine_ref, down_ref, partner_ref, other_ref, held_ref, sems,
):
    x, oy = coords_ref[0], coords_ref[1] % 2
    upper = x % 2
    copies = [
        pltpu.make_async_copy(
            cotangent_hbm.at[pl.ds(8 * upper, 8), pl.ds(8 * oy, 8)], mine_ref, sems.at[0]
        ),
        pltpu.make_async_copy(down_hbm, held_ref, sems.at[1]),
        pltpu.make_async_copy(field_hbm.at[15 - 15 * upper], partner_ref, sems.at[2]),
        pltpu.make_async_copy(field_hbm.at[15 * upper], other_ref, sems.at[3]),
    ]
    for copy in copies:
        copy.start()
    copies[1].wait()
    down_ref[...] = joined_down(held_ref)
    for k in (0, 2, 3):
        copies[k].wait()


def grad_kernel(
    coords_ref, parent_ref, mine_ref, theirs_ref, down_ref, partner_ref, other_ref,
    grads_ref, spread_ref, to_partner_ref, to_other_ref, wide_ref,
):
    x, oy, oz = coords_ref[0], coords_ref[1] % 2, coords_ref[2] % 2
    is_own = parent_ref[0] == x
    down = down_ref[...]
    to_partner_ref[0] = partner_ref[...]
    to_other_ref[0] = other_ref[...]
    wide_ref[...] = jnp.zeros_like(wide_ref)
    for i in range(8):
        mine = mine_ref[i].astype(F32)
        theirs = theirs_ref[i, pl.ds(8 * oy, 8)].astype(F32)
        both = jnp.where(is_own, mine, theirs)
        part = jnp.where(oz == 0, both[:, 0:8], both[:, 8:16]).reshape(64, 128)
        wide_ref[i, pl.ds(0, 64, stride=2), :] = part
    for i in range(8):
        even = wide_ref[i]
        spread = jnp.concatenate([even, pltpu.roll(even, 1, 0)], axis=1).astype(BF)
        spread_ref[i] = spread
        grads = dot(spread, down, NT).astype(BF)
        for p in range(2):
            for q in range(2):
                at = (2 * p + q) * 128
                part = grads[:, at : at + 128].reshape(8, 16, 128)
                grads_ref[2 * i + p, :, q] = part
    upper = x % 2
    to_partner_ref[1] = grads_ref[15 - 15 * upper]
    to_other_ref[1] = grads_ref[15 * upper]


def lay_weights(conv_ref, weights_ref):
    zero = jnp.zeros((128, 128), BF)
    for a in range(3):
        for c in range(3):
            for t in range(4):
                for s in range(2):
                    weights_ref[a, c, t * 128 : t * 128 + 128, s * 128 : s * 128 + 128] = (
                        conv_ref[a, t - s, c] if 0 <= t - s <= 2 else zero
                    )


def inner_kernel(field_ref, conv_ref, shifts_ref, weights_ref, outputs_ref):
    lay_interior(field_ref, shifts_ref, 0, 16, 0)
    lay_weights(conv_ref, weights_ref)
    for first, count in ((1, 7), (8, 7)):
        acc = None
        for a in range(3):
            for c in range(3):
                part = dot(window(shifts_ref, c, first + a - 1, count), weights_ref[a, c], NN)
                acc = part if acc is None else acc + part
        for s in range(2):
            field = field_ref[first : first + count, :, s].astype(F32)
            outputs_ref[first : first + count, :, s] = (
                acc[:, s * 128 : s * 128 + 128].reshape(count, 8, 16, 128) + field
            ).astype(BF)


def taps(rows):
    return jnp.concatenate(
        [rows[t // 2 : t // 2 + 8, t % 2].reshape(128, 128) for t in range(4)], axis=1
    )


def main_kernel(
    coords_ref, parent_ref, near_ref, field_ref, partner_ref, other_ref, shifts_ref, weights_ref,
    inner_ref, down_ref, grads_ref, spread_ref,
    kept_rows_ref, sent_ref, keep_ref, low_shifts_ref, high_shifts_ref, edges_ref, sums_ref,
):
    x, oy, oz = coords_ref[0], coords_ref[1] % 2, coords_ref[2] % 2
    first_core = x % 2 == 0
    kept = (parent_ref[0] == x).astype(F32)

    def part_rows(tap, rows):
        kept_rows_ref[tap] = jnp.where(first_core, rows[0:64], rows[64:128])
        sent_ref[tap] = jnp.where(first_core, rows[64:128], rows[0:64]).astype(BF)

    kept_rows_ref[35] = jnp.zeros((64, 128), F32)
    sent_ref[35] = jnp.zeros((64, 128), BF)
    sent_ref[52] = jnp.full((64, 128), oy, jnp.int32).astype(F32).astype(BF)
    partner, other = partner_ref[0].astype(F32), other_ref[0].astype(F32)
    low = jnp.where(first_core, other, partner).reshape(16, 16, 128)
    high = jnp.where(first_core, partner, other).reshape(16, 16, 128)
    lay_slab(low, near_flag(near_ref, 0), low_shifts_ref)
    lay_slab(high, near_flag(near_ref, 17), high_shifts_ref)

    acc = None
    for a in range(3):
        for c in range(3):
            below = taps(low_shifts_ref[c] if a == 0 else shifts_ref[c, a - 1])
            above = taps(high_shifts_ref[c] if a == 2 else shifts_ref[c, 14 + a])
            part = dot(jnp.concatenate([below, above], axis=0), weights_ref[a, c], NN)
            acc = part if acc is None else acc + part
    for s in range(2):
        for k in range(2):
            value = acc[128 * k : 128 * k + 128, s * 128 : s * 128 + 128].reshape(8, 16, 128)
            edges_ref[k, :, s] = (value + field_ref[15 * k, :, s].astype(F32)).astype(BF)

    down = down_ref[...]

    def corner(i, p, q):
        at = 2 * i + p
        rows = edges_ref[at // 15, :, q] if at in (0, 15) else inner_ref[at, :, q]
        return rows.reshape(128, 128)

    for i in range(8):
        corners = jnp.concatenate([corner(i, p, q) for p in range(2) for q in range(2)], axis=1)
        sums = dot(corners, down, NN)
        sums_ref[i, 0] = sums[:, 0:128]
        sums_ref[i, 1] = sums[:, 128:256]
        block = sums_ref[i, 0, pl.ds(0, 64, stride=2), :] + sums_ref[i, 1, pl.ds(1, 64, stride=2), :]
        block = block.reshape(8, 8, 128)
        none = jnp.zeros_like(block)
        low = jnp.where(oz == 0, block, none)
        high = jnp.where(oz == 0, none, block)
        placed = jnp.concatenate([low, high], axis=1).reshape(128, 128)
        keep_ref[i] = (placed * kept).astype(BF).reshape(8, 16, 128)
        away = (placed * (1 - kept)).astype(BF)
        sent_ref[36 + 2 * i] = away[0:64]
        sent_ref[37 + 2 * i] = away[64:128]

    spread = spread_ref[...].reshape(1024, 256)
    for p in range(2):
        for q in range(2):
            rows = jnp.concatenate([corner(i, p, q) for i in range(8)], axis=0)
            result = dot(rows, spread, TN) * (1.0 / 1024)
            part_rows(27 + 4 * p + 2 * q, result[:, 0:128])
            part_rows(28 + 4 * p + 2 * q, result[:, 128:256])

    pair = jnp.concatenate([grads_ref[:, :, s].reshape(2048, 128) for s in range(2)], axis=1)
    for a in range(3):
        for c in range(3):
            if a == 0:
                rows = jnp.concatenate(
                    [taps(low_shifts_ref[c]), window(shifts_ref, c, 0, 15)], axis=0
                )
            elif a == 1:
                rows = window(shifts_ref, c, 0, 16)
            else:
                rows = jnp.concatenate(
                    [window(shifts_ref, c, 1, 15), taps(high_shifts_ref[c])], axis=0
                )
            result = dot(rows, pair, TN) * (1.0 / 1024)
            for b in range(3):
                part_rows(
                    9 * a + 3 * b + c,
                    result[b * 128 : b * 128 + 128, 0:128]
                    + result[b * 128 + 128 : b * 128 + 256, 128:256],
                )


def input_kernel(near_ref, field_hbm, partner_hbm, other_hbm, conv_hbm, *refs, half, tile=4):
    (result_ref, token_ref, shifts_ref, weights_ref, held_ref, field_ref, layer_ref, conv_ref,
     sems) = refs[-9:]
    token_ref[...] = jnp.zeros_like(token_ref)
    first_layer = 7 * half
    fetches = [
        pltpu.make_async_copy(
            field_hbm.at[pl.ds(first_layer + 3 * k, 3)], field_ref.at[pl.ds(3 * k, 3)], sems.at[2 + k]
        )
        for k in range(3)
    ]
    layer_copies = [
        pltpu.make_async_copy(partner_hbm.at[1], layer_ref.at[0], sems.at[5]),
        pltpu.make_async_copy(other_hbm.at[1], layer_ref.at[1], sems.at[9]),
    ]
    conv_copies = [
        pltpu.make_async_copy(conv_hbm.at[a], conv_ref.at[a], sems.at[6 + a]) for a in range(3)
    ]
    for copy in (*fetches, *layer_copies, *conv_copies):
        copy.start()
    for k in range(3):
        fetches[k].wait()
        lay_interior(field_ref, shifts_ref, 3 * k, 3 * k + 3, 1 - half)
    for copy in layer_copies:
        copy.wait()
    layer = jnp.where(
        lax.axis_index("core") == half, layer_ref[1].astype(F32), layer_ref[0].astype(F32)
    )
    lay_slab(
        layer.reshape(16, 16, 128), near_flag(near_ref, 17 * half), shifts_ref.at[:, 9 * half]
    )
    zero = jnp.zeros((128, 128), BF)
    for a in (2, 1, 0):
        conv_copies[2 - a].wait()
        for c in range(3):
            for t in range(4):
                for s in range(2):
                    weights_ref[a, c, s * 128 : s * 128 + 128, t * 128 : t * 128 + 128] = (
                        conv_ref[2 - a, 2 - t + s, 2 - c] if 0 <= t - s <= 2 else zero
                    )
    copies = []
    for step in range(8 // tile):
        first = step * tile
        acc = None
        for a in range(3):
            for c in range(3):
                part = dot(window(shifts_ref, c, first + a, tile), weights_ref[a, c], NT)
                acc = part if acc is None else acc + part
        here = 8 * half + first
        for s in range(2):
            field = field_ref[first + half : first + half + tile, :, s].astype(F32)
            held_ref[first : first + tile, :, s] = (
                acc[:, s * 128 : s * 128 + 128].reshape(tile, 8, 16, 128) + field
            ).astype(BF)
        copy = pltpu.make_async_copy(
            held_ref.at[pl.ds(first, tile)], result_ref.at[pl.ds(here, tile)], sems.at[step]
        )
        copy.start()
        copies.append(copy)
    for copy in copies:
        copy.wait()


def coarse_kernel(coords_ref, keep_ref, got_ref, coarse_ref, token_ref, held_ref, sems):
    token_ref[...] = jnp.zeros_like(token_ref)
    upper, oy = coords_ref[0] % 2, coords_ref[1] % 2
    there = got_ref[52, 0:16].astype(F32)
    none = jnp.zeros((8, 16, 128), BF)
    for i in range(8):
        rows = jnp.concatenate([got_ref[36 + 2 * i], got_ref[37 + 2 * i]], axis=0)
        rows = rows.reshape(8, 16, 128).astype(F32)
        held_ref[0, i, pl.ds(8 * oy, 8)] = keep_ref[i]
        held_ref[0, i, pl.ds(8 - 8 * oy, 8)] = none
        held_ref[1, i, 0:8] = jnp.where(there == 0, rows, 0.0).astype(BF)
        held_ref[1, i, 8:16] = jnp.where(there == 1, rows, 0.0).astype(BF)
    keep = pltpu.make_async_copy(held_ref.at[0], coarse_ref.at[pl.ds(8 * upper, 8)], sems.at[0])
    got = pltpu.make_async_copy(held_ref.at[1], coarse_ref.at[pl.ds(8 - 8 * upper, 8)], sems.at[1])
    keep.start()
    got.start()
    keep.wait()
    got.wait()


ANY = pl.BlockSpec(memory_space=pl.ANY)
HBM = pl.BlockSpec(memory_space=pltpu.HBM)
TOKEN = jax.ShapeDtypeStruct((8, 128), F32)
sds = jax.ShapeDtypeStruct


def call(kernel, ins, outs, scratch=(), flops=0, moved=1 << 20, limit=8, out=VMEM, **kw):
    return pl.pallas_call(
        kernel,
        in_specs=ins,
        out_specs=[VMEM if shape is TOKEN else out for shape in outs],
        out_shape=outs,
        scratch_shapes=list(scratch),
        cost_estimate=pl.CostEstimate(flops=flops, bytes_accessed=moved, transcendentals=0),
        compiler_params=pltpu.CompilerParams(vmem_limit_bytes=limit << 20),
        **kw,
    )


def prepare_call(coords, cotangent, down, field, after):
    layer = sds((8, 2, 16, 128), BF)
    return call(
        prepare_kernel, [SMEM] + [HBM] * 3 + [ANY],
        [sds((8, 8, 16, 128), BF), sds((512, 256), BF), layer, layer],
        [pltpu.VMEM((2, 2, 2, 128, 128), BF), pltpu.SemaphoreType.DMA((4,))], moved=1 << 20,
    )(coords, cotangent, down, field, after)


def grad_call(coords, parent, mine, theirs, down, partner, other):
    layers = sds((2, 8, 2, 16, 128), BF)
    return call(
        grad_kernel, [SMEM] * 2 + [VMEM] * 5,
        [sds((16, 8, 2, 16, 128), BF), sds((8, 128, 256), BF), layers, layers],
        [pltpu.VMEM((8, 128, 128), F32)], flops=2 * 2**27, moved=4 << 20,
    )(coords, parent, mine, theirs, down, partner, other)


def inner_call(field, conv):
    return call(
        inner_kernel, [VMEM] * 2,
        [sds((3, 16, 9, 2, 16, 128), BF), sds((3, 3, 512, 256), BF), sds((16, 8, 2, 16, 128), BF)],
        flops=2 * 9 * 2048 * 512 * 256, moved=2 << 20, limit=16,
    )(field, conv)


def main_call(coords, parent, near, field, partner, other, inner, down, grads, spread):
    slab = pltpu.VMEM((3, 9, 2, 16, 128), BF)
    return call(
        main_kernel, [SMEM] * 3 + [VMEM] * 9,
        [sds((36, 64, 128), F32), sds((53, 64, 128), BF), sds((8, 8, 16, 128), BF)],
        [slab, slab, pltpu.VMEM((2, 8, 2, 16, 128), BF), pltpu.VMEM((8, 2, 128, 128), F32)],
        flops=2 * 9 * 2048 * 512 * 256, limit=24,
    )(coords, parent, near, field, partner, other, *inner, down, grads, spread)


def input_call(near, field, partner, other, conv, after, half, base=None):
    ins, values = [SMEM] + [HBM] * 4 + [ANY], [near, field, partner, other, conv, after]
    aliases = {}
    if base is not None:
        ins, values, aliases = ins + [ANY], values + [base], {6: 0}
    return call(
        functools.partial(input_kernel, half=half), ins, [sds((16, 8, 2, 16, 128), BF), TOKEN],
        [pltpu.VMEM((3, 10, 9, 2, 16, 128), BF), pltpu.VMEM((3, 3, 256, 512), BF),
         pltpu.VMEM((8, 8, 2, 16, 128), BF), pltpu.VMEM((9, 8, 2, 16, 128), BF),
         pltpu.VMEM((2, 8, 2, 16, 128), BF), pltpu.VMEM((3, 3, 3, 128, 128), BF),
         pltpu.SemaphoreType.DMA((10,))],
        flops=9 * 2048 * 512 * 256, limit=24, out=ANY, input_output_aliases=aliases,
    )(*values)


def coarse_call(coords, keep, got, after):
    def kernel(coords_ref, keep_ref, got_ref, after_ref, *refs):
        coarse_kernel(coords_ref, keep_ref, got_ref, *refs)

    return call(
        kernel, [SMEM] + [VMEM] * 2 + [ANY], [sds((16, 16, 16, 128), BF), TOKEN],
        [pltpu.VMEM((2, 8, 16, 16, 128), BF), pltpu.SemaphoreType.DMA((2,))], out=ANY,
    )(coords, keep, got, after)


def add_halves(kept_ref, got_ref, total_ref):
    total_ref[...] = (kept_ref[...] + got_ref[0:36].astype(F32)).astype(BF)


def add_sixteen(got_ref, *refs):
    total = got_ref[0].astype(F32)
    for k in range(1, 16):
        total = total + got_ref[k].astype(F32)
    refs[-1][...] = total.astype(BF)


def add_in_order(own_ref, *refs):
    y = lax.axis_index("dp")
    total_ref, slots_ref = refs[-2:]
    for k, ref in enumerate((own_ref, *refs[:3])):
        slots_ref[(y - k + 4) % 4] = ref[...].astype(F32)
    total = ((slots_ref[0] + slots_ref[1]) + (slots_ref[2] + slots_ref[3])).astype(BF)
    for k in range(16):
        total_ref[k] = total


def write_half(rows_ref, *refs, own):
    conv_ref, down_ref, token_ref, wide_ref, sems = refs[-5:]
    token_ref[...] = jnp.zeros_like(token_ref)
    core = lax.axis_index("core")
    here = pl.ds(pl.multiple_of(64 * (core if own else 1 - core), 64), 64)
    copies = []
    for k, (start, stop) in enumerate(((0, 9), (9, 18), (18, 27), (27, 35))):
        wide_ref[start:stop] = rows_ref[start:stop].astype(F32)
        if start < 27:
            target = conv_ref.at[start:stop, here]
        else:
            target = down_ref.at[:, here]
        copies.append(pltpu.make_async_copy(wide_ref.at[start:stop], target, sems.at[k]))
        copies[-1].start()
    for copy in copies:
        copy.wait()


def write_call(rows, bases=(), own=True):
    return call(
        functools.partial(write_half, own=own), [VMEM] + [ANY] * len(bases),
        [sds((27, 128, 128), F32), sds((8, 128, 128), F32), TOKEN],
        [pltpu.VMEM((36, 64, 128), F32), pltpu.SemaphoreType.DMA((4,))], out=ANY,
        input_output_aliases={1: 0, 2: 1} if bases else {},
    )(rows, *bases)[:2]


def over_core(value):
    return lax.ppermute(value, "core", [(0, 1), (1, 0)])


def over_y(value, by):
    return lax.ppermute(value, "dp", [(i, (i + by) % 4) for i in range(4)])


def over_plane(value):
    return lax.all_to_all(value, ("z", "x"), 0, 0, tiled=True)


def stage(kernel, values, outs, after=(), scratch=()):
    return call(kernel, [VMEM] * len(values) + [ANY] * len(after), outs, scratch)(*values, *after)


def over_other(value):
    pairs = [(i, i + 1) for i in range(1, 31, 2)] + [(i + 1, i) for i in range(1, 31, 2)]
    return lax.ppermute(value, ("z", "x", "core"), pairs)


def local(features, conv_weight, down_weight, coarse_cotangent, brick_coords, neighbours, parents):
    coords, near, parent = brick_coords.reshape(3), neighbours.reshape(26), parents.reshape(1)
    core = lax.axis_index("core")
    cotangent = coarse_cotangent.reshape(16, 16, 16, 128)
    half = lax.dynamic_slice_in_dim(cotangent, 8 * (1 - core), 8)
    theirs = over_core(half)
    field = features.reshape(16, 8, 2, 16, 128)
    far = functools.partial(pltpu.with_memory_space_constraint, memory_space=pltpu.HBM)
    mine, down, *layers = prepare_call(far(coords), far(cotangent), far(down_weight), far(field), half)
    grads, spread, to_partner, to_other = grad_call(far(coords), parent, mine, theirs, down, *layers)
    partner, other = over_core(to_partner), over_other(to_other)
    inner = inner_call(field, conv_weight)
    kept, sent, keep = main_call(
        coords, parent, near, field, partner, other, inner, down, grads, spread
    )

    got = over_core(sent)
    own = stage(add_halves, (kept, got), [sds((36, 64, 128), BF)])[0]
    gots = over_plane(own.reshape(16, 144, 128))
    partial_grad, token = input_call(near, grads, partner, other, far(conv_weight), own, 0)
    coarse, token = coarse_call(coords, keep, got, token)
    own = stage(add_sixteen, (gots,), [sds((144, 128), BF)], (token,))[0]
    gots = [over_y(own, k) for k in (1, 2, 3)]
    shares = stage(
        add_in_order, (own, *gots), [sds((16, 144, 128), BF)],
        scratch=[pltpu.VMEM((4, 144, 128), F32)],
    )[0]

    own = over_plane(shares).reshape(36, 64, 128)
    input_grad, token = input_call(near, grads, partner, other, far(conv_weight), shares, 1, partial_grad)
    own, token = lax.optimization_barrier((own, token))
    got = over_core(own)
    halves = write_call(own)
    conv_grad, down_grad = write_call(got, halves, own=False)
    whole = (1, 1, 16, 16, 16, 128)
    return (
        coarse.reshape(whole),
        input_grad.reshape(whole),
        conv_grad.reshape(3, 3, 3, 128, 128),
        down_grad.reshape(2, 2, 2, 128, 128),
    )


def solution(mesh):
    sizes = (mesh.devices.shape[0], 4, 4, 2)
    mesh = jax.sharding.Mesh(mesh.devices.reshape(sizes), ("dp", "z", "x", "core"))
    region = ("z", "x", "core")
    bricks = P("dp", region, None, None, None, None)
    rows = P("dp", region, None)
    return jax.shard_map(
        local,
        mesh=mesh,
        in_specs=(bricks, P(), P(), bricks, rows, rows, P("dp", region)),
        out_specs=(bricks, bricks, P(), P()),
        check_vma=False,
    )
```

```python
import functools
import jax
import jax.numpy as jnp
from jax import lax
from jax.experimental import pallas as pl
from jax.experimental.pallas import tpu as pltpu
from jax.sharding import PartitionSpec as P

BF, F32 = jnp.bfloat16, jnp.float32
SMEM = pl.BlockSpec(memory_space=pltpu.SMEM)
VMEM = pl.BlockSpec(memory_space=pltpu.VMEM)
NN = (((1,), (0,)), ((), ()))
NT = (((1,), (1,)), ((), ()))
TN = (((0,), (0,)), ((), ()))


def dot(lhs, rhs, dims):
    return lax.dot_general(lhs, rhs, dims, preferred_element_type=F32)


def z_index(rows):
    return lax.broadcasted_iota(jnp.int32, (rows, 128), 0) % 16


def lay_interior(field_ref, shifts_ref, start=0, stop=16, base=1):
    z = z_index(256)

    @pl.loop(start, stop)
    def _(x):
        plain = field_ref[x].reshape(256, 128)
        wide = plain.astype(F32)
        lower = jnp.where(z == 0, 0.0, pltpu.roll(wide, 1, 0)).astype(BF)
        upper = jnp.where(z == 15, 0.0, pltpu.roll(wide, 255, 0)).astype(BF)
        for c, value in enumerate((lower, plain, upper)):
            rows = value.reshape(8, 2, 16, 128)
            shifts_ref[c, x + base, 0:8, 1] = rows[:, 0]
            shifts_ref[c, x + base, 1:9, 0] = rows[:, 1]
            shifts_ref[c, x + base, 0, 0] = jnp.zeros((16, 128), BF)
            shifts_ref[c, x + base, 8, 1] = jnp.zeros((16, 128), BF)


def lay_slab(layer, flag, slab_ref):
    def three(value, b):
        rows = value.shape[0] * 16
        wide = value.astype(F32).reshape(rows, 128)
        z = z_index(rows)
        below, same, above = (flag(b, c) for c in (-1, 0, 1))
        lower = jnp.where(
            z == 0, pltpu.roll(wide, rows - 15, 0) * below, pltpu.roll(wide, 1, 0) * same
        )
        upper = jnp.where(
            z == 15, pltpu.roll(wide, 15, 0) * above, pltpu.roll(wide, rows - 1, 0) * same
        )
        return [v.astype(BF) for v in (lower, wide * same, upper)]

    for c, value in enumerate(three(layer, 0)):
        rows = value.reshape(8, 2, 16, 128)
        slab_ref[c, 0:8, 1] = rows[:, 0]
        slab_ref[c, 1:9, 0] = rows[:, 1]
    for c, value in enumerate(three(layer[15:16], -1)):
        slab_ref[c, 0, 0] = value.reshape(16, 128)
    for c, value in enumerate(three(layer[0:1], 1)):
        slab_ref[c, 8, 1] = value.reshape(16, 128)


def near_flag(near_ref, first):
    return lambda b, c: (near_ref[first + 3 * (b + 1) + c + 1] >= 0).astype(F32)


def window(shifts_ref, c, x, count):
    return jnp.concatenate(
        [
            shifts_ref[c, pl.ds(x, count), t // 2 : t // 2 + 8, t % 2].reshape(count * 128, 128)
            for t in range(4)
        ],
        axis=1,
    )


def joined_down(down_ref):
    return jnp.concatenate(
        [
            jnp.concatenate([down_ref[p, q, r] for r in range(2)], axis=1)
            for p in range(2)
            for q in range(2)
        ],
        axis=0,
    )


def prepare_kernel(
    coords_ref, cotangent_hbm, down_hbm, field_hbm, after_ref,
    mine_ref, down_ref, partner_ref, other_ref, held_ref, sems,
):
    x, oy = coords_ref[0], coords_ref[1] % 2
    upper = x % 2
    copies = [
        pltpu.make_async_copy(
            cotangent_hbm.at[pl.ds(8 * upper, 8), pl.ds(8 * oy, 8)], mine_ref, sems.at[0]
        ),
        pltpu.make_async_copy(down_hbm, held_ref, sems.at[1]),
        pltpu.make_async_copy(field_hbm.at[15 - 15 * upper], partner_ref, sems.at[2]),
        pltpu.make_async_copy(field_hbm.at[15 * upper], other_ref, sems.at[3]),
    ]
    for copy in copies:
        copy.start()
    copies[1].wait()
    down_ref[...] = joined_down(held_ref)
    for k in (0, 2, 3):
        copies[k].wait()


def grad_kernel(
    coords_ref, parent_ref, mine_ref, theirs_ref, down_ref, partner_ref, other_ref,
    grads_ref, spread_ref, to_partner_ref, to_other_ref, wide_ref,
):
    x, oy, oz = coords_ref[0], coords_ref[1] % 2, coords_ref[2] % 2
    is_own = parent_ref[0] == x
    down = down_ref[...]
    to_partner_ref[0] = partner_ref[...]
    to_other_ref[0] = other_ref[...]
    wide_ref[...] = jnp.zeros_like(wide_ref)
    for i in range(8):
        mine = mine_ref[i].astype(F32)
        theirs = theirs_ref[i, pl.ds(8 * oy, 8)].astype(F32)
        both = jnp.where(is_own, mine, theirs)
        part = jnp.where(oz == 0, both[:, 0:8], both[:, 8:16]).reshape(64, 128)
        wide_ref[i, pl.ds(0, 64, stride=2), :] = part
    for i in range(8):
        even = wide_ref[i]
        spread = jnp.concatenate([even, pltpu.roll(even, 1, 0)], axis=1).astype(BF)
        spread_ref[i] = spread
        grads = dot(spread, down, NT).astype(BF)
        for p in range(2):
            for q in range(2):
                at = (2 * p + q) * 128
                part = grads[:, at : at + 128].reshape(8, 16, 128)
                grads_ref[2 * i + p, :, q] = part
    upper = x % 2
    to_partner_ref[1] = grads_ref[15 - 15 * upper]
    to_other_ref[1] = grads_ref[15 * upper]


def lay_weights(conv_ref, weights_ref):
    zero = jnp.zeros((128, 128), BF)
    for a in range(3):
        for c in range(3):
            for t in range(4):
                for s in range(2):
                    weights_ref[a, c, t * 128 : t * 128 + 128, s * 128 : s * 128 + 128] = (
                        conv_ref[a, t - s, c] if 0 <= t - s <= 2 else zero
                    )


def inner_kernel(field_ref, conv_ref, shifts_ref, weights_ref, outputs_ref):
    lay_interior(field_ref, shifts_ref, 0, 16, 0)
    lay_weights(conv_ref, weights_ref)
    for first, count in ((1, 7), (8, 7)):
        acc = None
        for a in range(3):
            for c in range(3):
                part = dot(window(shifts_ref, c, first + a - 1, count), weights_ref[a, c], NN)
                acc = part if acc is None else acc + part
        for s in range(2):
            field = field_ref[first : first + count, :, s].astype(F32)
            outputs_ref[first : first + count, :, s] = (
                acc[:, s * 128 : s * 128 + 128].reshape(count, 8, 16, 128) + field
            ).astype(BF)


def taps(rows):
    return jnp.concatenate(
        [rows[t // 2 : t // 2 + 8, t % 2].reshape(128, 128) for t in range(4)], axis=1
    )


def main_kernel(
    coords_ref, parent_ref, near_ref, field_ref, partner_ref, other_ref, shifts_ref, weights_ref,
    inner_ref, down_ref, grads_ref, spread_ref,
    kept_rows_ref, sent_ref, keep_ref, low_shifts_ref, high_shifts_ref, edges_ref, sums_ref,
):
    x, oy, oz = coords_ref[0], coords_ref[1] % 2, coords_ref[2] % 2
    first_core = x % 2 == 0
    kept = (parent_ref[0] == x).astype(F32)

    def part_rows(tap, rows):
        kept_rows_ref[tap] = jnp.where(first_core, rows[0:64], rows[64:128])
        sent_ref[tap] = jnp.where(first_core, rows[64:128], rows[0:64]).astype(BF)

    kept_rows_ref[35] = jnp.zeros((64, 128), F32)
    sent_ref[35] = jnp.zeros((64, 128), BF)
    sent_ref[52] = jnp.full((64, 128), oy, jnp.int32).astype(F32).astype(BF)
    partner, other = partner_ref[0].astype(F32), other_ref[0].astype(F32)
    low = jnp.where(first_core, other, partner).reshape(16, 16, 128)
    high = jnp.where(first_core, partner, other).reshape(16, 16, 128)
    lay_slab(low, near_flag(near_ref, 0), low_shifts_ref)
    lay_slab(high, near_flag(near_ref, 17), high_shifts_ref)

    acc = None
    for a in range(3):
        for c in range(3):
            below = taps(low_shifts_ref[c] if a == 0 else shifts_ref[c, a - 1])
            above = taps(high_shifts_ref[c] if a == 2 else shifts_ref[c, 14 + a])
            part = dot(jnp.concatenate([below, above], axis=0), weights_ref[a, c], NN)
            acc = part if acc is None else acc + part
    for s in range(2):
        for k in range(2):
            value = acc[128 * k : 128 * k + 128, s * 128 : s * 128 + 128].reshape(8, 16, 128)
            edges_ref[k, :, s] = (value + field_ref[15 * k, :, s].astype(F32)).astype(BF)

    down = down_ref[...]

    def corner(i, p, q):
        at = 2 * i + p
        rows = edges_ref[at // 15, :, q] if at in (0, 15) else inner_ref[at, :, q]
        return rows.reshape(128, 128)

    for i in range(8):
        corners = jnp.concatenate([corner(i, p, q) for p in range(2) for q in range(2)], axis=1)
        sums = dot(corners, down, NN)
        sums_ref[i, 0] = sums[:, 0:128]
        sums_ref[i, 1] = sums[:, 128:256]
        block = sums_ref[i, 0, pl.ds(0, 64, stride=2), :] + sums_ref[i, 1, pl.ds(1, 64, stride=2), :]
        block = block.reshape(8, 8, 128)
        none = jnp.zeros_like(block)
        low = jnp.where(oz == 0, block, none)
        high = jnp.where(oz == 0, none, block)
        placed = jnp.concatenate([low, high], axis=1).reshape(128, 128)
        keep_ref[i] = (placed * kept).astype(BF).reshape(8, 16, 128)
        away = (placed * (1 - kept)).astype(BF)
        sent_ref[36 + 2 * i] = away[0:64]
        sent_ref[37 + 2 * i] = away[64:128]

    spread = spread_ref[...].reshape(1024, 256)
    for p in range(2):
        for q in range(2):
            rows = jnp.concatenate([corner(i, p, q) for i in range(8)], axis=0)
            result = dot(rows, spread, TN) * (1.0 / 1024)
            part_rows(27 + 4 * p + 2 * q, result[:, 0:128])
            part_rows(28 + 4 * p + 2 * q, result[:, 128:256])

    pair = jnp.concatenate([grads_ref[:, :, s].reshape(2048, 128) for s in range(2)], axis=1)
    for a in range(3):
        for c in range(3):
            if a == 0:
                rows = jnp.concatenate(
                    [taps(low_shifts_ref[c]), window(shifts_ref, c, 0, 15)], axis=0
                )
            elif a == 1:
                rows = window(shifts_ref, c, 0, 16)
            else:
                rows = jnp.concatenate(
                    [window(shifts_ref, c, 1, 15), taps(high_shifts_ref[c])], axis=0
                )
            result = dot(rows, pair, TN) * (1.0 / 1024)
            for b in range(3):
                part_rows(
                    9 * a + 3 * b + c,
                    result[b * 128 : b * 128 + 128, 0:128]
                    + result[b * 128 + 128 : b * 128 + 256, 128:256],
                )


def input_kernel(near_ref, field_hbm, partner_hbm, other_hbm, conv_hbm, *refs, half, tile=4):
    (result_ref, token_ref, shifts_ref, weights_ref, held_ref, field_ref, layer_ref, conv_ref,
     sems) = refs[-9:]
    token_ref[...] = jnp.zeros_like(token_ref)
    first_layer = 7 * half
    fetches = [
        pltpu.make_async_copy(
            field_hbm.at[pl.ds(first_layer + 3 * k, 3)], field_ref.at[pl.ds(3 * k, 3)], sems.at[2 + k]
        )
        for k in range(3)
    ]
    layer_copies = [
        pltpu.make_async_copy(partner_hbm.at[1], layer_ref.at[0], sems.at[5]),
        pltpu.make_async_copy(other_hbm.at[1], layer_ref.at[1], sems.at[9]),
    ]
    conv_copies = [
        pltpu.make_async_copy(conv_hbm.at[a], conv_ref.at[a], sems.at[6 + a]) for a in range(3)
    ]
    for copy in (*fetches, *layer_copies, *conv_copies):
        copy.start()
    for k in range(3):
        fetches[k].wait()
        lay_interior(field_ref, shifts_ref, 3 * k, 3 * k + 3, 1 - half)
    for copy in layer_copies:
        copy.wait()
    layer = jnp.where(
        lax.axis_index("core") == half, layer_ref[1].astype(F32), layer_ref[0].astype(F32)
    )
    lay_slab(
        layer.reshape(16, 16, 128), near_flag(near_ref, 17 * half), shifts_ref.at[:, 9 * half]
    )
    zero = jnp.zeros((128, 128), BF)
    for a in (2, 1, 0):
        conv_copies[2 - a].wait()
        for c in range(3):
            for t in range(4):
                for s in range(2):
                    weights_ref[a, c, s * 128 : s * 128 + 128, t * 128 : t * 128 + 128] = (
                        conv_ref[2 - a, 2 - t + s, 2 - c] if 0 <= t - s <= 2 else zero
                    )
    copies = []
    for step in range(8 // tile):
        first = step * tile
        acc = None
        for a in range(3):
            for c in range(3):
                part = dot(window(shifts_ref, c, first + a, tile), weights_ref[a, c], NT)
                acc = part if acc is None else acc + part
        here = 8 * half + first
        for s in range(2):
            field = field_ref[first + half : first + half + tile, :, s].astype(F32)
            held_ref[first : first + tile, :, s] = (
                acc[:, s * 128 : s * 128 + 128].reshape(tile, 8, 16, 128) + field
            ).astype(BF)
        copy = pltpu.make_async_copy(
            held_ref.at[pl.ds(first, tile)], result_ref.at[pl.ds(here, tile)], sems.at[step]
        )
        copy.start()
        copies.append(copy)
    for copy in copies:
        copy.wait()


def coarse_kernel(coords_ref, keep_ref, got_ref, coarse_ref, token_ref, held_ref, sems):
    token_ref[...] = jnp.zeros_like(token_ref)
    upper, oy = coords_ref[0] % 2, coords_ref[1] % 2
    there = got_ref[52, 0:16].astype(F32)
    none = jnp.zeros((8, 16, 128), BF)
    for i in range(8):
        rows = jnp.concatenate([got_ref[36 + 2 * i], got_ref[37 + 2 * i]], axis=0)
        rows = rows.reshape(8, 16, 128).astype(F32)
        held_ref[0, i, pl.ds(8 * oy, 8)] = keep_ref[i]
        held_ref[0, i, pl.ds(8 - 8 * oy, 8)] = none
        held_ref[1, i, 0:8] = jnp.where(there == 0, rows, 0.0).astype(BF)
        held_ref[1, i, 8:16] = jnp.where(there == 1, rows, 0.0).astype(BF)
    keep = pltpu.make_async_copy(held_ref.at[0], coarse_ref.at[pl.ds(8 * upper, 8)], sems.at[0])
    got = pltpu.make_async_copy(held_ref.at[1], coarse_ref.at[pl.ds(8 - 8 * upper, 8)], sems.at[1])
    keep.start()
    got.start()
    keep.wait()
    got.wait()


ANY = pl.BlockSpec(memory_space=pl.ANY)
HBM = pl.BlockSpec(memory_space=pltpu.HBM)
TOKEN = jax.ShapeDtypeStruct((8, 128), F32)
sds = jax.ShapeDtypeStruct


def call(kernel, ins, outs, scratch=(), flops=0, moved=1 << 20, limit=8, out=VMEM, **kw):
    return pl.pallas_call(
        kernel,
        in_specs=ins,
        out_specs=[VMEM if shape is TOKEN else out for shape in outs],
        out_shape=outs,
        scratch_shapes=list(scratch),
        cost_estimate=pl.CostEstimate(flops=flops, bytes_accessed=moved, transcendentals=0),
        compiler_params=pltpu.CompilerParams(vmem_limit_bytes=limit << 20),
        **kw,
    )


def prepare_call(coords, cotangent, down, field, after):
    layer = sds((8, 2, 16, 128), BF)
    return call(
        prepare_kernel, [SMEM] + [HBM] * 3 + [ANY],
        [sds((8, 8, 16, 128), BF), sds((512, 256), BF), layer, layer],
        [pltpu.VMEM((2, 2, 2, 128, 128), BF), pltpu.SemaphoreType.DMA((4,))], moved=1 << 20,
    )(coords, cotangent, down, field, after)


def grad_call(coords, parent, mine, theirs, down, partner, other):
    layers = sds((2, 8, 2, 16, 128), BF)
    return call(
        grad_kernel, [SMEM] * 2 + [VMEM] * 5,
        [sds((16, 8, 2, 16, 128), BF), sds((8, 128, 256), BF), layers, layers],
        [pltpu.VMEM((8, 128, 128), F32)], flops=2 * 2**27, moved=4 << 20,
    )(coords, parent, mine, theirs, down, partner, other)


def inner_call(field, conv):
    return call(
        inner_kernel, [VMEM] * 2,
        [sds((3, 16, 9, 2, 16, 128), BF), sds((3, 3, 512, 256), BF), sds((16, 8, 2, 16, 128), BF)],
        flops=2 * 9 * 2048 * 512 * 256, moved=2 << 20, limit=16,
    )(field, conv)


def main_call(coords, parent, near, field, partner, other, inner, down, grads, spread):
    slab = pltpu.VMEM((3, 9, 2, 16, 128), BF)
    return call(
        main_kernel, [SMEM] * 3 + [VMEM] * 9,
        [sds((36, 64, 128), F32), sds((53, 64, 128), BF), sds((8, 8, 16, 128), BF)],
        [slab, slab, pltpu.VMEM((2, 8, 2, 16, 128), BF), pltpu.VMEM((8, 2, 128, 128), F32)],
        flops=2 * 9 * 2048 * 512 * 256, limit=24,
    )(coords, parent, near, field, partner, other, *inner, down, grads, spread)


def input_call(near, field, partner, other, conv, after, half, base=None):
    ins, values = [SMEM] + [HBM] * 4 + [ANY], [near, field, partner, other, conv, after]
    aliases = {}
    if base is not None:
        ins, values, aliases = ins + [ANY], values + [base], {6: 0}
    return call(
        functools.partial(input_kernel, half=half), ins, [sds((16, 8, 2, 16, 128), BF), TOKEN],
        [pltpu.VMEM((3, 10, 9, 2, 16, 128), BF), pltpu.VMEM((3, 3, 256, 512), BF),
         pltpu.VMEM((8, 8, 2, 16, 128), BF), pltpu.VMEM((9, 8, 2, 16, 128), BF),
         pltpu.VMEM((2, 8, 2, 16, 128), BF), pltpu.VMEM((3, 3, 3, 128, 128), BF),
         pltpu.SemaphoreType.DMA((10,))],
        flops=9 * 2048 * 512 * 256, limit=24, out=ANY, input_output_aliases=aliases,
    )(*values)


def coarse_call(coords, keep, got, after):
    def kernel(coords_ref, keep_ref, got_ref, after_ref, *refs):
        coarse_kernel(coords_ref, keep_ref, got_ref, *refs)

    return call(
        kernel, [SMEM] + [VMEM] * 2 + [ANY], [sds((16, 16, 16, 128), BF), TOKEN],
        [pltpu.VMEM((2, 8, 16, 16, 128), BF), pltpu.SemaphoreType.DMA((2,))], out=ANY,
    )(coords, keep, got, after)


def add_halves(kept_ref, got_ref, total_ref):
    total_ref[...] = (kept_ref[...] + got_ref[0:36].astype(F32)).astype(BF)


def add_sixteen(got_ref, *refs):
    total = got_ref[0].astype(F32)
    for k in range(1, 16):
        total = total + got_ref[k].astype(F32)
    refs[-1][...] = total


def add_in_order(own_ref, *refs):
    y = lax.axis_index("dp")
    total_ref, slots_ref = refs[-2:]
    for k, ref in enumerate((own_ref, *refs[:3])):
        slots_ref[(y - k + 4) % 4] = ref[...]
    total = ((slots_ref[0] + slots_ref[1]) + (slots_ref[2] + slots_ref[3])).astype(BF)
    for k in range(16):
        total_ref[k] = total


def after_call(value, token):
    def kernel(value_ref, token_ref, same_ref):
        pass

    return call(
        kernel, [ANY] * 2, [sds(value.shape, value.dtype)], out=ANY, input_output_aliases={0: 0},
        moved=1024,
    )(value, token)[0]


def write_half(rows_ref, *refs, own):
    conv_ref, down_ref, token_ref, wide_ref, sems = refs[-5:]
    token_ref[...] = jnp.zeros_like(token_ref)
    core = lax.axis_index("core")
    here = pl.ds(pl.multiple_of(64 * (core if own else 1 - core), 64), 64)
    copies = []
    for k, (start, stop) in enumerate(((0, 9), (9, 18), (18, 27), (27, 35))):
        wide_ref[start:stop] = rows_ref[start:stop].astype(F32)
        if start < 27:
            target = conv_ref.at[start:stop, here]
        else:
            target = down_ref.at[:, here]
        copies.append(pltpu.make_async_copy(wide_ref.at[start:stop], target, sems.at[k]))
        copies[-1].start()
    for copy in copies:
        copy.wait()


def write_call(rows, bases=(), own=True):
    return call(
        functools.partial(write_half, own=own), [VMEM] + [ANY] * len(bases),
        [sds((27, 128, 128), F32), sds((8, 128, 128), F32), TOKEN],
        [pltpu.VMEM((36, 64, 128), F32), pltpu.SemaphoreType.DMA((4,))], out=ANY,
        input_output_aliases={1: 0, 2: 1} if bases else {},
    )(rows, *bases)[:2]


def over_core(value):
    return lax.ppermute(value, "core", [(0, 1), (1, 0)])


def over_y(value, by):
    return lax.ppermute(value, "dp", [(i, (i + by) % 4) for i in range(4)])


def over_plane(value):
    return lax.all_to_all(value, ("z", "x"), 0, 0, tiled=True)


def stage(kernel, values, outs, after=(), scratch=()):
    return call(kernel, [VMEM] * len(values) + [ANY] * len(after), outs, scratch)(*values, *after)


def over_other(value):
    pairs = [(i, i + 1) for i in range(1, 31, 2)] + [(i + 1, i) for i in range(1, 31, 2)]
    return lax.ppermute(value, ("z", "x", "core"), pairs)


def local(features, conv_weight, down_weight, coarse_cotangent, brick_coords, neighbours, parents):
    coords, near, parent = brick_coords.reshape(3), neighbours.reshape(26), parents.reshape(1)
    core = lax.axis_index("core")
    cotangent = coarse_cotangent.reshape(16, 16, 16, 128)
    half = lax.dynamic_slice_in_dim(cotangent, 8 * (1 - core), 8)
    theirs = over_core(half)
    field = features.reshape(16, 8, 2, 16, 128)
    far = functools.partial(pltpu.with_memory_space_constraint, memory_space=pltpu.HBM)
    mine, down, *layers = prepare_call(far(coords), far(cotangent), far(down_weight), far(field), half)
    grads, spread, to_partner, to_other = grad_call(far(coords), parent, mine, theirs, down, *layers)
    partner, other = over_core(to_partner), over_other(to_other)
    inner = inner_call(field, conv_weight)
    kept, sent, keep = main_call(
        coords, parent, near, field, partner, other, inner, down, grads, spread
    )

    got = over_core(sent)
    own = stage(add_halves, (kept, got), [sds((36, 64, 128), BF)])[0]
    gots = over_plane(own.reshape(16, 144, 128))
    partial_grad, token = input_call(near, grads, partner, other, far(conv_weight), own, 0)
    coarse, token = coarse_call(coords, keep, got, token)
    own = stage(add_sixteen, (gots,), [sds((144, 128), F32)], (token,))[0]
    gots = [over_y(own, k) for k in (1, 2, 3)]
    shares = stage(
        add_in_order, (own, *gots), [sds((16, 144, 128), BF)],
        scratch=[pltpu.VMEM((4, 144, 128), F32)],
    )[0]

    own = over_plane(shares).reshape(36, 64, 128)
    input_grad, token = input_call(near, grads, partner, other, far(conv_weight), shares, 1, partial_grad)
    own = after_call(own, token)
    got = over_core(own)
    halves = write_call(own)
    conv_grad, down_grad = write_call(got, halves, own=False)
    whole = (1, 1, 16, 16, 16, 128)
    return (
        coarse.reshape(whole),
        input_grad.reshape(whole),
        conv_grad.reshape(3, 3, 3, 128, 128),
        down_grad.reshape(2, 2, 2, 128, 128),
    )


def solution(mesh):
    sizes = (mesh.devices.shape[0], 4, 4, 2)
    mesh = jax.sharding.Mesh(mesh.devices.reshape(sizes), ("dp", "z", "x", "core"))
    region = ("z", "x", "core")
    bricks = P("dp", region, None, None, None, None)
    rows = P("dp", region, None)
    return jax.shard_map(
        local,
        mesh=mesh,
        in_specs=(bricks, P(), P(), bricks, rows, rows, P("dp", region)),
        out_specs=(bricks, bricks, P(), P()),
        check_vma=False,
    )
```

```python
import functools
import jax
import jax.numpy as jnp
from jax import lax
from jax.experimental import pallas as pl
from jax.experimental.pallas import tpu as pltpu
from jax.sharding import PartitionSpec as P

BF, F32 = jnp.bfloat16, jnp.float32
SMEM = pl.BlockSpec(memory_space=pltpu.SMEM)
VMEM = pl.BlockSpec(memory_space=pltpu.VMEM)
NN = (((1,), (0,)), ((), ()))
NT = (((1,), (1,)), ((), ()))
TN = (((0,), (0,)), ((), ()))


def dot(lhs, rhs, dims):
    return lax.dot_general(lhs, rhs, dims, preferred_element_type=F32)


def z_index(rows):
    return lax.broadcasted_iota(jnp.int32, (rows, 128), 0) % 16


def lay_interior(field_ref, shifts_ref, start=0, stop=16, base=1):
    z = z_index(256)

    for x in range(start, stop):
        plain = field_ref[x].reshape(256, 128)
        wide = plain.astype(F32)
        lower = jnp.where(z == 0, 0.0, pltpu.roll(wide, 1, 0)).astype(BF)
        upper = jnp.where(z == 15, 0.0, pltpu.roll(wide, 255, 0)).astype(BF)
        for c, value in enumerate((lower, plain, upper)):
            rows = value.reshape(8, 2, 16, 128)
            shifts_ref[c, x + base, 0:8, 1] = rows[:, 0]
            shifts_ref[c, x + base, 1:9, 0] = rows[:, 1]
            shifts_ref[c, x + base, 0, 0] = jnp.zeros((16, 128), BF)
            shifts_ref[c, x + base, 8, 1] = jnp.zeros((16, 128), BF)


def lay_slab(layer, flag, slab_ref):
    def three(value, b):
        rows = value.shape[0] * 16
        wide = value.astype(F32).reshape(rows, 128)
        z = z_index(rows)
        below, same, above = (flag(b, c) for c in (-1, 0, 1))
        lower = jnp.where(
            z == 0, pltpu.roll(wide, rows - 15, 0) * below, pltpu.roll(wide, 1, 0) * same
        )
        upper = jnp.where(
            z == 15, pltpu.roll(wide, 15, 0) * above, pltpu.roll(wide, rows - 1, 0) * same
        )
        return [v.astype(BF) for v in (lower, wide * same, upper)]

    for c, value in enumerate(three(layer, 0)):
        rows = value.reshape(8, 2, 16, 128)
        slab_ref[c, 0:8, 1] = rows[:, 0]
        slab_ref[c, 1:9, 0] = rows[:, 1]
    for c, value in enumerate(three(layer[15:16], -1)):
        slab_ref[c, 0, 0] = value.reshape(16, 128)
    for c, value in enumerate(three(layer[0:1], 1)):
        slab_ref[c, 8, 1] = value.reshape(16, 128)


def near_flag(near_ref, first):
    return lambda b, c: (near_ref[first + 3 * (b + 1) + c + 1] >= 0).astype(F32)


def window(shifts_ref, c, x, count):
    return jnp.concatenate(
        [
            shifts_ref[c, pl.ds(x, count), t // 2 : t // 2 + 8, t % 2].reshape(count * 128, 128)
            for t in range(4)
        ],
        axis=1,
    )


def prepare_kernel(
    cotangent_hbm, down_hbm, field_hbm, after_ref,
    mine_ref, down_ref, partner_ref, other_ref, sems,
):
    upper = lax.axis_index("core")
    copies = [
        pltpu.make_async_copy(field_hbm.at[15 - 15 * upper], partner_ref, sems.at[0]),
        pltpu.make_async_copy(field_hbm.at[15 * upper], other_ref, sems.at[1]),
    ]
    for k in range(4):
        copies.append(
            pltpu.make_async_copy(
                cotangent_hbm.at[pl.ds(8 * upper + 2 * k, 2)], mine_ref.at[2 * k : 2 * k + 2],
                sems.at[2 + k],
            )
        )
    for p in range(2):
        for q in range(2):
            for r in range(2):
                at = 2 * p + q
                rows, columns = slice(128 * at, 128 * at + 128), slice(128 * r, 128 * r + 128)
                copies.append(
                    pltpu.make_async_copy(
                        down_hbm.at[p, q, r], down_ref.at[rows, columns], sems.at[6 + 2 * at + r]
                    )
                )
    for copy in copies:
        copy.start()
    for copy in copies:
        copy.wait()


def grad_kernel(
    coords_ref, parent_ref, mine_ref, theirs_ref, down_ref, partner_ref, other_ref,
    grads_ref, spread_ref, to_partner_ref, to_other_ref, wide_ref,
):
    x, oy, oz = coords_ref[0], coords_ref[1] % 2, coords_ref[2] % 2
    is_own = parent_ref[0] == x
    down = down_ref[...]
    to_partner_ref[0] = partner_ref[...]
    to_other_ref[0] = other_ref[...]
    wide_ref[...] = jnp.zeros_like(wide_ref)
    for i in range(8):
        mine = mine_ref[i, pl.ds(8 * oy, 8)].astype(F32)
        theirs = theirs_ref[i, pl.ds(8 * oy, 8)].astype(F32)
        both = jnp.where(is_own, mine, theirs)
        part = jnp.where(oz == 0, both[:, 0:8], both[:, 8:16]).reshape(64, 128)
        wide_ref[i, pl.ds(0, 64, stride=2), :] = part
    for i in range(8):
        even = wide_ref[i]
        spread = jnp.concatenate([even, pltpu.roll(even, 1, 0)], axis=1).astype(BF)
        spread_ref[i] = spread
        grads = dot(spread, down, NT).astype(BF)
        for p in range(2):
            for q in range(2):
                at = (2 * p + q) * 128
                part = grads[:, at : at + 128].reshape(8, 16, 128)
                grads_ref[2 * i + p, :, q] = part
    upper = x % 2
    to_partner_ref[1] = grads_ref[15 - 15 * upper]
    to_other_ref[1] = grads_ref[15 * upper]


def lay_weights(conv_ref, weights_ref):
    zero = jnp.zeros((128, 128), BF)
    for a in range(3):
        for c in range(3):
            for t in range(4):
                for s in range(2):
                    weights_ref[a, c, t * 128 : t * 128 + 128, s * 128 : s * 128 + 128] = (
                        conv_ref[a, t - s, c] if 0 <= t - s <= 2 else zero
                    )


def inner_kernel(field_ref, conv_ref, shifts_ref, weights_ref, outputs_ref):
    lay_weights(conv_ref, weights_ref)
    lay_interior(field_ref, shifts_ref, 0, 6, 0)
    for first, count in ((1, 4), (5, 4), (9, 4), (13, 2)):
        lay_interior(field_ref, shifts_ref, min(first + 5, 16), min(first + 9, 16), 0)
        acc = None
        for a in range(3):
            for c in range(3):
                part = dot(window(shifts_ref, c, first + a - 1, count), weights_ref[a, c], NN)
                acc = part if acc is None else acc + part
        for s in range(2):
            field = field_ref[first : first + count, :, s].astype(F32)
            outputs_ref[first : first + count, :, s] = (
                acc[:, s * 128 : s * 128 + 128].reshape(count, 8, 16, 128) + field
            ).astype(BF)


def taps(rows):
    return jnp.concatenate(
        [rows[t // 2 : t // 2 + 8, t % 2].reshape(128, 128) for t in range(4)], axis=1
    )


def main_kernel(
    coords_ref, parent_ref, near_ref, field_ref, partner_ref, other_ref, shifts_ref, weights_ref,
    inner_ref, down_ref, grads_ref, spread_ref,
    kept_rows_ref, sent_ref, keep_ref, low_shifts_ref, high_shifts_ref, edges_ref, sums_ref,
):
    x, oy, oz = coords_ref[0], coords_ref[1] % 2, coords_ref[2] % 2
    first_core = x % 2 == 0
    kept = (parent_ref[0] == x).astype(F32)

    def part_rows(tap, rows):
        kept_rows_ref[tap] = jnp.where(first_core, rows[0:64], rows[64:128])
        sent_ref[tap] = jnp.where(first_core, rows[64:128], rows[0:64]).astype(BF)

    kept_rows_ref[35] = jnp.zeros((64, 128), F32)
    sent_ref[35] = jnp.zeros((64, 128), BF)
    sent_ref[52] = jnp.full((64, 128), oy, jnp.int32).astype(F32).astype(BF)
    partner, other = partner_ref[0].astype(F32), other_ref[0].astype(F32)
    low = jnp.where(first_core, other, partner).reshape(16, 16, 128)
    high = jnp.where(first_core, partner, other).reshape(16, 16, 128)
    lay_slab(low, near_flag(near_ref, 0), low_shifts_ref)
    lay_slab(high, near_flag(near_ref, 17), high_shifts_ref)

    acc = None
    for a in range(3):
        for c in range(3):
            below = taps(low_shifts_ref[c] if a == 0 else shifts_ref[c, a - 1])
            above = taps(high_shifts_ref[c] if a == 2 else shifts_ref[c, 14 + a])
            part = dot(jnp.concatenate([below, above], axis=0), weights_ref[a, c], NN)
            acc = part if acc is None else acc + part
    for s in range(2):
        for k in range(2):
            value = acc[128 * k : 128 * k + 128, s * 128 : s * 128 + 128].reshape(8, 16, 128)
            edges_ref[k, :, s] = (value + field_ref[15 * k, :, s].astype(F32)).astype(BF)

    down = down_ref[...]

    def corner(i, p, q):
        at = 2 * i + p
        rows = edges_ref[at // 15, :, q] if at in (0, 15) else inner_ref[at, :, q]
        return rows.reshape(128, 128)

    for i in range(8):
        corners = jnp.concatenate([corner(i, p, q) for p in range(2) for q in range(2)], axis=1)
        sums = dot(corners, down, NN)
        sums_ref[i, 0] = sums[:, 0:128]
        sums_ref[i, 1] = sums[:, 128:256]
        block = sums_ref[i, 0, pl.ds(0, 64, stride=2), :] + sums_ref[i, 1, pl.ds(1, 64, stride=2), :]
        block = block.reshape(8, 8, 128)
        none = jnp.zeros_like(block)
        low = jnp.where(oz == 0, block, none)
        high = jnp.where(oz == 0, none, block)
        placed = jnp.concatenate([low, high], axis=1).reshape(128, 128)
        keep_ref[i] = (placed * kept).astype(BF).reshape(8, 16, 128)
        away = (placed * (1 - kept)).astype(BF)
        sent_ref[36 + 2 * i] = away[0:64]
        sent_ref[37 + 2 * i] = away[64:128]

    spread = spread_ref[...].reshape(1024, 256)
    for p in range(2):
        for q in range(2):
            rows = jnp.concatenate([corner(i, p, q) for i in range(8)], axis=0)
            result = dot(rows, spread, TN) * (1.0 / 1024)
            part_rows(27 + 4 * p + 2 * q, result[:, 0:128])
            part_rows(28 + 4 * p + 2 * q, result[:, 128:256])

    pair = jnp.concatenate([grads_ref[:, :, s].reshape(2048, 128) for s in range(2)], axis=1)
    for a in range(3):
        for c in range(3):
            if a == 0:
                rows = jnp.concatenate(
                    [taps(low_shifts_ref[c]), window(shifts_ref, c, 0, 15)], axis=0
                )
            elif a == 1:
                rows = window(shifts_ref, c, 0, 16)
            else:
                rows = jnp.concatenate(
                    [window(shifts_ref, c, 1, 15), taps(high_shifts_ref[c])], axis=0
                )
            result = dot(rows, pair, TN) * (1.0 / 1024)
            for b in range(3):
                part_rows(
                    9 * a + 3 * b + c,
                    result[b * 128 : b * 128 + 128, 0:128]
                    + result[b * 128 + 128 : b * 128 + 256, 128:256],
                )


def input_kernel(near_ref, field_ref, partner_ref, other_ref, conv_hbm, *refs, half, tile=4):
    result_ref, token_ref, shifts_ref, weights_ref, held_ref, conv_ref, sems = refs[-7:]
    token_ref[...] = jnp.zeros_like(token_ref)
    conv_copies = [
        pltpu.make_async_copy(conv_hbm.at[a], conv_ref.at[a], sems.at[2 + a]) for a in range(3)
    ]
    for copy in conv_copies:
        copy.start()
    lay = functools.partial(lay_interior, field_ref, shifts_ref, base=1 - 8 * half)
    if half == 0:
        lay(0, 5)
    else:
        lay(7, 13)
    layer = jnp.where(
        lax.axis_index("core") == half, other_ref[1].astype(F32), partner_ref[1].astype(F32)
    )
    def lay_edge():
        lay_slab(
            layer.reshape(16, 16, 128), near_flag(near_ref, 17 * half), shifts_ref.at[:, 9 * half]
        )

    if half == 0:
        lay_edge()
    zero = jnp.zeros((128, 128), BF)
    for a in (2, 1, 0):
        conv_copies[2 - a].wait()
        for c in range(3):
            for t in range(4):
                for s in range(2):
                    weights_ref[a, c, s * 128 : s * 128 + 128, t * 128 : t * 128 + 128] = (
                        conv_ref[2 - a, 2 - t + s, 2 - c] if 0 <= t - s <= 2 else zero
                    )
    copies = []
    for step in range(8 // tile):
        first = step * tile
        if step == 1 and half == 0:
            lay(5, 9)
        if step == 1 and half == 1:
            lay(13, 16)
            lay_edge()
        acc = None
        for a in range(3):
            for c in range(3):
                part = dot(window(shifts_ref, c, first + a, tile), weights_ref[a, c], NT)
                acc = part if acc is None else acc + part
        here = 8 * half + first
        for s in range(2):
            field = field_ref[here : here + tile, :, s].astype(F32)
            held_ref[first : first + tile, :, s] = (
                acc[:, s * 128 : s * 128 + 128].reshape(tile, 8, 16, 128) + field
            ).astype(BF)
        copy = pltpu.make_async_copy(
            held_ref.at[pl.ds(first, tile)], result_ref.at[pl.ds(here, tile)], sems.at[step]
        )
        copy.start()
        copies.append(copy)
    for copy in copies:
        copy.wait()


def coarse_kernel(coords_ref, keep_ref, got_ref, coarse_ref, token_ref, held_ref, sems):
    token_ref[...] = jnp.zeros_like(token_ref)
    upper, oy = coords_ref[0] % 2, coords_ref[1] % 2
    there = got_ref[52, 0:16].astype(F32)
    none = jnp.zeros((8, 16, 128), BF)
    for i in range(8):
        rows = jnp.concatenate([got_ref[36 + 2 * i], got_ref[37 + 2 * i]], axis=0)
        rows = rows.reshape(8, 16, 128).astype(F32)
        held_ref[0, i, pl.ds(8 * oy, 8)] = keep_ref[i]
        held_ref[0, i, pl.ds(8 - 8 * oy, 8)] = none
        held_ref[1, i, 0:8] = jnp.where(there == 0, rows, 0.0).astype(BF)
        held_ref[1, i, 8:16] = jnp.where(there == 1, rows, 0.0).astype(BF)
    keep = pltpu.make_async_copy(held_ref.at[0], coarse_ref.at[pl.ds(8 * upper, 8)], sems.at[0])
    got = pltpu.make_async_copy(held_ref.at[1], coarse_ref.at[pl.ds(8 - 8 * upper, 8)], sems.at[1])
    keep.start()
    got.start()
    keep.wait()
    got.wait()


ANY = pl.BlockSpec(memory_space=pl.ANY)
HBM = pl.BlockSpec(memory_space=pltpu.HBM)
TOKEN = jax.ShapeDtypeStruct((8, 128), F32)
sds = jax.ShapeDtypeStruct


def call(kernel, ins, outs, scratch=(), flops=0, moved=1 << 20, limit=8, out=VMEM, **kw):
    return pl.pallas_call(
        kernel,
        in_specs=ins,
        out_specs=[VMEM if shape is TOKEN else out for shape in outs],
        out_shape=outs,
        scratch_shapes=list(scratch),
        cost_estimate=pl.CostEstimate(flops=flops, bytes_accessed=moved, transcendentals=0),
        compiler_params=pltpu.CompilerParams(vmem_limit_bytes=limit << 20),
        **kw,
    )


def prepare_call(cotangent, down, field, after):
    layer = sds((8, 2, 16, 128), BF)
    return call(
        prepare_kernel, [HBM] * 3 + [ANY],
        [sds((8, 16, 16, 128), BF), sds((512, 256), BF), layer, layer],
        [pltpu.SemaphoreType.DMA((14,))], moved=1 << 20,
    )(cotangent, down, field, after)


def grad_call(coords, parent, mine, theirs, down, partner, other):
    layers = sds((2, 8, 2, 16, 128), BF)
    return call(
        grad_kernel, [SMEM] * 2 + [VMEM] * 5,
        [sds((16, 8, 2, 16, 128), BF), sds((8, 128, 256), BF), layers, layers],
        [pltpu.VMEM((8, 128, 128), F32)], flops=2 * 2**27, moved=4 << 20,
    )(coords, parent, mine, theirs, down, partner, other)


def inner_call(field, conv):
    return call(
        inner_kernel, [VMEM] * 2,
        [sds((3, 16, 9, 2, 16, 128), BF), sds((3, 3, 512, 256), BF), sds((16, 8, 2, 16, 128), BF)],
        flops=2 * 9 * 2048 * 512 * 256, moved=2 << 20, limit=16,
    )(field, conv)


def main_call(coords, parent, near, field, partner, other, inner, down, grads, spread):
    slab = pltpu.VMEM((3, 9, 2, 16, 128), BF)
    return call(
        main_kernel, [SMEM] * 3 + [VMEM] * 9,
        [sds((36, 64, 128), F32), sds((53, 64, 128), BF), sds((8, 8, 16, 128), BF)],
        [slab, slab, pltpu.VMEM((2, 8, 2, 16, 128), BF), pltpu.VMEM((8, 2, 128, 128), F32)],
        flops=2 * 9 * 2048 * 512 * 256, limit=24,
    )(coords, parent, near, field, partner, other, *inner, down, grads, spread)


def input_call(near, field, partner, other, conv, after, half, base=None):
    ins, values = [SMEM] + [VMEM] * 3 + [HBM, ANY], [near, field, partner, other, conv, after]
    aliases = {}
    if base is not None:
        ins, values, aliases = ins + [ANY], values + [base], {6: 0}
    return call(
        functools.partial(input_kernel, half=half), ins, [sds((16, 8, 2, 16, 128), BF), TOKEN],
        [pltpu.VMEM((3, 10, 9, 2, 16, 128), BF), pltpu.VMEM((3, 3, 256, 512), BF),
         pltpu.VMEM((8, 8, 2, 16, 128), BF), pltpu.VMEM((3, 3, 3, 128, 128), BF),
         pltpu.SemaphoreType.DMA((5,))],
        flops=9 * 2048 * 512 * 256, limit=24, out=ANY, input_output_aliases=aliases,
    )(*values)


def coarse_call(coords, keep, got, after):
    def kernel(coords_ref, keep_ref, got_ref, after_ref, *refs):
        coarse_kernel(coords_ref, keep_ref, got_ref, *refs)

    return call(
        kernel, [SMEM] + [VMEM] * 2 + [ANY], [sds((16, 16, 16, 128), BF), TOKEN],
        [pltpu.VMEM((2, 8, 16, 16, 128), BF), pltpu.SemaphoreType.DMA((2,))], out=ANY,
    )(coords, keep, got, after)


def add_halves(kept_ref, got_ref, total_ref):
    total_ref[...] = (kept_ref[...] + got_ref[0:36].astype(F32)).astype(BF)


def add_sixteen(got_ref, *refs):
    total = got_ref[0].astype(F32)
    for k in range(1, 16):
        total = total + got_ref[k].astype(F32)
    refs[-1][...] = total


def add_in_order(own_ref, *refs):
    y = lax.axis_index("dp")
    total_ref, slots_ref = refs[-2:]
    for k, ref in enumerate((own_ref, *refs[:3])):
        slots_ref[(y - k + 4) % 4] = ref[...]
    total = ((slots_ref[0] + slots_ref[1]) + (slots_ref[2] + slots_ref[3])).astype(BF)
    for k in range(16):
        total_ref[k] = total


def after_call(value, token):
    def kernel(value_ref, token_ref, same_ref):
        pass

    return call(
        kernel, [ANY] * 2, [sds(value.shape, value.dtype)], out=ANY, input_output_aliases={0: 0},
        moved=1024,
    )(value, token)[0]


def write_half(rows_ref, *refs, own):
    conv_ref, down_ref, token_ref, wide_ref, sems = refs[-5:]
    token_ref[...] = jnp.zeros_like(token_ref)
    core = lax.axis_index("core")
    here = pl.ds(pl.multiple_of(64 * (core if own else 1 - core), 64), 64)
    copies = []
    for k, (start, stop) in enumerate(((0, 9), (9, 18), (18, 27), (27, 35))):
        wide_ref[start:stop] = rows_ref[start:stop].astype(F32)
        if start < 27:
            target = conv_ref.at[start:stop, here]
        else:
            target = down_ref.at[:, here]
        copies.append(pltpu.make_async_copy(wide_ref.at[start:stop], target, sems.at[k]))
        copies[-1].start()
    for copy in copies:
        copy.wait()


def write_call(rows, bases=(), own=True):
    return call(
        functools.partial(write_half, own=own), [VMEM] + [ANY] * len(bases),
        [sds((27, 128, 128), F32), sds((8, 128, 128), F32), TOKEN],
        [pltpu.VMEM((36, 64, 128), F32), pltpu.SemaphoreType.DMA((4,))], out=ANY,
        input_output_aliases={1: 0, 2: 1} if bases else {},
    )(rows, *bases)[:2]


def over_core(value):
    return lax.ppermute(value, "core", [(0, 1), (1, 0)])


def over_y(value, by):
    return lax.ppermute(value, "dp", [(i, (i + by) % 4) for i in range(4)])


def over_plane(value):
    return lax.all_to_all(value, ("z", "x"), 0, 0, tiled=True)


def stage(kernel, values, outs, after=(), scratch=()):
    return call(kernel, [VMEM] * len(values) + [ANY] * len(after), outs, scratch)(*values, *after)


def over_other(value):
    pairs = [(i, i + 1) for i in range(1, 31, 2)] + [(i + 1, i) for i in range(1, 31, 2)]
    return lax.ppermute(value, ("z", "x", "core"), pairs)


def local(features, conv_weight, down_weight, coarse_cotangent, brick_coords, neighbours, parents):
    coords, near, parent = brick_coords.reshape(3), neighbours.reshape(26), parents.reshape(1)
    core = lax.axis_index("core")
    cotangent = coarse_cotangent.reshape(16, 16, 16, 128)
    half = lax.dynamic_slice_in_dim(cotangent, 8 * (1 - core), 8)
    theirs = over_core(half)
    field = features.reshape(16, 8, 2, 16, 128)
    far = functools.partial(pltpu.with_memory_space_constraint, memory_space=pltpu.HBM)
    mine, down, *layers = prepare_call(far(cotangent), far(down_weight), far(field), half)
    grads, spread, to_partner, to_other = grad_call(far(coords), parent, mine, theirs, down, *layers)
    partner, other = over_core(to_partner), over_other(to_other)
    inner = inner_call(field, conv_weight)
    kept, sent, keep = main_call(
        coords, parent, near, field, partner, other, inner, down, grads, spread
    )

    got = over_core(sent)
    own = stage(add_halves, (kept, got), [sds((36, 64, 128), BF)])[0]
    gots = over_plane(own.reshape(16, 144, 128))
    partial_grad, token = input_call(near, grads, partner, other, far(conv_weight), own, 0)
    own = stage(add_sixteen, (gots,), [sds((144, 128), F32)], (token,))[0]
    gots = [over_y(own, k) for k in (1, 2, 3)]
    coarse, token = coarse_call(coords, keep, got, own)
    shares = stage(
        add_in_order, (own, *gots), [sds((16, 144, 128), BF)], (token,),
        scratch=[pltpu.VMEM((4, 144, 128), F32)],
    )[0]

    own = over_plane(shares).reshape(36, 64, 128)
    input_grad, token = input_call(near, grads, partner, other, far(conv_weight), shares, 1, partial_grad)
    own = after_call(own, token)
    got = over_core(own)
    halves = write_call(own)
    conv_grad, down_grad = write_call(got, halves, own=False)
    whole = (1, 1, 16, 16, 16, 128)
    return (
        coarse.reshape(whole),
        input_grad.reshape(whole),
        conv_grad.reshape(3, 3, 3, 128, 128),
        down_grad.reshape(2, 2, 2, 128, 128),
    )


def solution(mesh):
    sizes = (mesh.devices.shape[0], 4, 4, 2)
    mesh = jax.sharding.Mesh(mesh.devices.reshape(sizes), ("dp", "z", "x", "core"))
    region = ("z", "x", "core")
    bricks = P("dp", region, None, None, None, None)
    rows = P("dp", region, None)
    return jax.shard_map(
        local,
        mesh=mesh,
        in_specs=(bricks, P(), P(), bricks, rows, rows, P("dp", region)),
        out_specs=(bricks, bricks, P(), P()),
        check_vma=False,
    )
```

```python
import functools
import jax
import jax.numpy as jnp
from jax import lax
from jax.experimental import pallas as pl
from jax.experimental.pallas import tpu as pltpu
from jax.sharding import PartitionSpec as P

BF, F32 = jnp.bfloat16, jnp.float32
SMEM = pl.BlockSpec(memory_space=pltpu.SMEM)
VMEM = pl.BlockSpec(memory_space=pltpu.VMEM)
NN = (((1,), (0,)), ((), ()))
NT = (((1,), (1,)), ((), ()))
TN = (((0,), (0,)), ((), ()))


def dot(lhs, rhs, dims):
    return lax.dot_general(lhs, rhs, dims, preferred_element_type=F32)


def z_index(rows):
    return lax.broadcasted_iota(jnp.int32, (rows, 128), 0) % 16


def lay_interior(field_ref, shifts_ref, start=0, stop=16, base=1):
    z = z_index(256)

    for x in range(start, stop):
        plain = field_ref[x].reshape(256, 128)
        wide = plain.astype(F32)
        lower = jnp.where(z == 0, 0.0, pltpu.roll(wide, 1, 0)).astype(BF)
        upper = jnp.where(z == 15, 0.0, pltpu.roll(wide, 255, 0)).astype(BF)
        for c, value in enumerate((lower, plain, upper)):
            rows = value.reshape(8, 2, 16, 128)
            shifts_ref[c, x + base, 0:8, 1] = rows[:, 0]
            shifts_ref[c, x + base, 1:9, 0] = rows[:, 1]
            shifts_ref[c, x + base, 0, 0] = jnp.zeros((16, 128), BF)
            shifts_ref[c, x + base, 8, 1] = jnp.zeros((16, 128), BF)


def lay_slab(layer, flag, slab_ref):
    def three(value, b):
        rows = value.shape[0] * 16
        wide = value.astype(F32).reshape(rows, 128)
        z = z_index(rows)
        below, same, above = (flag(b, c) for c in (-1, 0, 1))
        lower = jnp.where(
            z == 0, pltpu.roll(wide, rows - 15, 0) * below, pltpu.roll(wide, 1, 0) * same
        )
        upper = jnp.where(
            z == 15, pltpu.roll(wide, 15, 0) * above, pltpu.roll(wide, rows - 1, 0) * same
        )
        return [v.astype(BF) for v in (lower, wide * same, upper)]

    for c, value in enumerate(three(layer, 0)):
        rows = value.reshape(8, 2, 16, 128)
        slab_ref[c, 0:8, 1] = rows[:, 0]
        slab_ref[c, 1:9, 0] = rows[:, 1]
    for c, value in enumerate(three(layer[15:16], -1)):
        slab_ref[c, 0, 0] = value.reshape(16, 128)
    for c, value in enumerate(three(layer[0:1], 1)):
        slab_ref[c, 8, 1] = value.reshape(16, 128)


def near_flag(near_ref, first):
    return lambda b, c: (near_ref[first + 3 * (b + 1) + c + 1] >= 0).astype(F32)


def window(shifts_ref, c, x, count):
    return jnp.concatenate(
        [
            shifts_ref[c, pl.ds(x, count), t // 2 : t // 2 + 8, t % 2].reshape(count * 128, 128)
            for t in range(4)
        ],
        axis=1,
    )


def prepare_kernel(
    cotangent_hbm, down_hbm, field_hbm, after_ref,
    mine_ref, down_ref, partner_ref, other_ref, sems,
):
    upper = lax.axis_index("core")
    copies = [
        pltpu.make_async_copy(field_hbm.at[15 - 15 * upper], partner_ref, sems.at[0]),
        pltpu.make_async_copy(field_hbm.at[15 * upper], other_ref, sems.at[1]),
    ]
    for k in range(4):
        copies.append(
            pltpu.make_async_copy(
                cotangent_hbm.at[pl.ds(8 * upper + 2 * k, 2)], mine_ref.at[2 * k : 2 * k + 2],
                sems.at[2 + k],
            )
        )
    for p in range(2):
        for q in range(2):
            for r in range(2):
                at = 2 * p + q
                rows, columns = slice(128 * at, 128 * at + 128), slice(128 * r, 128 * r + 128)
                copies.append(
                    pltpu.make_async_copy(
                        down_hbm.at[p, q, r], down_ref.at[rows, columns], sems.at[6 + 2 * at + r]
                    )
                )
    for copy in copies:
        copy.start()
    for copy in copies:
        copy.wait()


def grad_kernel(
    coords_ref, parent_ref, mine_ref, theirs_ref, down_ref, partner_ref, other_ref,
    grads_ref, spread_ref, to_partner_ref, to_other_ref, wide_ref,
):
    x, oy, oz = coords_ref[0], coords_ref[1] % 2, coords_ref[2] % 2
    is_own = parent_ref[0] == x
    down = down_ref[...]
    to_partner_ref[0] = partner_ref[...]
    to_other_ref[0] = other_ref[...]
    wide_ref[...] = jnp.zeros_like(wide_ref)
    for i in range(8):
        mine = mine_ref[i, pl.ds(8 * oy, 8)].astype(F32)
        theirs = theirs_ref[i, pl.ds(8 * oy, 8)].astype(F32)
        both = jnp.where(is_own, mine, theirs)
        part = jnp.where(oz == 0, both[:, 0:8], both[:, 8:16]).reshape(64, 128)
        wide_ref[i, pl.ds(0, 64, stride=2), :] = part
    for i in range(8):
        even = wide_ref[i]
        spread = jnp.concatenate([even, pltpu.roll(even, 1, 0)], axis=1).astype(BF)
        spread_ref[i] = spread
        grads = dot(spread, down, NT).astype(BF)
        for p in range(2):
            for q in range(2):
                at = (2 * p + q) * 128
                part = grads[:, at : at + 128].reshape(8, 16, 128)
                grads_ref[2 * i + p, :, q] = part
    upper = x % 2
    to_partner_ref[1] = grads_ref[15 - 15 * upper]
    to_other_ref[1] = grads_ref[15 * upper]


def lay_weights(conv_ref, weights_ref):
    zero = jnp.zeros((128, 128), BF)
    for a in range(3):
        for c in range(3):
            for t in range(4):
                for s in range(2):
                    weights_ref[a, c, t * 128 : t * 128 + 128, s * 128 : s * 128 + 128] = (
                        conv_ref[a, t - s, c] if 0 <= t - s <= 2 else zero
                    )


def inner_kernel(field_ref, conv_ref, shifts_ref, weights_ref, outputs_ref):
    lay_weights(conv_ref, weights_ref)
    lay_interior(field_ref, shifts_ref, 0, 11, 0)
    for first in (1, 5):
        acc = None
        for a in range(3):
            for c in range(3):
                part = dot(window(shifts_ref, c, first + a - 1, 4), weights_ref[a, c], NN)
                acc = part if acc is None else acc + part
        for s in range(2):
            field = field_ref[first : first + 4, :, s].astype(F32)
            outputs_ref[first - 1 : first + 3, :, s] = (
                acc[:, s * 128 : s * 128 + 128].reshape(4, 8, 16, 128) + field
            ).astype(BF)
        if first == 1:
            lay_interior(field_ref, shifts_ref, 11, 16, 0)


def taps(rows):
    return jnp.concatenate(
        [rows[t // 2 : t // 2 + 8, t % 2].reshape(128, 128) for t in range(4)], axis=1
    )


def main_kernel(
    coords_ref, parent_ref, near_ref, field_ref, partner_ref, other_ref, shifts_ref, weights_ref,
    inner_ref, down_ref, grads_ref, spread_ref,
    kept_rows_ref, sent_ref, keep_ref, low_shifts_ref, high_shifts_ref, edges_ref, sums_ref,
):
    x, oy, oz = coords_ref[0], coords_ref[1] % 2, coords_ref[2] % 2
    first_core = x % 2 == 0
    kept = (parent_ref[0] == x).astype(F32)

    def part_rows(tap, rows):
        kept_rows_ref[tap] = jnp.where(first_core, rows[0:64], rows[64:128])
        sent_ref[tap] = jnp.where(first_core, rows[64:128], rows[0:64]).astype(BF)

    kept_rows_ref[35] = jnp.zeros((64, 128), F32)
    sent_ref[35] = jnp.zeros((64, 128), BF)
    sent_ref[52] = jnp.full((64, 128), oy, jnp.int32).astype(F32).astype(BF)
    partner, other = partner_ref[0].astype(F32), other_ref[0].astype(F32)
    low = jnp.where(first_core, other, partner).reshape(16, 16, 128)
    high = jnp.where(first_core, partner, other).reshape(16, 16, 128)
    lay_slab(low, near_flag(near_ref, 0), low_shifts_ref)
    lay_slab(high, near_flag(near_ref, 17), high_shifts_ref)

    acc = None
    for a in range(3):
        for c in range(3):
            rows = [
                taps(low_shifts_ref[c] if a == 0 else shifts_ref[c, a - 1]),
                window(shifts_ref, c, 8 + a, 6 if a == 2 else 7),
            ]
            if a == 2:
                rows.append(taps(high_shifts_ref[c]))
            part = dot(jnp.concatenate(rows, axis=0), weights_ref[a, c], NN)
            acc = part if acc is None else acc + part
    for s in range(2):
        value = acc[:, s * 128 : s * 128 + 128].reshape(8, 8, 16, 128)
        edges_ref[0, :, s] = (value[0] + field_ref[0, :, s].astype(F32)).astype(BF)
        edges_ref[1:8, :, s] = (value[1:8] + field_ref[9:16, :, s].astype(F32)).astype(BF)

    down = down_ref[...]

    def corner(i, p, q):
        at = 2 * i + p
        rows = inner_ref[at - 1, :, q] if 1 <= at <= 8 else edges_ref[max(at - 8, 0), :, q]
        return rows.reshape(128, 128)

    for i in range(8):
        corners = jnp.concatenate([corner(i, p, q) for p in range(2) for q in range(2)], axis=1)
        sums = dot(corners, down, NN)
        sums_ref[i, 0] = sums[:, 0:128]
        sums_ref[i, 1] = sums[:, 128:256]
        block = sums_ref[i, 0, pl.ds(0, 64, stride=2), :] + sums_ref[i, 1, pl.ds(1, 64, stride=2), :]
        block = block.reshape(8, 8, 128)
        none = jnp.zeros_like(block)
        low = jnp.where(oz == 0, block, none)
        high = jnp.where(oz == 0, none, block)
        placed = jnp.concatenate([low, high], axis=1).reshape(128, 128)
        keep_ref[i] = (placed * kept).astype(BF).reshape(8, 16, 128)
        away = (placed * (1 - kept)).astype(BF)
        sent_ref[36 + 2 * i] = away[0:64]
        sent_ref[37 + 2 * i] = away[64:128]

    spread = spread_ref[...].reshape(1024, 256)
    for p in range(2):
        for q in range(2):
            rows = jnp.concatenate([corner(i, p, q) for i in range(8)], axis=0)
            result = dot(rows, spread, TN) * (1.0 / 1024)
            part_rows(27 + 4 * p + 2 * q, result[:, 0:128])
            part_rows(28 + 4 * p + 2 * q, result[:, 128:256])

    pair = jnp.concatenate([grads_ref[:, :, s].reshape(2048, 128) for s in range(2)], axis=1)
    for a in range(3):
        for c in range(3):
            if a == 0:
                rows = jnp.concatenate(
                    [taps(low_shifts_ref[c]), window(shifts_ref, c, 0, 15)], axis=0
                )
            elif a == 1:
                rows = window(shifts_ref, c, 0, 16)
            else:
                rows = jnp.concatenate(
                    [window(shifts_ref, c, 1, 15), taps(high_shifts_ref[c])], axis=0
                )
            result = dot(rows, pair, TN) * (1.0 / 1024)
            for b in range(3):
                part_rows(
                    9 * a + 3 * b + c,
                    result[b * 128 : b * 128 + 128, 0:128]
                    + result[b * 128 + 128 : b * 128 + 256, 128:256],
                )


def input_kernel(near_ref, field_ref, partner_ref, other_ref, conv_hbm, *refs, half, tile=4):
    result_ref, token_ref, shifts_ref, weights_ref, held_ref, conv_ref, sems = refs[-7:]
    token_ref[...] = jnp.zeros_like(token_ref)
    conv_copies = [
        pltpu.make_async_copy(conv_hbm.at[a], conv_ref.at[a], sems.at[2 + a]) for a in range(3)
    ]
    for copy in conv_copies:
        copy.start()
    lay = functools.partial(lay_interior, field_ref, shifts_ref, base=1 - 8 * half)
    if half == 0:
        lay(0, 5)
    else:
        lay(7, 13)
    layer = jnp.where(
        lax.axis_index("core") == half, other_ref[1].astype(F32), partner_ref[1].astype(F32)
    )
    def lay_edge():
        lay_slab(
            layer.reshape(16, 16, 128), near_flag(near_ref, 17 * half), shifts_ref.at[:, 9 * half]
        )

    if half == 0:
        lay_edge()
    zero = jnp.zeros((128, 128), BF)
    for a in (2, 1, 0):
        conv_copies[2 - a].wait()
        for c in range(3):
            for t in range(4):
                for s in range(2):
                    weights_ref[a, c, s * 128 : s * 128 + 128, t * 128 : t * 128 + 128] = (
                        conv_ref[2 - a, 2 - t + s, 2 - c] if 0 <= t - s <= 2 else zero
                    )
    copies = []
    for step in range(8 // tile):
        first = step * tile
        if step == 1 and half == 0:
            lay(5, 9)
        if step == 1 and half == 1:
            lay(13, 16)
            lay_edge()
        acc = None
        for a in range(3):
            for c in range(3):
                part = dot(window(shifts_ref, c, first + a, tile), weights_ref[a, c], NT)
                acc = part if acc is None else acc + part
        here = 8 * half + first
        for s in range(2):
            field = field_ref[here : here + tile, :, s].astype(F32)
            held_ref[first : first + tile, :, s] = (
                acc[:, s * 128 : s * 128 + 128].reshape(tile, 8, 16, 128) + field
            ).astype(BF)
        copy = pltpu.make_async_copy(
            held_ref.at[pl.ds(first, tile)], result_ref.at[pl.ds(here, tile)], sems.at[step]
        )
        copy.start()
        copies.append(copy)
    for copy in copies:
        copy.wait()


def coarse_kernel(coords_ref, keep_ref, got_ref, coarse_ref, token_ref, held_ref, sems):
    token_ref[...] = jnp.zeros_like(token_ref)
    upper, oy = coords_ref[0] % 2, coords_ref[1] % 2
    there = got_ref[52, 0:16].astype(F32)
    none = jnp.zeros((8, 16, 128), BF)
    for i in range(8):
        rows = jnp.concatenate([got_ref[36 + 2 * i], got_ref[37 + 2 * i]], axis=0)
        rows = rows.reshape(8, 16, 128).astype(F32)
        held_ref[0, i, pl.ds(8 * oy, 8)] = keep_ref[i]
        held_ref[0, i, pl.ds(8 - 8 * oy, 8)] = none
        held_ref[1, i, 0:8] = jnp.where(there == 0, rows, 0.0).astype(BF)
        held_ref[1, i, 8:16] = jnp.where(there == 1, rows, 0.0).astype(BF)
    keep = pltpu.make_async_copy(held_ref.at[0], coarse_ref.at[pl.ds(8 * upper, 8)], sems.at[0])
    got = pltpu.make_async_copy(held_ref.at[1], coarse_ref.at[pl.ds(8 - 8 * upper, 8)], sems.at[1])
    keep.start()
    got.start()
    keep.wait()
    got.wait()


ANY = pl.BlockSpec(memory_space=pl.ANY)
HBM = pl.BlockSpec(memory_space=pltpu.HBM)
TOKEN = jax.ShapeDtypeStruct((8, 128), F32)
sds = jax.ShapeDtypeStruct


def call(kernel, ins, outs, scratch=(), flops=0, moved=1 << 20, limit=8, out=VMEM, **kw):
    return pl.pallas_call(
        kernel,
        in_specs=ins,
        out_specs=[VMEM if shape is TOKEN else out for shape in outs],
        out_shape=outs,
        scratch_shapes=list(scratch),
        cost_estimate=pl.CostEstimate(flops=flops, bytes_accessed=moved, transcendentals=0),
        compiler_params=pltpu.CompilerParams(vmem_limit_bytes=limit << 20),
        **kw,
    )


def prepare_call(cotangent, down, field, after):
    layer = sds((8, 2, 16, 128), BF)
    return call(
        prepare_kernel, [HBM] * 3 + [ANY],
        [sds((8, 16, 16, 128), BF), sds((512, 256), BF), layer, layer],
        [pltpu.SemaphoreType.DMA((14,))], moved=1 << 20,
    )(cotangent, down, field, after)


def grad_call(coords, parent, mine, theirs, down, partner, other):
    layers = sds((2, 8, 2, 16, 128), BF)
    return call(
        grad_kernel, [SMEM] * 2 + [VMEM] * 5,
        [sds((16, 8, 2, 16, 128), BF), sds((8, 128, 256), BF), layers, layers],
        [pltpu.VMEM((8, 128, 128), F32)], flops=2 * 2**27, moved=4 << 20,
    )(coords, parent, mine, theirs, down, partner, other)


def inner_call(field, conv):
    return call(
        inner_kernel, [VMEM] * 2,
        [sds((3, 16, 9, 2, 16, 128), BF), sds((3, 3, 512, 256), BF), sds((8, 8, 2, 16, 128), BF)],
        flops=9 * 2048 * 512 * 256, moved=2 << 20, limit=16,
    )(field, conv)


def main_call(coords, parent, near, field, partner, other, inner, down, grads, spread):
    slab = pltpu.VMEM((3, 9, 2, 16, 128), BF)
    return call(
        main_kernel, [SMEM] * 3 + [VMEM] * 9,
        [sds((36, 64, 128), F32), sds((53, 64, 128), BF), sds((8, 8, 16, 128), BF)],
        [slab, slab, pltpu.VMEM((8, 8, 2, 16, 128), BF), pltpu.VMEM((8, 2, 128, 128), F32)],
        flops=3 * 9 * 2048 * 512 * 256, limit=24,
    )(coords, parent, near, field, partner, other, *inner, down, grads, spread)


def input_call(near, field, partner, other, conv, after, half, base=None):
    ins, values = [SMEM] + [VMEM] * 3 + [HBM, ANY], [near, field, partner, other, conv, after]
    aliases = {}
    if base is not None:
        ins, values, aliases = ins + [ANY], values + [base], {6: 0}
    return call(
        functools.partial(input_kernel, half=half), ins, [sds((16, 8, 2, 16, 128), BF), TOKEN],
        [pltpu.VMEM((3, 10, 9, 2, 16, 128), BF), pltpu.VMEM((3, 3, 256, 512), BF),
         pltpu.VMEM((8, 8, 2, 16, 128), BF), pltpu.VMEM((3, 3, 3, 128, 128), BF),
         pltpu.SemaphoreType.DMA((5,))],
        flops=9 * 2048 * 512 * 256, limit=24, out=ANY, input_output_aliases=aliases,
    )(*values)


def coarse_call(coords, keep, got, after):
    def kernel(coords_ref, keep_ref, got_ref, after_ref, *refs):
        coarse_kernel(coords_ref, keep_ref, got_ref, *refs)

    return call(
        kernel, [SMEM] + [VMEM] * 2 + [ANY], [sds((16, 16, 16, 128), BF), TOKEN],
        [pltpu.VMEM((2, 8, 16, 16, 128), BF), pltpu.SemaphoreType.DMA((2,))], out=ANY,
    )(coords, keep, got, after)


def add_halves(kept_ref, got_ref, total_ref):
    total_ref[...] = (kept_ref[...] + got_ref[0:36].astype(F32)).astype(BF)


def add_sixteen(got_ref, *refs):
    total = got_ref[0].astype(F32)
    for k in range(1, 16):
        total = total + got_ref[k].astype(F32)
    refs[-1][...] = total


def add_in_order(own_ref, *refs):
    y = lax.axis_index("dp")
    total_ref, slots_ref = refs[-2:]
    for k, ref in enumerate((own_ref, *refs[:3])):
        slots_ref[(y - k + 4) % 4] = ref[...]
    total = ((slots_ref[0] + slots_ref[1]) + (slots_ref[2] + slots_ref[3])).astype(BF)
    for k in range(16):
        total_ref[k] = total


def after_call(value, token):
    def kernel(value_ref, token_ref, same_ref):
        pass

    return call(
        kernel, [ANY] * 2, [sds(value.shape, value.dtype)], out=ANY, input_output_aliases={0: 0},
        moved=1024,
    )(value, token)[0]


def write_half(rows_ref, *refs, own):
    conv_ref, down_ref, token_ref, wide_ref, sems = refs[-5:]
    token_ref[...] = jnp.zeros_like(token_ref)
    core = lax.axis_index("core")
    here = pl.ds(pl.multiple_of(64 * (core if own else 1 - core), 64), 64)
    copies = []
    for k, start in enumerate((*range(0, 27, 3), 27, 31)):
        stop = start + (3 if start < 27 else 4)
        wide_ref[start:stop] = rows_ref[start:stop].astype(F32)
        if start < 27:
            target = conv_ref.at[start:stop, here]
        else:
            target = down_ref.at[start - 27 : stop - 27, here]
        copies.append(pltpu.make_async_copy(wide_ref.at[start:stop], target, sems.at[k]))
        copies[-1].start()
    for copy in copies:
        copy.wait()


def write_call(rows, bases=(), own=True):
    return call(
        functools.partial(write_half, own=own), [VMEM] + [ANY] * len(bases),
        [sds((27, 128, 128), F32), sds((8, 128, 128), F32), TOKEN],
        [pltpu.VMEM((36, 64, 128), F32), pltpu.SemaphoreType.DMA((11,))], out=ANY,
        input_output_aliases={1: 0, 2: 1} if bases else {},
    )(rows, *bases)[:2]


def over_core(value):
    return lax.ppermute(value, "core", [(0, 1), (1, 0)])


def over_y(value, by):
    return lax.ppermute(value, "dp", [(i, (i + by) % 4) for i in range(4)])


def over_plane(value):
    return lax.all_to_all(value, ("z", "x"), 0, 0, tiled=True)


def stage(kernel, values, outs, after=(), scratch=()):
    return call(kernel, [VMEM] * len(values) + [ANY] * len(after), outs, scratch)(*values, *after)


def over_other(value):
    pairs = [(i, i + 1) for i in range(1, 31, 2)] + [(i + 1, i) for i in range(1, 31, 2)]
    return lax.ppermute(value, ("z", "x", "core"), pairs)


def local(features, conv_weight, down_weight, coarse_cotangent, brick_coords, neighbours, parents):
    coords, near, parent = brick_coords.reshape(3), neighbours.reshape(26), parents.reshape(1)
    core = lax.axis_index("core")
    cotangent = coarse_cotangent.reshape(16, 16, 16, 128)
    half = lax.dynamic_slice_in_dim(cotangent, 8 * (1 - core), 8)
    theirs = over_core(half)
    field = features.reshape(16, 8, 2, 16, 128)
    far = functools.partial(pltpu.with_memory_space_constraint, memory_space=pltpu.HBM)
    mine, down, *layers = prepare_call(far(cotangent), far(down_weight), far(field), half)
    grads, spread, to_partner, to_other = grad_call(far(coords), parent, mine, theirs, down, *layers)
    partner, other = over_core(to_partner), over_other(to_other)
    inner = inner_call(field, conv_weight)
    kept, sent, keep = main_call(
        coords, parent, near, field, partner, other, inner, down, grads, spread
    )

    got = over_core(sent)
    own = stage(add_halves, (kept, got), [sds((36, 64, 128), BF)])[0]
    gots = over_plane(own.reshape(16, 144, 128))
    partial_grad, token = input_call(near, grads, partner, other, far(conv_weight), own, 0)
    coarse, token = coarse_call(coords, keep, got, token)
    own = stage(add_sixteen, (gots,), [sds((144, 128), F32)], (token,))[0]
    gots = [over_y(own, k) for k in (1, 2, 3)]
    shares = stage(
        add_in_order, (own, *gots), [sds((16, 144, 128), BF)],
        scratch=[pltpu.VMEM((4, 144, 128), F32)],
    )[0]

    own = over_plane(shares).reshape(36, 64, 128)
    input_grad, token = input_call(near, grads, partner, other, far(conv_weight), shares, 1, partial_grad)
    own = after_call(own, token)
    got = over_core(own)
    halves = write_call(own)
    conv_grad, down_grad = write_call(got, halves, own=False)
    whole = (1, 1, 16, 16, 16, 128)
    return (
        coarse.reshape(whole),
        input_grad.reshape(whole),
        conv_grad.reshape(3, 3, 3, 128, 128),
        down_grad.reshape(2, 2, 2, 128, 128),
    )


def solution(mesh):
    sizes = (mesh.devices.shape[0], 4, 4, 2)
    mesh = jax.sharding.Mesh(mesh.devices.reshape(sizes), ("dp", "z", "x", "core"))
    region = ("z", "x", "core")
    bricks = P("dp", region, None, None, None, None)
    rows = P("dp", region, None)
    return jax.shard_map(
        local,
        mesh=mesh,
        in_specs=(bricks, P(), P(), bricks, rows, rows, P("dp", region)),
        out_specs=(bricks, bricks, P(), P()),
        check_vma=False,
    )
```

```python
import functools
import jax
import jax.numpy as jnp
from jax import lax
from jax.experimental import pallas as pl
from jax.experimental.pallas import tpu as pltpu
from jax.sharding import PartitionSpec as P

BF, F32 = jnp.bfloat16, jnp.float32
SMEM = pl.BlockSpec(memory_space=pltpu.SMEM)
VMEM = pl.BlockSpec(memory_space=pltpu.VMEM)
NN = (((1,), (0,)), ((), ()))
NT = (((1,), (1,)), ((), ()))
TN = (((0,), (0,)), ((), ()))


def dot(lhs, rhs, dims):
    return lax.dot_general(lhs, rhs, dims, preferred_element_type=F32)


def z_index(rows):
    return lax.broadcasted_iota(jnp.int32, (rows, 128), 0) % 16


def lay_interior(field_ref, shifts_ref, start=0, stop=16, base=1):
    z = z_index(256)

    for x in range(start, stop):
        plain = field_ref[x].reshape(256, 128)
        wide = plain.astype(F32)
        lower = jnp.where(z == 0, 0.0, pltpu.roll(wide, 1, 0)).astype(BF)
        upper = jnp.where(z == 15, 0.0, pltpu.roll(wide, 255, 0)).astype(BF)
        for c, value in enumerate((lower, plain, upper)):
            rows = value.reshape(8, 2, 16, 128)
            shifts_ref[c, x + base, 0:8, 1] = rows[:, 0]
            shifts_ref[c, x + base, 1:9, 0] = rows[:, 1]
            shifts_ref[c, x + base, 0, 0] = jnp.zeros((16, 128), BF)
            shifts_ref[c, x + base, 8, 1] = jnp.zeros((16, 128), BF)


def lay_slab(layer, flag, slab_ref):
    def three(value, b):
        rows = value.shape[0] * 16
        wide = value.astype(F32).reshape(rows, 128)
        z = z_index(rows)
        below, same, above = (flag(b, c) for c in (-1, 0, 1))
        lower = jnp.where(
            z == 0, pltpu.roll(wide, rows - 15, 0) * below, pltpu.roll(wide, 1, 0) * same
        )
        upper = jnp.where(
            z == 15, pltpu.roll(wide, 15, 0) * above, pltpu.roll(wide, rows - 1, 0) * same
        )
        return [v.astype(BF) for v in (lower, wide * same, upper)]

    for c, value in enumerate(three(layer, 0)):
        rows = value.reshape(8, 2, 16, 128)
        slab_ref[c, 0:8, 1] = rows[:, 0]
        slab_ref[c, 1:9, 0] = rows[:, 1]
    for c, value in enumerate(three(layer[15:16], -1)):
        slab_ref[c, 0, 0] = value.reshape(16, 128)
    for c, value in enumerate(three(layer[0:1], 1)):
        slab_ref[c, 8, 1] = value.reshape(16, 128)


def near_flag(near_ref, first):
    return lambda b, c: (near_ref[first + 3 * (b + 1) + c + 1] >= 0).astype(F32)


def window(shifts_ref, c, x, count):
    return jnp.concatenate(
        [
            shifts_ref[c, pl.ds(x, count), t // 2 : t // 2 + 8, t % 2].reshape(count * 128, 128)
            for t in range(4)
        ],
        axis=1,
    )


def prepare_kernel(
    cotangent_hbm, down_hbm, field_hbm, after_ref,
    mine_ref, down_ref, partner_ref, other_ref, sems,
):
    upper = lax.axis_index("core")
    copies = [
        pltpu.make_async_copy(field_hbm.at[15 - 15 * upper], partner_ref, sems.at[0]),
        pltpu.make_async_copy(field_hbm.at[15 * upper], other_ref, sems.at[1]),
    ]
    for k in range(4):
        copies.append(
            pltpu.make_async_copy(
                cotangent_hbm.at[pl.ds(8 * upper + 2 * k, 2)], mine_ref.at[2 * k : 2 * k + 2],
                sems.at[2 + k],
            )
        )
    for p in range(2):
        for q in range(2):
            for r in range(2):
                at = 2 * p + q
                rows, columns = slice(128 * at, 128 * at + 128), slice(128 * r, 128 * r + 128)
                copies.append(
                    pltpu.make_async_copy(
                        down_hbm.at[p, q, r], down_ref.at[rows, columns], sems.at[6 + 2 * at + r]
                    )
                )
    for copy in copies:
        copy.start()
    for copy in copies:
        copy.wait()


def grad_kernel(
    coords_ref, parent_ref, mine_ref, theirs_ref, down_ref, partner_ref, other_ref,
    grads_ref, spread_ref, to_partner_ref, to_other_ref, wide_ref,
):
    x, oy, oz = coords_ref[0], coords_ref[1] % 2, coords_ref[2] % 2
    is_own = parent_ref[0] == x
    down = down_ref[...]
    to_partner_ref[0] = partner_ref[...]
    to_other_ref[0] = other_ref[...]
    wide_ref[...] = jnp.zeros_like(wide_ref)
    for i in range(8):
        mine = mine_ref[i, pl.ds(8 * oy, 8)].astype(F32)
        theirs = theirs_ref[i, pl.ds(8 * oy, 8)].astype(F32)
        both = jnp.where(is_own, mine, theirs)
        part = jnp.where(oz == 0, both[:, 0:8], both[:, 8:16]).reshape(64, 128)
        wide_ref[i, pl.ds(0, 64, stride=2), :] = part
    for i in range(8):
        even = wide_ref[i]
        spread = jnp.concatenate([even, pltpu.roll(even, 1, 0)], axis=1).astype(BF)
        spread_ref[i] = spread
        grads = dot(spread, down, NT).astype(BF)
        for p in range(2):
            for q in range(2):
                at = (2 * p + q) * 128
                part = grads[:, at : at + 128].reshape(8, 16, 128)
                grads_ref[2 * i + p, :, q] = part
    upper = x % 2
    to_partner_ref[1] = grads_ref[15 - 15 * upper]
    to_other_ref[1] = grads_ref[15 * upper]


def lay_weights(conv_ref, weights_ref):
    zero = jnp.zeros((128, 128), BF)
    for a in range(3):
        for c in range(3):
            for t in range(4):
                for s in range(2):
                    weights_ref[a, c, t * 128 : t * 128 + 128, s * 128 : s * 128 + 128] = (
                        conv_ref[a, t - s, c] if 0 <= t - s <= 2 else zero
                    )


def inner_kernel(field_ref, conv_ref, shifts_ref, weights_ref, outputs_ref):
    lay_weights(conv_ref, weights_ref)
    lay_interior(field_ref, shifts_ref, 0, 6, 0)
    for first, count in ((1, 4), (5, 4), (9, 4), (13, 2)):
        lay_interior(field_ref, shifts_ref, min(first + 5, 16), min(first + 9, 16), 0)
        acc = None
        for a in range(3):
            for c in range(3):
                part = dot(window(shifts_ref, c, first + a - 1, count), weights_ref[a, c], NN)
                acc = part if acc is None else acc + part
        for s in range(2):
            field = field_ref[first : first + count, :, s].astype(F32)
            outputs_ref[first : first + count, :, s] = (
                acc[:, s * 128 : s * 128 + 128].reshape(count, 8, 16, 128) + field
            ).astype(BF)


def taps(rows):
    return jnp.concatenate(
        [rows[t // 2 : t // 2 + 8, t % 2].reshape(128, 128) for t in range(4)], axis=1
    )


def main_kernel(
    coords_ref, parent_ref, near_ref, field_ref, partner_ref, other_ref, shifts_ref, weights_ref,
    inner_ref, down_ref, grads_ref, spread_ref,
    kept_rows_ref, sent_ref, keep_ref, low_shifts_ref, high_shifts_ref, edges_ref, sums_ref,
):
    x, oy, oz = coords_ref[0], coords_ref[1] % 2, coords_ref[2] % 2
    first_core = x % 2 == 0
    kept = (parent_ref[0] == x).astype(F32)

    def part_rows(tap, rows):
        kept_rows_ref[tap] = jnp.where(first_core, rows[0:64], rows[64:128])
        sent_ref[tap] = jnp.where(first_core, rows[64:128], rows[0:64]).astype(BF)

    kept_rows_ref[35] = jnp.zeros((64, 128), F32)
    sent_ref[35] = jnp.zeros((64, 128), BF)
    sent_ref[52] = jnp.full((64, 128), oy, jnp.int32).astype(F32).astype(BF)
    partner, other = partner_ref[0].astype(F32), other_ref[0].astype(F32)
    low = jnp.where(first_core, other, partner).reshape(16, 16, 128)
    high = jnp.where(first_core, partner, other).reshape(16, 16, 128)
    lay_slab(low, near_flag(near_ref, 0), low_shifts_ref)
    lay_slab(high, near_flag(near_ref, 17), high_shifts_ref)

    accs = [None, None]
    for a in range(3):
        for c in range(3):
            for k, rows in enumerate((
                low_shifts_ref[c] if a == 0 else shifts_ref[c, a - 1],
                high_shifts_ref[c] if a == 2 else shifts_ref[c, 14 + a],
            )):
                part = dot(taps(rows), weights_ref[a, c], NN)
                accs[k] = part if accs[k] is None else accs[k] + part
    for s in range(2):
        for k in range(2):
            value = accs[k][:, s * 128 : s * 128 + 128].reshape(8, 16, 128)
            edges_ref[k, :, s] = (value + field_ref[15 * k, :, s].astype(F32)).astype(BF)

    down = down_ref[...]

    def corner(i, p, q):
        at = 2 * i + p
        rows = edges_ref[at // 15, :, q] if at in (0, 15) else inner_ref[at, :, q]
        return rows.reshape(128, 128)

    for i in range(8):
        corners = jnp.concatenate([corner(i, p, q) for p in range(2) for q in range(2)], axis=1)
        sums = dot(corners, down, NN)
        sums_ref[i, 0] = sums[:, 0:128]
        sums_ref[i, 1] = sums[:, 128:256]
        block = sums_ref[i, 0, pl.ds(0, 64, stride=2), :] + sums_ref[i, 1, pl.ds(1, 64, stride=2), :]
        block = block.reshape(8, 8, 128)
        none = jnp.zeros_like(block)
        low = jnp.where(oz == 0, block, none)
        high = jnp.where(oz == 0, none, block)
        placed = jnp.concatenate([low, high], axis=1).reshape(128, 128)
        keep_ref[i] = (placed * kept).astype(BF).reshape(8, 16, 128)
        away = (placed * (1 - kept)).astype(BF)
        sent_ref[36 + 2 * i] = away[0:64]
        sent_ref[37 + 2 * i] = away[64:128]

    spread = spread_ref[...].reshape(1024, 256)
    for p in range(2):
        for q in range(2):
            rows = jnp.concatenate([corner(i, p, q) for i in range(8)], axis=0)
            result = dot(rows, spread, TN) * (1.0 / 1024)
            part_rows(27 + 4 * p + 2 * q, result[:, 0:128])
            part_rows(28 + 4 * p + 2 * q, result[:, 128:256])

    pair = jnp.concatenate([grads_ref[:, :, s].reshape(2048, 128) for s in range(2)], axis=1)
    for a in range(3):
        for c in range(3):
            if a == 0:
                rows = jnp.concatenate(
                    [taps(low_shifts_ref[c]), window(shifts_ref, c, 0, 15)], axis=0
                )
            elif a == 1:
                rows = window(shifts_ref, c, 0, 16)
            else:
                rows = jnp.concatenate(
                    [window(shifts_ref, c, 1, 15), taps(high_shifts_ref[c])], axis=0
                )
            result = dot(rows, pair, TN) * (1.0 / 1024)
            for b in range(3):
                part_rows(
                    9 * a + 3 * b + c,
                    result[b * 128 : b * 128 + 128, 0:128]
                    + result[b * 128 + 128 : b * 128 + 256, 128:256],
                )


def input_kernel(near_ref, field_ref, partner_ref, other_ref, conv_hbm, *refs, half, tile=4):
    result_ref, token_ref, shifts_ref, weights_ref, held_ref, conv_ref, sems = refs[-7:]
    token_ref[...] = jnp.zeros_like(token_ref)
    conv_copies = [
        pltpu.make_async_copy(conv_hbm.at[a], conv_ref.at[a], sems.at[2 + a]) for a in range(3)
    ]
    for copy in conv_copies:
        copy.start()
    lay = functools.partial(lay_interior, field_ref, shifts_ref, base=1 - 8 * half)
    if half == 0:
        lay(0, 5)
    else:
        lay(7, 13)
    layer = jnp.where(
        lax.axis_index("core") == half, other_ref[1].astype(F32), partner_ref[1].astype(F32)
    )
    def lay_edge():
        lay_slab(
            layer.reshape(16, 16, 128), near_flag(near_ref, 17 * half), shifts_ref.at[:, 9 * half]
        )

    if half == 0:
        lay_edge()
    zero = jnp.zeros((128, 128), BF)
    for a in (2, 1, 0):
        conv_copies[2 - a].wait()
        for c in range(3):
            for t in range(4):
                for s in range(2):
                    weights_ref[a, c, s * 128 : s * 128 + 128, t * 128 : t * 128 + 128] = (
                        conv_ref[2 - a, 2 - t + s, 2 - c] if 0 <= t - s <= 2 else zero
                    )
    copies = []
    for step in range(8 // tile):
        first = step * tile
        if step == 1 and half == 0:
            lay(5, 9)
        if step == 1 and half == 1:
            lay(13, 16)
            lay_edge()
        acc = None
        for a in range(3):
            for c in range(3):
                part = dot(window(shifts_ref, c, first + a, tile), weights_ref[a, c], NT)
                acc = part if acc is None else acc + part
        here = 8 * half + first
        for s in range(2):
            field = field_ref[here : here + tile, :, s].astype(F32)
            held_ref[first : first + tile, :, s] = (
                acc[:, s * 128 : s * 128 + 128].reshape(tile, 8, 16, 128) + field
            ).astype(BF)
        copy = pltpu.make_async_copy(
            held_ref.at[pl.ds(first, tile)], result_ref.at[pl.ds(here, tile)], sems.at[step]
        )
        copy.start()
        copies.append(copy)
    for copy in copies:
        copy.wait()


def coarse_kernel(coords_ref, keep_ref, got_ref, coarse_ref, token_ref, held_ref, sems):
    token_ref[...] = jnp.zeros_like(token_ref)
    upper, oy = coords_ref[0] % 2, coords_ref[1] % 2
    there = got_ref[52, 0:16].astype(F32)
    none = jnp.zeros((8, 16, 128), BF)
    for i in range(8):
        rows = jnp.concatenate([got_ref[36 + 2 * i], got_ref[37 + 2 * i]], axis=0)
        rows = rows.reshape(8, 16, 128).astype(F32)
        held_ref[0, i, pl.ds(8 * oy, 8)] = keep_ref[i]
        held_ref[0, i, pl.ds(8 - 8 * oy, 8)] = none
        held_ref[1, i, 0:8] = jnp.where(there == 0, rows, 0.0).astype(BF)
        held_ref[1, i, 8:16] = jnp.where(there == 1, rows, 0.0).astype(BF)
    keep = pltpu.make_async_copy(held_ref.at[0], coarse_ref.at[pl.ds(8 * upper, 8)], sems.at[0])
    got = pltpu.make_async_copy(held_ref.at[1], coarse_ref.at[pl.ds(8 - 8 * upper, 8)], sems.at[1])
    keep.start()
    got.start()
    keep.wait()
    got.wait()


ANY = pl.BlockSpec(memory_space=pl.ANY)
HBM = pl.BlockSpec(memory_space=pltpu.HBM)
TOKEN = jax.ShapeDtypeStruct((8, 128), F32)
sds = jax.ShapeDtypeStruct


def call(kernel, ins, outs, scratch=(), flops=0, moved=1 << 20, limit=8, out=VMEM, **kw):
    return pl.pallas_call(
        kernel,
        in_specs=ins,
        out_specs=[VMEM if shape is TOKEN else out for shape in outs],
        out_shape=outs,
        scratch_shapes=list(scratch),
        cost_estimate=pl.CostEstimate(flops=flops, bytes_accessed=moved, transcendentals=0),
        compiler_params=pltpu.CompilerParams(vmem_limit_bytes=limit << 20),
        **kw,
    )


def prepare_call(cotangent, down, field, after):
    layer = sds((8, 2, 16, 128), BF)
    return call(
        prepare_kernel, [HBM] * 3 + [ANY],
        [sds((8, 16, 16, 128), BF), sds((512, 256), BF), layer, layer],
        [pltpu.SemaphoreType.DMA((14,))], moved=1 << 20,
    )(cotangent, down, field, after)


def grad_call(coords, parent, mine, theirs, down, partner, other):
    layers = sds((2, 8, 2, 16, 128), BF)
    return call(
        grad_kernel, [SMEM] * 2 + [VMEM] * 5,
        [sds((16, 8, 2, 16, 128), BF), sds((8, 128, 256), BF), layers, layers],
        [pltpu.VMEM((8, 128, 128), F32)], flops=2 * 2**27, moved=4 << 20,
    )(coords, parent, mine, theirs, down, partner, other)


def inner_call(field, conv):
    return call(
        inner_kernel, [VMEM] * 2,
        [sds((3, 16, 9, 2, 16, 128), BF), sds((3, 3, 512, 256), BF), sds((16, 8, 2, 16, 128), BF)],
        flops=2 * 9 * 2048 * 512 * 256, moved=2 << 20, limit=16,
    )(field, conv)


def main_call(coords, parent, near, field, partner, other, inner, down, grads, spread):
    slab = pltpu.VMEM((3, 9, 2, 16, 128), BF)
    return call(
        main_kernel, [SMEM] * 3 + [VMEM] * 9,
        [sds((36, 64, 128), F32), sds((53, 64, 128), BF), sds((8, 8, 16, 128), BF)],
        [slab, slab, pltpu.VMEM((2, 8, 2, 16, 128), BF), pltpu.VMEM((8, 2, 128, 128), F32)],
        flops=2 * 9 * 2048 * 512 * 256, limit=24,
    )(coords, parent, near, field, partner, other, *inner, down, grads, spread)


def input_call(near, field, partner, other, conv, after, half, base=None):
    ins, values = [SMEM] + [VMEM] * 3 + [HBM, ANY], [near, field, partner, other, conv, after]
    aliases = {}
    if base is not None:
        ins, values, aliases = ins + [ANY], values + [base], {6: 0}
    return call(
        functools.partial(input_kernel, half=half), ins, [sds((16, 8, 2, 16, 128), BF), TOKEN],
        [pltpu.VMEM((3, 10, 9, 2, 16, 128), BF), pltpu.VMEM((3, 3, 256, 512), BF),
         pltpu.VMEM((8, 8, 2, 16, 128), BF), pltpu.VMEM((3, 3, 3, 128, 128), BF),
         pltpu.SemaphoreType.DMA((5,))],
        flops=9 * 2048 * 512 * 256, limit=24, out=ANY, input_output_aliases=aliases,
    )(*values)


def coarse_call(coords, keep, got, after):
    def kernel(coords_ref, keep_ref, got_ref, after_ref, *refs):
        coarse_kernel(coords_ref, keep_ref, got_ref, *refs)

    return call(
        kernel, [SMEM] + [VMEM] * 2 + [ANY], [sds((16, 16, 16, 128), BF), TOKEN],
        [pltpu.VMEM((2, 8, 16, 16, 128), BF), pltpu.SemaphoreType.DMA((2,))], out=ANY,
    )(coords, keep, got, after)


def add_halves(kept_ref, got_ref, total_ref):
    total_ref[...] = (kept_ref[...] + got_ref[0:36].astype(F32)).astype(BF)


def add_sixteen(got_ref, *refs):
    total = got_ref[0].astype(F32)
    for k in range(1, 16):
        total = total + got_ref[k].astype(F32)
    refs[-1][...] = total


def add_in_order(own_ref, *refs):
    y = lax.axis_index("dp")
    total_ref, slots_ref = refs[-2:]
    for k, ref in enumerate((own_ref, *refs[:3])):
        slots_ref[(y - k + 4) % 4] = ref[...]
    total = ((slots_ref[0] + slots_ref[1]) + (slots_ref[2] + slots_ref[3])).astype(BF)
    for k in range(16):
        total_ref[k] = total


def after_call(value, token):
    def kernel(value_ref, token_ref, same_ref):
        pass

    return call(
        kernel, [ANY] * 2, [sds(value.shape, value.dtype)], out=ANY, input_output_aliases={0: 0},
        moved=1024,
    )(value, token)[0]


def write_half(rows_ref, *refs, own):
    conv_ref, down_ref, token_ref, wide_ref, sems = refs[-5:]
    token_ref[...] = jnp.zeros_like(token_ref)
    core = lax.axis_index("core")
    here = pl.ds(pl.multiple_of(64 * (core if own else 1 - core), 64), 64)
    copies = []
    for k, (start, stop) in enumerate(((0, 9), (9, 18), (18, 27), (27, 35))):
        wide_ref[start:stop] = rows_ref[start:stop].astype(F32)
        if start < 27:
            target = conv_ref.at[start:stop, here]
        else:
            target = down_ref.at[:, here]
        copies.append(pltpu.make_async_copy(wide_ref.at[start:stop], target, sems.at[k]))
        copies[-1].start()
    for copy in copies:
        copy.wait()


def write_call(rows, bases=(), own=True):
    return call(
        functools.partial(write_half, own=own), [VMEM] + [ANY] * len(bases),
        [sds((27, 128, 128), F32), sds((8, 128, 128), F32), TOKEN],
        [pltpu.VMEM((36, 64, 128), F32), pltpu.SemaphoreType.DMA((4,))], out=ANY,
        input_output_aliases={1: 0, 2: 1} if bases else {},
    )(rows, *bases)[:2]


def over_core(value):
    return lax.ppermute(value, "core", [(0, 1), (1, 0)])


def over_y(value, by):
    return lax.ppermute(value, "dp", [(i, (i + by) % 4) for i in range(4)])


def over_plane(value):
    return lax.all_to_all(value, ("z", "x"), 0, 0, tiled=True)


def stage(kernel, values, outs, after=(), scratch=()):
    return call(kernel, [VMEM] * len(values) + [ANY] * len(after), outs, scratch)(*values, *after)


def over_other(value):
    pairs = [(i, i + 1) for i in range(1, 31, 2)] + [(i + 1, i) for i in range(1, 31, 2)]
    return lax.ppermute(value, ("z", "x", "core"), pairs)


def local(features, conv_weight, down_weight, coarse_cotangent, brick_coords, neighbours, parents):
    coords, near, parent = brick_coords.reshape(3), neighbours.reshape(26), parents.reshape(1)
    core = lax.axis_index("core")
    cotangent = coarse_cotangent.reshape(16, 16, 16, 128)
    half = lax.dynamic_slice_in_dim(cotangent, 8 * (1 - core), 8)
    theirs = over_core(half)
    field = features.reshape(16, 8, 2, 16, 128)
    far = functools.partial(pltpu.with_memory_space_constraint, memory_space=pltpu.HBM)
    mine, down, *layers = prepare_call(far(cotangent), far(down_weight), far(field), half)
    grads, spread, to_partner, to_other = grad_call(far(coords), parent, mine, theirs, down, *layers)
    partner, other = over_core(to_partner), over_other(to_other)
    inner = inner_call(field, conv_weight)
    kept, sent, keep = main_call(
        coords, parent, near, field, partner, other, inner, down, grads, spread
    )

    got = over_core(sent)
    own = stage(add_halves, (kept, got), [sds((36, 64, 128), BF)])[0]
    gots = over_plane(own.reshape(16, 144, 128))
    partial_grad, token = input_call(near, grads, partner, other, far(conv_weight), own, 0)
    own = stage(add_sixteen, (gots,), [sds((144, 128), F32)], (token,))[0]
    gots = [over_y(own, k) for k in (1, 2, 3)]
    coarse, token = coarse_call(coords, keep, got, own)
    shares = stage(
        add_in_order, (own, *gots), [sds((16, 144, 128), BF)], (token,),
        scratch=[pltpu.VMEM((4, 144, 128), F32)],
    )[0]

    own = over_plane(shares).reshape(36, 64, 128)
    input_grad, token = input_call(near, grads, partner, other, far(conv_weight), shares, 1, partial_grad)
    own = after_call(own, token)
    got = over_core(own)
    halves = write_call(own)
    conv_grad, down_grad = write_call(got, halves, own=False)
    whole = (1, 1, 16, 16, 16, 128)
    return (
        coarse.reshape(whole),
        input_grad.reshape(whole),
        conv_grad.reshape(3, 3, 3, 128, 128),
        down_grad.reshape(2, 2, 2, 128, 128),
    )


def solution(mesh):
    sizes = (mesh.devices.shape[0], 4, 4, 2)
    mesh = jax.sharding.Mesh(mesh.devices.reshape(sizes), ("dp", "z", "x", "core"))
    region = ("z", "x", "core")
    bricks = P("dp", region, None, None, None, None)
    rows = P("dp", region, None)
    return jax.shard_map(
        local,
        mesh=mesh,
        in_specs=(bricks, P(), P(), bricks, rows, rows, P("dp", region)),
        out_specs=(bricks, bricks, P(), P()),
        check_vma=False,
    )
```

```python
import functools
import jax
import jax.numpy as jnp
from jax import lax
from jax.experimental import pallas as pl
from jax.experimental.pallas import tpu as pltpu
from jax.sharding import PartitionSpec as P

BF, F32 = jnp.bfloat16, jnp.float32
SMEM = pl.BlockSpec(memory_space=pltpu.SMEM)
VMEM = pl.BlockSpec(memory_space=pltpu.VMEM)
NN = (((1,), (0,)), ((), ()))
NT = (((1,), (1,)), ((), ()))
TN = (((0,), (0,)), ((), ()))


def dot(lhs, rhs, dims):
    return lax.dot_general(lhs, rhs, dims, preferred_element_type=F32)


def z_index(rows):
    return lax.broadcasted_iota(jnp.int32, (rows, 128), 0) % 16


def lay_interior(field_ref, shifts_ref, start=0, stop=16, base=1):
    z = z_index(256)

    for x in range(start, stop):
        plain = field_ref[x].reshape(256, 128)
        wide = plain.astype(F32)
        lower = jnp.where(z == 0, 0.0, pltpu.roll(wide, 1, 0)).astype(BF)
        upper = jnp.where(z == 15, 0.0, pltpu.roll(wide, 255, 0)).astype(BF)
        for c, value in enumerate((lower, plain, upper)):
            rows = value.reshape(8, 2, 16, 128)
            shifts_ref[c, x + base, 0:8, 1] = rows[:, 0]
            shifts_ref[c, x + base, 1:9, 0] = rows[:, 1]
            shifts_ref[c, x + base, 0, 0] = jnp.zeros((16, 128), BF)
            shifts_ref[c, x + base, 8, 1] = jnp.zeros((16, 128), BF)


def lay_slab(layer, flag, slab_ref):
    def three(value, b):
        rows = value.shape[0] * 16
        wide = value.astype(F32).reshape(rows, 128)
        z = z_index(rows)
        below, same, above = (flag(b, c) for c in (-1, 0, 1))
        lower = jnp.where(
            z == 0, pltpu.roll(wide, rows - 15, 0) * below, pltpu.roll(wide, 1, 0) * same
        )
        upper = jnp.where(
            z == 15, pltpu.roll(wide, 15, 0) * above, pltpu.roll(wide, rows - 1, 0) * same
        )
        return [v.astype(BF) for v in (lower, wide * same, upper)]

    for c, value in enumerate(three(layer, 0)):
        rows = value.reshape(8, 2, 16, 128)
        slab_ref[c, 0:8, 1] = rows[:, 0]
        slab_ref[c, 1:9, 0] = rows[:, 1]
    for c, value in enumerate(three(layer[15:16], -1)):
        slab_ref[c, 0, 0] = value.reshape(16, 128)
    for c, value in enumerate(three(layer[0:1], 1)):
        slab_ref[c, 8, 1] = value.reshape(16, 128)


def near_flag(near_ref, first):
    return lambda b, c: (near_ref[first + 3 * (b + 1) + c + 1] >= 0).astype(F32)


def window(shifts_ref, c, x, count):
    return jnp.concatenate(
        [
            shifts_ref[c, pl.ds(x, count), t // 2 : t // 2 + 8, t % 2].reshape(count * 128, 128)
            for t in range(4)
        ],
        axis=1,
    )


def prepare_kernel(
    cotangent_hbm, down_hbm, field_hbm, after_ref,
    mine_ref, down_ref, partner_ref, other_ref, sems,
):
    upper = lax.axis_index("core")
    copies = [
        pltpu.make_async_copy(field_hbm.at[15 - 15 * upper], partner_ref, sems.at[0]),
        pltpu.make_async_copy(field_hbm.at[15 * upper], other_ref, sems.at[1]),
    ]
    for k in range(4):
        copies.append(
            pltpu.make_async_copy(
                cotangent_hbm.at[pl.ds(8 * upper + 2 * k, 2)], mine_ref.at[2 * k : 2 * k + 2],
                sems.at[2 + k],
            )
        )
    for p in range(2):
        for q in range(2):
            for r in range(2):
                at = 2 * p + q
                rows, columns = slice(128 * at, 128 * at + 128), slice(128 * r, 128 * r + 128)
                copies.append(
                    pltpu.make_async_copy(
                        down_hbm.at[p, q, r], down_ref.at[rows, columns], sems.at[6 + 2 * at + r]
                    )
                )
    for copy in copies:
        copy.start()
    for copy in copies:
        copy.wait()


def grad_kernel(
    coords_ref, parent_ref, mine_ref, theirs_ref, down_ref, partner_ref, other_ref,
    grads_ref, spread_ref, to_partner_ref, to_other_ref, wide_ref,
):
    x, oy, oz = coords_ref[0], coords_ref[1] % 2, coords_ref[2] % 2
    is_own = parent_ref[0] == x
    down = down_ref[...]
    to_partner_ref[0] = partner_ref[...]
    to_other_ref[0] = other_ref[...]
    wide_ref[...] = jnp.zeros_like(wide_ref)
    for i in range(8):
        mine = mine_ref[i, pl.ds(8 * oy, 8)].astype(F32)
        theirs = theirs_ref[i, pl.ds(8 * oy, 8)].astype(F32)
        both = jnp.where(is_own, mine, theirs)
        part = jnp.where(oz == 0, both[:, 0:8], both[:, 8:16]).reshape(64, 128)
        wide_ref[i, pl.ds(0, 64, stride=2), :] = part
    for i in range(8):
        even = wide_ref[i]
        spread = jnp.concatenate([even, pltpu.roll(even, 1, 0)], axis=1).astype(BF)
        spread_ref[i] = spread
        grads = dot(spread, down, NT).astype(BF)
        for p in range(2):
            for q in range(2):
                at = (2 * p + q) * 128
                part = grads[:, at : at + 128].reshape(8, 16, 128)
                grads_ref[2 * i + p, :, q] = part
    upper = x % 2
    to_partner_ref[1] = grads_ref[15 - 15 * upper]
    to_other_ref[1] = grads_ref[15 * upper]


def lay_weights(conv_ref, weights_ref):
    zero = jnp.zeros((128, 128), BF)
    for a in range(3):
        for c in range(3):
            for t in range(4):
                for s in range(2):
                    weights_ref[a, c, t * 128 : t * 128 + 128, s * 128 : s * 128 + 128] = (
                        conv_ref[a, t - s, c] if 0 <= t - s <= 2 else zero
                    )


def inner_kernel(field_ref, conv_ref, shifts_ref, weights_ref, outputs_ref):
    lay_weights(conv_ref, weights_ref)
    lay_interior(field_ref, shifts_ref, 0, 6, 0)
    for first, count in ((1, 4), (5, 4), (9, 4), (13, 2)):
        lay_interior(field_ref, shifts_ref, min(first + 5, 16), min(first + 9, 16), 0)
        acc = None
        for a in range(3):
            for c in range(3):
                part = dot(window(shifts_ref, c, first + a - 1, count), weights_ref[a, c], NN)
                acc = part if acc is None else acc + part
        for s in range(2):
            field = field_ref[first : first + count, :, s].astype(F32)
            outputs_ref[first : first + count, :, s] = (
                acc[:, s * 128 : s * 128 + 128].reshape(count, 8, 16, 128) + field
            ).astype(BF)


def taps(rows):
    return jnp.concatenate(
        [rows[t // 2 : t // 2 + 8, t % 2].reshape(128, 128) for t in range(4)], axis=1
    )


def main_kernel(
    coords_ref, parent_ref, near_ref, field_ref, partner_ref, other_ref, shifts_ref, weights_ref,
    inner_ref, down_ref, grads_ref, spread_ref,
    kept_rows_ref, sent_ref, keep_ref, low_shifts_ref, high_shifts_ref, edges_ref, sums_ref,
):
    x, oy, oz = coords_ref[0], coords_ref[1] % 2, coords_ref[2] % 2
    first_core = x % 2 == 0
    kept = (parent_ref[0] == x).astype(F32)

    def part_rows(tap, rows):
        kept_rows_ref[tap] = jnp.where(first_core, rows[0:64], rows[64:128])
        sent_ref[tap] = jnp.where(first_core, rows[64:128], rows[0:64]).astype(BF)

    kept_rows_ref[35] = jnp.zeros((64, 128), F32)
    sent_ref[35] = jnp.zeros((64, 128), BF)
    sent_ref[52] = jnp.full((64, 128), oy, jnp.int32).astype(F32).astype(BF)
    partner, other = partner_ref[0].astype(F32), other_ref[0].astype(F32)
    low = jnp.where(first_core, other, partner).reshape(16, 16, 128)
    high = jnp.where(first_core, partner, other).reshape(16, 16, 128)
    lay_slab(low, near_flag(near_ref, 0), low_shifts_ref)
    lay_slab(high, near_flag(near_ref, 17), high_shifts_ref)

    accs = [None, None]
    for a in range(3):
        for c in range(3):
            for k, rows in enumerate((
                low_shifts_ref[c] if a == 0 else shifts_ref[c, a - 1],
                high_shifts_ref[c] if a == 2 else shifts_ref[c, 14 + a],
            )):
                part = dot(taps(rows), weights_ref[a, c], NN)
                accs[k] = part if accs[k] is None else accs[k] + part
    for s in range(2):
        for k in range(2):
            value = accs[k][:, s * 128 : s * 128 + 128].reshape(8, 16, 128)
            edges_ref[k, :, s] = (value + field_ref[15 * k, :, s].astype(F32)).astype(BF)

    down = down_ref[...]

    def corner(i, p, q):
        at = 2 * i + p
        rows = edges_ref[at // 15, :, q] if at in (0, 15) else inner_ref[at, :, q]
        return rows.reshape(128, 128)

    for i in range(8):
        corners = jnp.concatenate([corner(i, p, q) for p in range(2) for q in range(2)], axis=1)
        sums = dot(corners, down, NN)
        sums_ref[i, 0] = sums[:, 0:128]
        sums_ref[i, 1] = sums[:, 128:256]
        block = sums_ref[i, 0, pl.ds(0, 64, stride=2), :] + sums_ref[i, 1, pl.ds(1, 64, stride=2), :]
        block = block.reshape(8, 8, 128)
        none = jnp.zeros_like(block)
        low = jnp.where(oz == 0, block, none)
        high = jnp.where(oz == 0, none, block)
        placed = jnp.concatenate([low, high], axis=1).reshape(128, 128)
        keep_ref[i] = (placed * kept).astype(BF).reshape(8, 16, 128)
        away = (placed * (1 - kept)).astype(BF)
        sent_ref[36 + 2 * i] = away[0:64]
        sent_ref[37 + 2 * i] = away[64:128]

    spread = spread_ref[...].reshape(1024, 256)
    for p in range(2):
        for q in range(2):
            rows = jnp.concatenate([corner(i, p, q) for i in range(8)], axis=0)
            result = dot(rows, spread, TN) * (1.0 / 1024)
            part_rows(27 + 4 * p + 2 * q, result[:, 0:128])
            part_rows(28 + 4 * p + 2 * q, result[:, 128:256])

    pair = jnp.concatenate([grads_ref[:, :, s].reshape(2048, 128) for s in range(2)], axis=1)
    for a in range(3):
        for c in range(3):
            if a == 0:
                rows = jnp.concatenate(
                    [taps(low_shifts_ref[c]), window(shifts_ref, c, 0, 15)], axis=0
                )
            elif a == 1:
                rows = window(shifts_ref, c, 0, 16)
            else:
                rows = jnp.concatenate(
                    [window(shifts_ref, c, 1, 15), taps(high_shifts_ref[c])], axis=0
                )
            result = dot(rows, pair, TN) * (1.0 / 1024)
            for b in range(3):
                part_rows(
                    9 * a + 3 * b + c,
                    result[b * 128 : b * 128 + 128, 0:128]
                    + result[b * 128 + 128 : b * 128 + 256, 128:256],
                )


def input_kernel(near_ref, field_ref, partner_ref, other_ref, conv_hbm, *refs, half, tile=4):
    result_ref, token_ref, shifts_ref, weights_ref, held_ref, conv_ref, sems = refs[-7:]
    token_ref[...] = jnp.zeros_like(token_ref)
    conv_copies = [
        pltpu.make_async_copy(conv_hbm.at[a], conv_ref.at[a], sems.at[2 + a]) for a in range(3)
    ]
    for copy in conv_copies:
        copy.start()
    lay = functools.partial(lay_interior, field_ref, shifts_ref, base=1 - 8 * half)
    if half == 0:
        lay(0, 5)
    else:
        lay(7, 13)
    layer = jnp.where(
        lax.axis_index("core") == half, other_ref[1].astype(F32), partner_ref[1].astype(F32)
    )
    def lay_edge():
        lay_slab(
            layer.reshape(16, 16, 128), near_flag(near_ref, 17 * half), shifts_ref.at[:, 9 * half]
        )

    if half == 0:
        lay_edge()
    zero = jnp.zeros((128, 128), BF)
    for a in (2, 1, 0):
        conv_copies[2 - a].wait()
        for c in range(3):
            for t in range(4):
                for s in range(2):
                    weights_ref[a, c, s * 128 : s * 128 + 128, t * 128 : t * 128 + 128] = (
                        conv_ref[2 - a, 2 - t + s, 2 - c] if 0 <= t - s <= 2 else zero
                    )
    copies = []
    for step in range(8 // tile):
        first = step * tile
        if step == 1 and half == 0:
            lay(5, 9)
        if step == 1 and half == 1:
            lay(13, 16)
            lay_edge()
        acc = None
        for a in range(3):
            for c in range(3):
                part = dot(window(shifts_ref, c, first + a, tile), weights_ref[a, c], NT)
                acc = part if acc is None else acc + part
        here = 8 * half + first
        for s in range(2):
            field = field_ref[here : here + tile, :, s].astype(F32)
            held_ref[first : first + tile, :, s] = (
                acc[:, s * 128 : s * 128 + 128].reshape(tile, 8, 16, 128) + field
            ).astype(BF)
        copy = pltpu.make_async_copy(
            held_ref.at[pl.ds(first, tile)], result_ref.at[pl.ds(here, tile)], sems.at[step]
        )
        copy.start()
        copies.append(copy)
    for copy in copies:
        copy.wait()


def coarse_kernel(coords_ref, keep_ref, got_ref, coarse_ref, token_ref, held_ref, sems):
    token_ref[...] = jnp.zeros_like(token_ref)
    upper, oy = coords_ref[0] % 2, coords_ref[1] % 2
    there = got_ref[52, 0:16].astype(F32)
    none = jnp.zeros((8, 16, 128), BF)
    for i in range(8):
        rows = jnp.concatenate([got_ref[36 + 2 * i], got_ref[37 + 2 * i]], axis=0)
        rows = rows.reshape(8, 16, 128).astype(F32)
        held_ref[0, i, pl.ds(8 * oy, 8)] = keep_ref[i]
        held_ref[0, i, pl.ds(8 - 8 * oy, 8)] = none
        held_ref[1, i, 0:8] = jnp.where(there == 0, rows, 0.0).astype(BF)
        held_ref[1, i, 8:16] = jnp.where(there == 1, rows, 0.0).astype(BF)
    keep = pltpu.make_async_copy(held_ref.at[0], coarse_ref.at[pl.ds(8 * upper, 8)], sems.at[0])
    got = pltpu.make_async_copy(held_ref.at[1], coarse_ref.at[pl.ds(8 - 8 * upper, 8)], sems.at[1])
    keep.start()
    got.start()
    keep.wait()
    got.wait()


ANY = pl.BlockSpec(memory_space=pl.ANY)
HBM = pl.BlockSpec(memory_space=pltpu.HBM)
TOKEN = jax.ShapeDtypeStruct((8, 128), F32)
sds = jax.ShapeDtypeStruct


def call(kernel, ins, outs, scratch=(), flops=0, moved=1 << 20, limit=8, out=VMEM, **kw):
    return pl.pallas_call(
        kernel,
        in_specs=ins,
        out_specs=[VMEM if shape is TOKEN else out for shape in outs],
        out_shape=outs,
        scratch_shapes=list(scratch),
        cost_estimate=pl.CostEstimate(flops=flops, bytes_accessed=moved, transcendentals=0),
        compiler_params=pltpu.CompilerParams(vmem_limit_bytes=limit << 20),
        **kw,
    )


def halves_call(kept, got):
    return call(
        add_halves, [VMEM] * 2, [sds((36, 64, 128), BF)],
        [pltpu.VMEM((36, 64, 128), BF), pltpu.SemaphoreType.DMA((4,))], out=ANY,
    )(kept, got)[0]


def share_call(own, gots):
    return call(
        add_in_order, [VMEM] * 4, [sds((16, 144, 128), BF)],
        [pltpu.VMEM((4, 144, 128), F32), pltpu.VMEM((144, 128), BF),
         pltpu.SemaphoreType.DMA((16,))], out=ANY,
    )(own, *gots)[0]


def prepare_call(cotangent, down, field, after):
    layer = sds((8, 2, 16, 128), BF)
    return call(
        prepare_kernel, [HBM] * 3 + [ANY],
        [sds((8, 16, 16, 128), BF), sds((512, 256), BF), layer, layer],
        [pltpu.SemaphoreType.DMA((14,))], moved=1 << 20,
    )(cotangent, down, field, after)


def grad_call(coords, parent, mine, theirs, down, partner, other):
    layers = sds((2, 8, 2, 16, 128), BF)
    return call(
        grad_kernel, [SMEM] * 2 + [VMEM] * 5,
        [sds((16, 8, 2, 16, 128), BF), sds((8, 128, 256), BF), layers, layers],
        [pltpu.VMEM((8, 128, 128), F32)], flops=2 * 2**27, moved=4 << 20,
    )(coords, parent, mine, theirs, down, partner, other)


def inner_call(field, conv):
    return call(
        inner_kernel, [VMEM] * 2,
        [sds((3, 16, 9, 2, 16, 128), BF), sds((3, 3, 512, 256), BF), sds((16, 8, 2, 16, 128), BF)],
        flops=2 * 9 * 2048 * 512 * 256, moved=2 << 20, limit=16,
    )(field, conv)


def main_call(coords, parent, near, field, partner, other, inner, down, grads, spread):
    slab = pltpu.VMEM((3, 9, 2, 16, 128), BF)
    return call(
        main_kernel, [SMEM] * 3 + [VMEM] * 9,
        [sds((36, 64, 128), F32), sds((53, 64, 128), BF), sds((8, 8, 16, 128), BF)],
        [slab, slab, pltpu.VMEM((2, 8, 2, 16, 128), BF), pltpu.VMEM((8, 2, 128, 128), F32)],
        flops=2 * 9 * 2048 * 512 * 256, limit=24,
    )(coords, parent, near, field, partner, other, *inner, down, grads, spread)


def input_call(near, field, partner, other, conv, after, half, base=None):
    ins, values = [SMEM] + [VMEM] * 3 + [HBM, ANY], [near, field, partner, other, conv, after]
    aliases = {}
    if base is not None:
        ins, values, aliases = ins + [ANY], values + [base], {6: 0}
    return call(
        functools.partial(input_kernel, half=half), ins, [sds((16, 8, 2, 16, 128), BF), TOKEN],
        [pltpu.VMEM((3, 10, 9, 2, 16, 128), BF), pltpu.VMEM((3, 3, 256, 512), BF),
         pltpu.VMEM((8, 8, 2, 16, 128), BF), pltpu.VMEM((3, 3, 3, 128, 128), BF),
         pltpu.SemaphoreType.DMA((5,))],
        flops=9 * 2048 * 512 * 256, limit=24, out=ANY, input_output_aliases=aliases,
    )(*values)


def coarse_call(coords, keep, got, after):
    def kernel(coords_ref, keep_ref, got_ref, after_ref, *refs):
        coarse_kernel(coords_ref, keep_ref, got_ref, *refs)

    return call(
        kernel, [SMEM] + [VMEM] * 2 + [ANY], [sds((16, 16, 16, 128), BF), TOKEN],
        [pltpu.VMEM((2, 8, 16, 16, 128), BF), pltpu.SemaphoreType.DMA((2,))], out=ANY,
    )(coords, keep, got, after)


def add_halves(kept_ref, got_ref, total_ref, held_ref, sems):
    copies = []
    for k in range(4):
        part = slice(9 * k, 9 * k + 9)
        held_ref[part] = (kept_ref[part] + got_ref[part].astype(F32)).astype(BF)
        copies.append(pltpu.make_async_copy(held_ref.at[part], total_ref.at[part], sems.at[k]))
        copies[-1].start()
    for copy in copies:
        copy.wait()


def add_sixteen(got_ref, *refs):
    total = got_ref[0].astype(F32)
    for k in range(1, 16):
        total = total + got_ref[k].astype(F32)
    refs[-1][...] = total


def add_in_order(own_ref, *refs):
    y = lax.axis_index("dp")
    total_ref, slots_ref, held_ref, sems = refs[-4:]
    for k, ref in enumerate((own_ref, *refs[:3])):
        slots_ref[(y - k + 4) % 4] = ref[...]
    held_ref[...] = ((slots_ref[0] + slots_ref[1]) + (slots_ref[2] + slots_ref[3])).astype(BF)
    copies = [pltpu.make_async_copy(held_ref, total_ref.at[k], sems.at[k]) for k in range(16)]
    for copy in copies:
        copy.start()
    for copy in copies:
        copy.wait()


def after_call(value, token):
    def kernel(value_ref, token_ref, same_ref):
        pass

    return call(
        kernel, [ANY] * 2, [sds(value.shape, value.dtype)], out=ANY, input_output_aliases={0: 0},
        moved=1024,
    )(value, token)[0]


def write_half(rows_ref, *refs, own):
    conv_ref, down_ref, token_ref, wide_ref, sems = refs[-5:]
    token_ref[...] = jnp.zeros_like(token_ref)
    core = lax.axis_index("core")
    here = pl.ds(pl.multiple_of(64 * (core if own else 1 - core), 64), 64)
    copies = []
    for k, (start, stop) in enumerate(((0, 9), (9, 18), (18, 27), (27, 35))):
        wide_ref[start:stop] = rows_ref[start:stop].astype(F32)
        if start < 27:
            target = conv_ref.at[start:stop, here]
        else:
            target = down_ref.at[:, here]
        copies.append(pltpu.make_async_copy(wide_ref.at[start:stop], target, sems.at[k]))
        copies[-1].start()
    for copy in copies:
        copy.wait()


def write_call(rows, bases=(), own=True):
    return call(
        functools.partial(write_half, own=own), [VMEM] + [ANY] * len(bases),
        [sds((27, 128, 128), F32), sds((8, 128, 128), F32), TOKEN],
        [pltpu.VMEM((36, 64, 128), F32), pltpu.SemaphoreType.DMA((4,))], out=ANY,
        input_output_aliases={1: 0, 2: 1} if bases else {},
    )(rows, *bases)[:2]


def over_core(value):
    return lax.ppermute(value, "core", [(0, 1), (1, 0)])


def over_y(value, by):
    return lax.ppermute(value, "dp", [(i, (i + by) % 4) for i in range(4)])


def over_plane(value):
    return lax.all_to_all(value, ("z", "x"), 0, 0, tiled=True)


def stage(kernel, values, outs, after=(), scratch=()):
    return call(kernel, [VMEM] * len(values) + [ANY] * len(after), outs, scratch)(*values, *after)


def over_other(value):
    pairs = [(i, i + 1) for i in range(1, 31, 2)] + [(i + 1, i) for i in range(1, 31, 2)]
    return lax.ppermute(value, ("z", "x", "core"), pairs)


def local(features, conv_weight, down_weight, coarse_cotangent, brick_coords, neighbours, parents):
    coords, near, parent = brick_coords.reshape(3), neighbours.reshape(26), parents.reshape(1)
    core = lax.axis_index("core")
    cotangent = coarse_cotangent.reshape(16, 16, 16, 128)
    half = lax.dynamic_slice_in_dim(cotangent, 8 * (1 - core), 8)
    theirs = over_core(half)
    field = features.reshape(16, 8, 2, 16, 128)
    far = functools.partial(pltpu.with_memory_space_constraint, memory_space=pltpu.HBM)
    mine, down, *layers = prepare_call(far(cotangent), far(down_weight), far(field), half)
    grads, spread, to_partner, to_other = grad_call(far(coords), parent, mine, theirs, down, *layers)
    partner, other = over_core(to_partner), over_other(to_other)
    inner = inner_call(field, conv_weight)
    kept, sent, keep = main_call(
        coords, parent, near, field, partner, other, inner, down, grads, spread
    )

    got = over_core(sent)
    own = halves_call(kept, got)
    gots = over_plane(own.reshape(16, 144, 128))
    partial_grad, token = input_call(near, grads, partner, other, far(conv_weight), own, 0)
    coarse, token = coarse_call(coords, keep, got, token)
    own = stage(add_sixteen, (gots,), [sds((144, 128), F32)], (token,))[0]
    gots = [over_y(own, k) for k in (1, 2, 3)]
    shares = share_call(own, gots)

    own = over_plane(shares).reshape(36, 64, 128)
    input_grad, token = input_call(near, grads, partner, other, far(conv_weight), shares, 1, partial_grad)
    own = after_call(own, token)
    got = over_core(own)
    halves = write_call(own)
    conv_grad, down_grad = write_call(got, halves, own=False)
    whole = (1, 1, 16, 16, 16, 128)
    return (
        coarse.reshape(whole),
        input_grad.reshape(whole),
        conv_grad.reshape(3, 3, 3, 128, 128),
        down_grad.reshape(2, 2, 2, 128, 128),
    )


def solution(mesh):
    sizes = (mesh.devices.shape[0], 4, 4, 2)
    mesh = jax.sharding.Mesh(mesh.devices.reshape(sizes), ("dp", "z", "x", "core"))
    region = ("z", "x", "core")
    bricks = P("dp", region, None, None, None, None)
    rows = P("dp", region, None)
    return jax.shard_map(
        local,
        mesh=mesh,
        in_specs=(bricks, P(), P(), bricks, rows, rows, P("dp", region)),
        out_specs=(bricks, bricks, P(), P()),
        check_vma=False,
    )
```

```python
import functools
import jax
import jax.numpy as jnp
from jax import lax
from jax.experimental import pallas as pl
from jax.experimental.pallas import tpu as pltpu
from jax.sharding import PartitionSpec as P

BF, F32 = jnp.bfloat16, jnp.float32
SMEM = pl.BlockSpec(memory_space=pltpu.SMEM)
VMEM = pl.BlockSpec(memory_space=pltpu.VMEM)
NN = (((1,), (0,)), ((), ()))
NT = (((1,), (1,)), ((), ()))
TN = (((0,), (0,)), ((), ()))


def dot(lhs, rhs, dims):
    return lax.dot_general(lhs, rhs, dims, preferred_element_type=F32)


def z_index(rows):
    return lax.broadcasted_iota(jnp.int32, (rows, 128), 0) % 16


def lay_interior(field_ref, shifts_ref, start=0, stop=16, base=1):
    z = z_index(256)

    for x in range(start, stop):
        plain = field_ref[x].reshape(256, 128)
        wide = plain.astype(F32)
        lower = jnp.where(z == 0, 0.0, pltpu.roll(wide, 1, 0)).astype(BF)
        upper = jnp.where(z == 15, 0.0, pltpu.roll(wide, 255, 0)).astype(BF)
        for c, value in enumerate((lower, plain, upper)):
            rows = value.reshape(8, 2, 16, 128)
            shifts_ref[c, x + base, 0:8, 1] = rows[:, 0]
            shifts_ref[c, x + base, 1:9, 0] = rows[:, 1]
            shifts_ref[c, x + base, 0, 0] = jnp.zeros((16, 128), BF)
            shifts_ref[c, x + base, 8, 1] = jnp.zeros((16, 128), BF)


def lay_slab(layer, flag, slab_ref):
    def three(value, b):
        rows = value.shape[0] * 16
        wide = value.astype(F32).reshape(rows, 128)
        z = z_index(rows)
        below, same, above = (flag(b, c) for c in (-1, 0, 1))
        lower = jnp.where(
            z == 0, pltpu.roll(wide, rows - 15, 0) * below, pltpu.roll(wide, 1, 0) * same
        )
        upper = jnp.where(
            z == 15, pltpu.roll(wide, 15, 0) * above, pltpu.roll(wide, rows - 1, 0) * same
        )
        return [v.astype(BF) for v in (lower, wide * same, upper)]

    for c, value in enumerate(three(layer, 0)):
        rows = value.reshape(8, 2, 16, 128)
        slab_ref[c, 0:8, 1] = rows[:, 0]
        slab_ref[c, 1:9, 0] = rows[:, 1]
    for c, value in enumerate(three(layer[15:16], -1)):
        slab_ref[c, 0, 0] = value.reshape(16, 128)
    for c, value in enumerate(three(layer[0:1], 1)):
        slab_ref[c, 8, 1] = value.reshape(16, 128)


def near_flag(near_ref, first):
    return lambda b, c: (near_ref[first + 3 * (b + 1) + c + 1] >= 0).astype(F32)


def window(shifts_ref, c, x, count):
    return jnp.concatenate(
        [
            shifts_ref[c, pl.ds(x, count), t // 2 : t // 2 + 8, t % 2].reshape(count * 128, 128)
            for t in range(4)
        ],
        axis=1,
    )


def prepare_kernel(
    cotangent_hbm, down_hbm, field_hbm, conv_hbm,
    mine_ref, down_ref, partner_ref, other_ref, shifts_ref, weights_ref,
    field_ref, conv_ref, sems,
):
    upper = lax.axis_index("core")
    fetches = [
        pltpu.make_async_copy(
            field_hbm.at[pl.ds(4 * k, 4)], field_ref.at[pl.ds(4 * k, 4)], sems.at[14 + k]
        )
        for k in range(4)
    ]
    conv_copy = pltpu.make_async_copy(conv_hbm, conv_ref, sems.at[18])
    for copy in (*fetches, conv_copy):
        copy.start()
    copies = [
        pltpu.make_async_copy(field_hbm.at[15 - 15 * upper], partner_ref, sems.at[0]),
        pltpu.make_async_copy(field_hbm.at[15 * upper], other_ref, sems.at[1]),
    ]
    for k in range(4):
        copies.append(
            pltpu.make_async_copy(
                cotangent_hbm.at[pl.ds(8 * upper + 2 * k, 2)], mine_ref.at[2 * k : 2 * k + 2],
                sems.at[2 + k],
            )
        )
    for p in range(2):
        for q in range(2):
            for r in range(2):
                at = 2 * p + q
                rows, columns = slice(128 * at, 128 * at + 128), slice(128 * r, 128 * r + 128)
                copies.append(
                    pltpu.make_async_copy(
                        down_hbm.at[p, q, r], down_ref.at[rows, columns], sems.at[6 + 2 * at + r]
                    )
                )
    for copy in copies:
        copy.start()
    for k in range(4):
        fetches[k].wait()
        lay_interior(field_ref, shifts_ref, 4 * k, 4 * k + 4, 0)
    conv_copy.wait()
    lay_weights(conv_ref, weights_ref)
    for copy in copies:
        copy.wait()


def grad_kernel(
    coords_ref, parent_ref, mine_ref, theirs_ref, down_ref, partner_ref, other_ref,
    grads_ref, spread_ref, to_partner_ref, to_other_ref, wide_ref,
):
    x, oy, oz = coords_ref[0], coords_ref[1] % 2, coords_ref[2] % 2
    is_own = parent_ref[0] == x
    down = down_ref[...]
    to_partner_ref[0] = partner_ref[...]
    to_other_ref[0] = other_ref[...]
    wide_ref[...] = jnp.zeros_like(wide_ref)
    for i in range(8):
        mine = mine_ref[i, pl.ds(8 * oy, 8)].astype(F32)
        theirs = theirs_ref[8 * (x % 2) + i, pl.ds(8 * oy, 8)].astype(F32)
        both = jnp.where(is_own, mine, theirs)
        part = jnp.where(oz == 0, both[:, 0:8], both[:, 8:16]).reshape(64, 128)
        wide_ref[i, pl.ds(0, 64, stride=2), :] = part
    for i in range(8):
        even = wide_ref[i]
        spread = jnp.concatenate([even, pltpu.roll(even, 1, 0)], axis=1).astype(BF)
        spread_ref[i] = spread
        grads = dot(spread, down, NT).astype(BF)
        for p in range(2):
            for q in range(2):
                at = (2 * p + q) * 128
                part = grads[:, at : at + 128].reshape(8, 16, 128)
                grads_ref[2 * i + p, :, q] = part
    upper = x % 2
    to_partner_ref[1] = grads_ref[15 - 15 * upper]
    to_other_ref[1] = grads_ref[15 * upper]


def lay_weights(conv_ref, weights_ref):
    zero = jnp.zeros((128, 128), BF)
    for a in range(3):
        for c in range(3):
            for t in range(4):
                for s in range(2):
                    weights_ref[a, c, t * 128 : t * 128 + 128, s * 128 : s * 128 + 128] = (
                        conv_ref[a, t - s, c] if 0 <= t - s <= 2 else zero
                    )


def inner_kernel(shifts_ref, weights_ref, outputs_ref):
    for first, count in ((1, 7), (8, 7)):
        acc = None
        for a in range(3):
            for c in range(3):
                part = dot(window(shifts_ref, c, first + a - 1, count), weights_ref[a, c], NN)
                acc = part if acc is None else acc + part
        for s in range(2):
            field = center(shifts_ref, first, count, s)
            outputs_ref[first : first + count, :, s] = (
                acc[:, s * 128 : s * 128 + 128].reshape(count, 8, 16, 128) + field
            ).astype(BF)


def center(shifts_ref, x, count, s):
    return shifts_ref[1, x : x + count, s : s + 8, 1 - s].astype(F32)


def taps(rows):
    return jnp.concatenate(
        [rows[t // 2 : t // 2 + 8, t % 2].reshape(128, 128) for t in range(4)], axis=1
    )


def main_kernel(
    coords_ref, parent_ref, near_ref, partner_ref, other_ref, shifts_ref, weights_ref,
    inner_ref, down_ref, grads_ref, spread_ref,
    kept_rows_ref, sent_ref, keep_ref, low_shifts_ref, high_shifts_ref, edges_ref, sums_ref,
):
    x, oy, oz = coords_ref[0], coords_ref[1] % 2, coords_ref[2] % 2
    first_core = x % 2 == 0
    kept = (parent_ref[0] == x).astype(F32)

    def part_rows(tap, rows):
        kept_rows_ref[tap] = jnp.where(first_core, rows[0:64], rows[64:128])
        sent_ref[tap] = jnp.where(first_core, rows[64:128], rows[0:64]).astype(BF)

    kept_rows_ref[35] = jnp.zeros((64, 128), F32)
    sent_ref[35] = jnp.zeros((64, 128), BF)
    sent_ref[52] = jnp.full((64, 128), oy, jnp.int32).astype(F32).astype(BF)
    partner, other = partner_ref[0].astype(F32), other_ref[0].astype(F32)
    low = jnp.where(first_core, other, partner).reshape(16, 16, 128)
    high = jnp.where(first_core, partner, other).reshape(16, 16, 128)
    lay_slab(low, near_flag(near_ref, 0), low_shifts_ref)
    lay_slab(high, near_flag(near_ref, 17), high_shifts_ref)

    accs = [None, None]
    for a in range(3):
        for c in range(3):
            for k, rows in enumerate((
                low_shifts_ref[c] if a == 0 else shifts_ref[c, a - 1],
                high_shifts_ref[c] if a == 2 else shifts_ref[c, 14 + a],
            )):
                part = dot(taps(rows), weights_ref[a, c], NN)
                accs[k] = part if accs[k] is None else accs[k] + part
    for s in range(2):
        for k in range(2):
            value = accs[k][:, s * 128 : s * 128 + 128].reshape(8, 16, 128)
            edges_ref[k, :, s] = (value + center(shifts_ref, 15 * k, 1, s)[0]).astype(BF)

    down = down_ref[...]

    def corner(i, p, q):
        at = 2 * i + p
        rows = edges_ref[at // 15, :, q] if at in (0, 15) else inner_ref[at, :, q]
        return rows.reshape(128, 128)

    for i in range(8):
        corners = jnp.concatenate([corner(i, p, q) for p in range(2) for q in range(2)], axis=1)
        sums = dot(corners, down, NN)
        sums_ref[i, 0] = sums[:, 0:128]
        sums_ref[i, 1] = sums[:, 128:256]
        block = sums_ref[i, 0, pl.ds(0, 64, stride=2), :] + sums_ref[i, 1, pl.ds(1, 64, stride=2), :]
        block = block.reshape(8, 8, 128)
        none = jnp.zeros_like(block)
        low = jnp.where(oz == 0, block, none)
        high = jnp.where(oz == 0, none, block)
        placed = jnp.concatenate([low, high], axis=1).reshape(128, 128)
        keep_ref[i] = (placed * kept).astype(BF).reshape(8, 16, 128)
        away = (placed * (1 - kept)).astype(BF)
        sent_ref[36 + 2 * i] = away[0:64]
        sent_ref[37 + 2 * i] = away[64:128]

    spread = spread_ref[...].reshape(1024, 256)
    for p in range(2):
        for q in range(2):
            rows = jnp.concatenate([corner(i, p, q) for i in range(8)], axis=0)
            result = dot(rows, spread, TN) * (1.0 / 1024)
            part_rows(27 + 4 * p + 2 * q, result[:, 0:128])
            part_rows(28 + 4 * p + 2 * q, result[:, 128:256])

    pair = jnp.concatenate([grads_ref[:, :, s].reshape(2048, 128) for s in range(2)], axis=1)
    for a in range(3):
        for c in range(3):
            if a == 0:
                rows = jnp.concatenate(
                    [taps(low_shifts_ref[c]), window(shifts_ref, c, 0, 15)], axis=0
                )
            elif a == 1:
                rows = window(shifts_ref, c, 0, 16)
            else:
                rows = jnp.concatenate(
                    [window(shifts_ref, c, 1, 15), taps(high_shifts_ref[c])], axis=0
                )
            result = dot(rows, pair, TN) * (1.0 / 1024)
            for b in range(3):
                part_rows(
                    9 * a + 3 * b + c,
                    result[b * 128 : b * 128 + 128, 0:128]
                    + result[b * 128 + 128 : b * 128 + 256, 128:256],
                )


def input_kernel(near_ref, field_ref, partner_ref, other_ref, conv_hbm, *refs, half, tile=4):
    result_ref, token_ref, shifts_ref, weights_ref, held_ref, conv_ref, sems = refs[-7:]
    token_ref[...] = jnp.zeros_like(token_ref)
    conv_copies = [
        pltpu.make_async_copy(conv_hbm.at[a], conv_ref.at[a], sems.at[2 + a]) for a in range(3)
    ]
    for copy in conv_copies:
        copy.start()
    lay = functools.partial(lay_interior, field_ref, shifts_ref, base=1 - 8 * half)
    if half == 0:
        lay(0, 5)
    else:
        lay(7, 13)
    layer = jnp.where(
        lax.axis_index("core") == half, other_ref[1].astype(F32), partner_ref[1].astype(F32)
    )
    def lay_edge():
        lay_slab(
            layer.reshape(16, 16, 128), near_flag(near_ref, 17 * half), shifts_ref.at[:, 9 * half]
        )

    if half == 0:
        lay_edge()
    zero = jnp.zeros((128, 128), BF)
    for a in (2, 1, 0):
        conv_copies[2 - a].wait()
        for c in range(3):
            for t in range(4):
                for s in range(2):
                    weights_ref[a, c, s * 128 : s * 128 + 128, t * 128 : t * 128 + 128] = (
                        conv_ref[2 - a, 2 - t + s, 2 - c] if 0 <= t - s <= 2 else zero
                    )
    copies = []
    for step in range(8 // tile):
        first = step * tile
        if step == 1 and half == 0:
            lay(5, 9)
        if step == 1 and half == 1:
            lay(13, 16)
            lay_edge()
        acc = None
        for a in range(3):
            for c in range(3):
                part = dot(window(shifts_ref, c, first + a, tile), weights_ref[a, c], NT)
                acc = part if acc is None else acc + part
        here = 8 * half + first
        for s in range(2):
            field = field_ref[here : here + tile, :, s].astype(F32)
            held_ref[first : first + tile, :, s] = (
                acc[:, s * 128 : s * 128 + 128].reshape(tile, 8, 16, 128) + field
            ).astype(BF)
        copy = pltpu.make_async_copy(
            held_ref.at[pl.ds(first, tile)], result_ref.at[pl.ds(here, tile)], sems.at[step]
        )
        copy.start()
        copies.append(copy)
    for copy in copies:
        copy.wait()


def coarse_kernel(coords_ref, keep_ref, got_ref, coarse_ref, token_ref, held_ref, sems):
    token_ref[...] = jnp.zeros_like(token_ref)
    upper, oy = coords_ref[0] % 2, coords_ref[1] % 2
    there = got_ref[52, 0:16].astype(F32)
    none = jnp.zeros((8, 16, 128), BF)
    for i in range(8):
        rows = jnp.concatenate([got_ref[36 + 2 * i], got_ref[37 + 2 * i]], axis=0)
        rows = rows.reshape(8, 16, 128).astype(F32)
        held_ref[0, i, pl.ds(8 * oy, 8)] = keep_ref[i]
        held_ref[0, i, pl.ds(8 - 8 * oy, 8)] = none
        held_ref[1, i, 0:8] = jnp.where(there == 0, rows, 0.0).astype(BF)
        held_ref[1, i, 8:16] = jnp.where(there == 1, rows, 0.0).astype(BF)
    keep = pltpu.make_async_copy(held_ref.at[0], coarse_ref.at[pl.ds(8 * upper, 8)], sems.at[0])
    got = pltpu.make_async_copy(held_ref.at[1], coarse_ref.at[pl.ds(8 - 8 * upper, 8)], sems.at[1])
    keep.start()
    got.start()
    keep.wait()
    got.wait()


ANY = pl.BlockSpec(memory_space=pl.ANY)
HBM = pl.BlockSpec(memory_space=pltpu.HBM)
TOKEN = jax.ShapeDtypeStruct((8, 128), F32)
sds = jax.ShapeDtypeStruct


def call(kernel, ins, outs, scratch=(), flops=0, moved=1 << 20, limit=8, out=VMEM, **kw):
    return pl.pallas_call(
        kernel,
        in_specs=ins,
        out_specs=[VMEM if shape is TOKEN else out for shape in outs],
        out_shape=outs,
        scratch_shapes=list(scratch),
        cost_estimate=pl.CostEstimate(flops=flops, bytes_accessed=moved, transcendentals=0),
        compiler_params=pltpu.CompilerParams(vmem_limit_bytes=limit << 20),
        **kw,
    )


def prepare_call(cotangent, down, field, conv):
    layer = sds((8, 2, 16, 128), BF)
    return call(
        prepare_kernel, [HBM] * 4,
        [sds((8, 16, 16, 128), BF), sds((512, 256), BF), layer, layer,
         sds((3, 16, 9, 2, 16, 128), BF), sds((3, 3, 512, 256), BF)],
        [pltpu.VMEM((16, 8, 2, 16, 128), BF), pltpu.VMEM((3, 3, 3, 128, 128), BF),
         pltpu.SemaphoreType.DMA((19,))], moved=4 << 20,
    )(cotangent, down, field, conv)


def grad_call(coords, parent, mine, theirs, down, partner, other):
    layers = sds((2, 8, 2, 16, 128), BF)
    return call(
        grad_kernel, [SMEM] * 2 + [VMEM] * 5,
        [sds((16, 8, 2, 16, 128), BF), sds((8, 128, 256), BF), layers, layers],
        [pltpu.VMEM((8, 128, 128), F32)], flops=2 * 2**27, moved=4 << 20,
    )(coords, parent, mine, theirs, down, partner, other)


def inner_call(shifts, weights):
    return call(
        inner_kernel, [VMEM] * 2, [sds((16, 8, 2, 16, 128), BF)],
        flops=2 * 9 * 2048 * 512 * 256, moved=2 << 20, limit=16,
    )(shifts, weights)[0]


def main_call(coords, parent, near, partner, other, inner, down, grads, spread):
    slab = pltpu.VMEM((3, 9, 2, 16, 128), BF)
    return call(
        main_kernel, [SMEM] * 3 + [VMEM] * 8,
        [sds((36, 64, 128), F32), sds((53, 64, 128), BF), sds((8, 8, 16, 128), BF)],
        [slab, slab, pltpu.VMEM((2, 8, 2, 16, 128), BF), pltpu.VMEM((8, 2, 128, 128), F32)],
        flops=2 * 9 * 2048 * 512 * 256, limit=24,
    )(coords, parent, near, partner, other, *inner, down, grads, spread)


def input_call(near, field, partner, other, conv, after, half, base=None):
    ins, values = [SMEM] + [VMEM] * 3 + [HBM, ANY], [near, field, partner, other, conv, after]
    aliases = {}
    if base is not None:
        ins, values, aliases = ins + [ANY], values + [base], {6: 0}
    return call(
        functools.partial(input_kernel, half=half), ins, [sds((16, 8, 2, 16, 128), BF), TOKEN],
        [pltpu.VMEM((3, 10, 9, 2, 16, 128), BF), pltpu.VMEM((3, 3, 256, 512), BF),
         pltpu.VMEM((8, 8, 2, 16, 128), BF), pltpu.VMEM((3, 3, 3, 128, 128), BF),
         pltpu.SemaphoreType.DMA((5,))],
        flops=9 * 2048 * 512 * 256, limit=24, out=ANY, input_output_aliases=aliases,
    )(*values)


def coarse_call(coords, keep, got, after):
    def kernel(coords_ref, keep_ref, got_ref, after_ref, *refs):
        coarse_kernel(coords_ref, keep_ref, got_ref, *refs)

    return call(
        kernel, [SMEM] + [VMEM] * 2 + [ANY], [sds((16, 16, 16, 128), BF), TOKEN],
        [pltpu.VMEM((2, 8, 16, 16, 128), BF), pltpu.SemaphoreType.DMA((2,))], out=ANY,
    )(coords, keep, got, after)


def add_halves(kept_ref, got_ref, total_ref):
    total_ref[...] = (kept_ref[...] + got_ref[0:36].astype(F32)).astype(BF)


def add_sixteen(got_ref, *refs):
    total = got_ref[0].astype(F32)
    for k in range(1, 16):
        total = total + got_ref[k].astype(F32)
    refs[-1][...] = total


def add_in_order(own_ref, *refs):
    y = lax.axis_index("dp")
    total_ref, slots_ref = refs[-2:]
    for k, ref in enumerate((own_ref, *refs[:3])):
        slots_ref[(y - k + 4) % 4] = ref[...]
    total = ((slots_ref[0] + slots_ref[1]) + (slots_ref[2] + slots_ref[3])).astype(BF)
    for k in range(16):
        total_ref[k] = total


def after_call(value, token):
    def kernel(value_ref, token_ref, same_ref):
        pass

    return call(
        kernel, [ANY] * 2, [sds(value.shape, value.dtype)], out=ANY, input_output_aliases={0: 0},
        moved=1024,
    )(value, token)[0]


def write_half(rows_ref, *refs, own):
    conv_ref, down_ref, token_ref, wide_ref, sems = refs[-5:]
    token_ref[...] = jnp.zeros_like(token_ref)
    core = lax.axis_index("core")
    here = pl.ds(pl.multiple_of(64 * (core if own else 1 - core), 64), 64)
    copies = []
    for k, (start, stop) in enumerate(((0, 9), (9, 18), (18, 27), (27, 35))):
        wide_ref[start:stop] = rows_ref[start:stop].astype(F32)
        if start < 27:
            target = conv_ref.at[start:stop, here]
        else:
            target = down_ref.at[:, here]
        copies.append(pltpu.make_async_copy(wide_ref.at[start:stop], target, sems.at[k]))
        copies[-1].start()
    for copy in copies:
        copy.wait()


def write_call(rows, bases=(), own=True):
    return call(
        functools.partial(write_half, own=own), [VMEM] + [ANY] * len(bases),
        [sds((27, 128, 128), F32), sds((8, 128, 128), F32), TOKEN],
        [pltpu.VMEM((36, 64, 128), F32), pltpu.SemaphoreType.DMA((4,))], out=ANY,
        input_output_aliases={1: 0, 2: 1} if bases else {},
    )(rows, *bases)[:2]


def over_core(value):
    return lax.ppermute(value, "core", [(0, 1), (1, 0)])


def over_y(value, by):
    return lax.ppermute(value, "dp", [(i, (i + by) % 4) for i in range(4)])


def over_plane(value):
    return lax.all_to_all(value, ("z", "x"), 0, 0, tiled=True)


def stage(kernel, values, outs, after=(), scratch=()):
    return call(kernel, [VMEM] * len(values) + [ANY] * len(after), outs, scratch)(*values, *after)


def over_other(value):
    pairs = [(i, i + 1) for i in range(1, 31, 2)] + [(i + 1, i) for i in range(1, 31, 2)]
    return lax.ppermute(value, ("z", "x", "core"), pairs)


def local(features, conv_weight, down_weight, coarse_cotangent, brick_coords, neighbours, parents):
    coords, near, parent = brick_coords.reshape(3), neighbours.reshape(26), parents.reshape(1)
    cotangent = coarse_cotangent.reshape(16, 16, 16, 128)
    theirs = over_core(cotangent)
    field = features.reshape(16, 8, 2, 16, 128)
    far = functools.partial(pltpu.with_memory_space_constraint, memory_space=pltpu.HBM)
    mine, down, partner, other, shifts, weights = prepare_call(
        far(cotangent), far(down_weight), far(field), far(conv_weight)
    )
    layers = (partner, other)
    grads, spread, to_partner, to_other = grad_call(far(coords), parent, mine, theirs, down, *layers)
    partner, other = over_core(to_partner), over_other(to_other)
    inner = (shifts, weights, inner_call(shifts, weights))
    kept, sent, keep = main_call(
        coords, parent, near, partner, other, inner, down, grads, spread
    )

    got = over_core(sent)
    own = stage(add_halves, (kept, got), [sds((36, 64, 128), BF)])[0]
    gots = over_plane(own.reshape(16, 144, 128))
    partial_grad, token = input_call(near, grads, partner, other, far(conv_weight), own, 0)
    own = stage(add_sixteen, (gots,), [sds((144, 128), F32)], (token,))[0]
    gots = [over_y(own, k) for k in (1, 2, 3)]
    coarse, token = coarse_call(coords, keep, got, own)
    shares = stage(
        add_in_order, (own, *gots), [sds((16, 144, 128), BF)], (token,),
        scratch=[pltpu.VMEM((4, 144, 128), F32)],
    )[0]

    own = over_plane(shares).reshape(36, 64, 128)
    input_grad, token = input_call(near, grads, partner, other, far(conv_weight), shares, 1, partial_grad)
    own = after_call(own, token)
    got = over_core(own)
    halves = write_call(own)
    conv_grad, down_grad = write_call(got, halves, own=False)
    whole = (1, 1, 16, 16, 16, 128)
    return (
        coarse.reshape(whole),
        input_grad.reshape(whole),
        conv_grad.reshape(3, 3, 3, 128, 128),
        down_grad.reshape(2, 2, 2, 128, 128),
    )


def solution(mesh):
    sizes = (mesh.devices.shape[0], 4, 4, 2)
    mesh = jax.sharding.Mesh(mesh.devices.reshape(sizes), ("dp", "z", "x", "core"))
    region = ("z", "x", "core")
    bricks = P("dp", region, None, None, None, None)
    rows = P("dp", region, None)
    return jax.shard_map(
        local,
        mesh=mesh,
        in_specs=(bricks, P(), P(), bricks, rows, rows, P("dp", region)),
        out_specs=(bricks, bricks, P(), P()),
        check_vma=False,
    )
```

```python
import functools
import jax
import jax.numpy as jnp
from jax import lax
from jax.experimental import pallas as pl
from jax.experimental.pallas import tpu as pltpu
from jax.sharding import PartitionSpec as P

BF, F32 = jnp.bfloat16, jnp.float32
SMEM = pl.BlockSpec(memory_space=pltpu.SMEM)
VMEM = pl.BlockSpec(memory_space=pltpu.VMEM)
NN = (((1,), (0,)), ((), ()))
NT = (((1,), (1,)), ((), ()))
TN = (((0,), (0,)), ((), ()))


def dot(lhs, rhs, dims):
    return lax.dot_general(lhs, rhs, dims, preferred_element_type=F32)


def z_index(rows):
    return lax.broadcasted_iota(jnp.int32, (rows, 128), 0) % 16


def lay_interior(field_ref, shifts_ref, start=0, stop=16, base=1):
    z = z_index(256)

    for x in range(start, stop):
        plain = field_ref[x].reshape(256, 128)
        wide = plain.astype(F32)
        lower = jnp.where(z == 0, 0.0, pltpu.roll(wide, 1, 0)).astype(BF)
        upper = jnp.where(z == 15, 0.0, pltpu.roll(wide, 255, 0)).astype(BF)
        for c, value in enumerate((lower, plain, upper)):
            rows = value.reshape(8, 2, 16, 128)
            shifts_ref[c, x + base, 0:8, 1] = rows[:, 0]
            shifts_ref[c, x + base, 1:9, 0] = rows[:, 1]
            shifts_ref[c, x + base, 0, 0] = jnp.zeros((16, 128), BF)
            shifts_ref[c, x + base, 8, 1] = jnp.zeros((16, 128), BF)


def lay_slab(layer, flag, slab_ref):
    def three(value, b):
        rows = value.shape[0] * 16
        wide = value.astype(F32).reshape(rows, 128)
        z = z_index(rows)
        below, same, above = (flag(b, c) for c in (-1, 0, 1))
        lower = jnp.where(
            z == 0, pltpu.roll(wide, rows - 15, 0) * below, pltpu.roll(wide, 1, 0) * same
        )
        upper = jnp.where(
            z == 15, pltpu.roll(wide, 15, 0) * above, pltpu.roll(wide, rows - 1, 0) * same
        )
        return [v.astype(BF) for v in (lower, wide * same, upper)]

    for c, value in enumerate(three(layer, 0)):
        rows = value.reshape(8, 2, 16, 128)
        slab_ref[c, 0:8, 1] = rows[:, 0]
        slab_ref[c, 1:9, 0] = rows[:, 1]
    for c, value in enumerate(three(layer[15:16], -1)):
        slab_ref[c, 0, 0] = value.reshape(16, 128)
    for c, value in enumerate(three(layer[0:1], 1)):
        slab_ref[c, 8, 1] = value.reshape(16, 128)


def near_flag(near_ref, first):
    return lambda b, c: (near_ref[first + 3 * (b + 1) + c + 1] >= 0).astype(F32)


def window(shifts_ref, c, x, count):
    return jnp.concatenate(
        [
            shifts_ref[c, pl.ds(x, count), t // 2 : t // 2 + 8, t % 2].reshape(count * 128, 128)
            for t in range(4)
        ],
        axis=1,
    )


def prepare_kernel(
    cotangent_hbm, down_hbm, field_hbm, conv_hbm,
    mine_ref, down_ref, partner_ref, other_ref, shifts_ref, weights_ref,
    field_ref, conv_ref, sems,
):
    upper = lax.axis_index("core")
    fetches = [
        pltpu.make_async_copy(
            field_hbm.at[pl.ds(4 * k, 4)], field_ref.at[pl.ds(4 * k, 4)], sems.at[14 + k]
        )
        for k in range(4)
    ]
    conv_copy = pltpu.make_async_copy(conv_hbm, conv_ref, sems.at[18])
    for copy in (*fetches, conv_copy):
        copy.start()
    copies = [
        pltpu.make_async_copy(field_hbm.at[15 - 15 * upper], partner_ref, sems.at[0]),
        pltpu.make_async_copy(field_hbm.at[15 * upper], other_ref, sems.at[1]),
    ]
    for k in range(4):
        copies.append(
            pltpu.make_async_copy(
                cotangent_hbm.at[pl.ds(8 * upper + 2 * k, 2)], mine_ref.at[2 * k : 2 * k + 2],
                sems.at[2 + k],
            )
        )
    for p in range(2):
        for q in range(2):
            for r in range(2):
                at = 2 * p + q
                rows, columns = slice(128 * at, 128 * at + 128), slice(128 * r, 128 * r + 128)
                copies.append(
                    pltpu.make_async_copy(
                        down_hbm.at[p, q, r], down_ref.at[rows, columns], sems.at[6 + 2 * at + r]
                    )
                )
    for copy in copies:
        copy.start()
    for k in range(4):
        fetches[k].wait()
        lay_interior(field_ref, shifts_ref, 4 * k, 4 * k + 4, 0)
    conv_copy.wait()
    lay_weights(conv_ref, weights_ref)
    for copy in copies:
        copy.wait()


def grad_kernel(
    coords_ref, parent_ref, mine_ref, theirs_ref, down_ref, partner_ref, other_ref,
    grads_ref, spread_ref, to_partner_ref, to_other_ref, wide_ref,
):
    x, oy, oz = coords_ref[0], coords_ref[1] % 2, coords_ref[2] % 2
    is_own = parent_ref[0] == x
    down = down_ref[...]
    to_partner_ref[0] = partner_ref[...]
    to_other_ref[0] = other_ref[...]
    wide_ref[...] = jnp.zeros_like(wide_ref)
    for i in range(8):
        mine = mine_ref[i, pl.ds(8 * oy, 8)].astype(F32)
        theirs = theirs_ref[8 * (x % 2) + i, pl.ds(8 * oy, 8)].astype(F32)
        both = jnp.where(is_own, mine, theirs)
        part = jnp.where(oz == 0, both[:, 0:8], both[:, 8:16]).reshape(64, 128)
        wide_ref[i, pl.ds(0, 64, stride=2), :] = part
    for i in range(8):
        even = wide_ref[i]
        spread = jnp.concatenate([even, pltpu.roll(even, 1, 0)], axis=1).astype(BF)
        spread_ref[i] = spread
    for first in (0, 4):
        spread = spread_ref[first : first + 4].reshape(512, 256)
        grads = dot(spread, down, NT).astype(BF)
        for p in range(2):
            for q in range(2):
                at = (2 * p + q) * 128
                part = grads[:, at : at + 128].reshape(4, 8, 16, 128)
                for i in range(4):
                    grads_ref[2 * (first + i) + p, :, q] = part[i]
    upper = x % 2
    to_partner_ref[1] = grads_ref[15 - 15 * upper]
    to_other_ref[1] = grads_ref[15 * upper]


def lay_weights(conv_ref, weights_ref):
    zero = jnp.zeros((128, 128), BF)
    for a in range(3):
        for c in range(3):
            for t in range(4):
                for s in range(2):
                    weights_ref[a, c, t * 128 : t * 128 + 128, s * 128 : s * 128 + 128] = (
                        conv_ref[a, t - s, c] if 0 <= t - s <= 2 else zero
                    )


def inner_kernel(shifts_ref, weights_ref, outputs_ref):
    for first, count in ((1, 7), (8, 7)):
        acc = None
        for a in range(3):
            for c in range(3):
                part = dot(window(shifts_ref, c, first + a - 1, count), weights_ref[a, c], NN)
                acc = part if acc is None else acc + part
        for s in range(2):
            field = center(shifts_ref, first, count, s)
            outputs_ref[first : first + count, :, s] = (
                acc[:, s * 128 : s * 128 + 128].reshape(count, 8, 16, 128) + field
            ).astype(BF)


def center(shifts_ref, x, count, s):
    return shifts_ref[1, x : x + count, s : s + 8, 1 - s].astype(F32)


def taps(rows):
    return jnp.concatenate(
        [rows[t // 2 : t // 2 + 8, t % 2].reshape(128, 128) for t in range(4)], axis=1
    )


def main_kernel(
    coords_ref, parent_ref, near_ref, partner_ref, other_ref, shifts_ref, weights_ref,
    inner_ref, down_ref, grads_ref, spread_ref,
    kept_rows_ref, sent_ref, keep_ref, low_shifts_ref, high_shifts_ref, edges_ref, sums_ref,
):
    x, oy, oz = coords_ref[0], coords_ref[1] % 2, coords_ref[2] % 2
    first_core = x % 2 == 0
    kept = (parent_ref[0] == x).astype(F32)

    def part_rows(tap, rows):
        kept_rows_ref[tap] = jnp.where(first_core, rows[0:64], rows[64:128])
        sent_ref[tap] = jnp.where(first_core, rows[64:128], rows[0:64]).astype(BF)

    kept_rows_ref[35] = jnp.zeros((64, 128), F32)
    sent_ref[35] = jnp.zeros((64, 128), BF)
    sent_ref[52] = jnp.full((64, 128), oy, jnp.int32).astype(F32).astype(BF)
    partner, other = partner_ref[0].astype(F32), other_ref[0].astype(F32)
    low = jnp.where(first_core, other, partner).reshape(16, 16, 128)
    high = jnp.where(first_core, partner, other).reshape(16, 16, 128)
    lay_slab(low, near_flag(near_ref, 0), low_shifts_ref)
    lay_slab(high, near_flag(near_ref, 17), high_shifts_ref)

    accs = [None, None]
    for a in range(3):
        for c in range(3):
            for k, rows in enumerate((
                low_shifts_ref[c] if a == 0 else shifts_ref[c, a - 1],
                high_shifts_ref[c] if a == 2 else shifts_ref[c, 14 + a],
            )):
                part = dot(taps(rows), weights_ref[a, c], NN)
                accs[k] = part if accs[k] is None else accs[k] + part
    for s in range(2):
        for k in range(2):
            value = accs[k][:, s * 128 : s * 128 + 128].reshape(8, 16, 128)
            edges_ref[k, :, s] = (value + center(shifts_ref, 15 * k, 1, s)[0]).astype(BF)

    down = down_ref[...]

    def corner(i, p, q):
        at = 2 * i + p
        rows = edges_ref[at // 15, :, q] if at in (0, 15) else inner_ref[at, :, q]
        return rows.reshape(128, 128)

    for i in range(8):
        corners = jnp.concatenate([corner(i, p, q) for p in range(2) for q in range(2)], axis=1)
        sums = dot(corners, down, NN)
        sums_ref[i, 0] = sums[:, 0:128]
        sums_ref[i, 1] = sums[:, 128:256]
        block = sums_ref[i, 0, pl.ds(0, 64, stride=2), :] + sums_ref[i, 1, pl.ds(1, 64, stride=2), :]
        block = block.reshape(8, 8, 128)
        none = jnp.zeros_like(block)
        low = jnp.where(oz == 0, block, none)
        high = jnp.where(oz == 0, none, block)
        placed = jnp.concatenate([low, high], axis=1).reshape(128, 128)
        keep_ref[i] = (placed * kept).astype(BF).reshape(8, 16, 128)
        away = (placed * (1 - kept)).astype(BF)
        sent_ref[36 + 2 * i] = away[0:64]
        sent_ref[37 + 2 * i] = away[64:128]

    spread = spread_ref[...].reshape(1024, 256)
    for p in range(2):
        for q in range(2):
            rows = jnp.concatenate([corner(i, p, q) for i in range(8)], axis=0)
            result = dot(rows, spread, TN) * (1.0 / 1024)
            part_rows(27 + 4 * p + 2 * q, result[:, 0:128])
            part_rows(28 + 4 * p + 2 * q, result[:, 128:256])

    pair = jnp.concatenate([grads_ref[:, :, s].reshape(2048, 128) for s in range(2)], axis=1)
    for a in range(3):
        for c in range(3):
            if a == 0:
                rows = jnp.concatenate(
                    [taps(low_shifts_ref[c]), window(shifts_ref, c, 0, 15)], axis=0
                )
            elif a == 1:
                rows = window(shifts_ref, c, 0, 16)
            else:
                rows = jnp.concatenate(
                    [window(shifts_ref, c, 1, 15), taps(high_shifts_ref[c])], axis=0
                )
            result = dot(rows, pair, TN) * (1.0 / 1024)
            for b in range(3):
                part_rows(
                    9 * a + 3 * b + c,
                    result[b * 128 : b * 128 + 128, 0:128]
                    + result[b * 128 + 128 : b * 128 + 256, 128:256],
                )


def input_kernel(near_ref, field_ref, partner_ref, other_ref, conv_hbm, *refs, half, tile=4):
    result_ref, token_ref, shifts_ref, weights_ref, held_ref, conv_ref, sems = refs[-7:]
    token_ref[...] = jnp.zeros_like(token_ref)
    conv_copies = [
        pltpu.make_async_copy(conv_hbm.at[a], conv_ref.at[a], sems.at[2 + a]) for a in range(3)
    ]
    for copy in conv_copies:
        copy.start()
    lay = functools.partial(lay_interior, field_ref, shifts_ref, base=1 - 8 * half)
    if half == 0:
        lay(0, 5)
    else:
        lay(7, 13)
    layer = jnp.where(
        lax.axis_index("core") == half, other_ref[1].astype(F32), partner_ref[1].astype(F32)
    )
    def lay_edge():
        lay_slab(
            layer.reshape(16, 16, 128), near_flag(near_ref, 17 * half), shifts_ref.at[:, 9 * half]
        )

    if half == 0:
        lay_edge()
    zero = jnp.zeros((128, 128), BF)
    for a in (2, 1, 0):
        conv_copies[2 - a].wait()
        for c in range(3):
            for t in range(4):
                for s in range(2):
                    weights_ref[a, c, s * 128 : s * 128 + 128, t * 128 : t * 128 + 128] = (
                        conv_ref[2 - a, 2 - t + s, 2 - c] if 0 <= t - s <= 2 else zero
                    )
    copies = []
    for step in range(8 // tile):
        first = step * tile
        if step == 1 and half == 0:
            lay(5, 9)
        if step == 1 and half == 1:
            lay(13, 16)
            lay_edge()
        acc = None
        for a in range(3):
            for c in range(3):
                part = dot(window(shifts_ref, c, first + a, tile), weights_ref[a, c], NT)
                acc = part if acc is None else acc + part
        here = 8 * half + first
        for s in range(2):
            field = field_ref[here : here + tile, :, s].astype(F32)
            held_ref[first : first + tile, :, s] = (
                acc[:, s * 128 : s * 128 + 128].reshape(tile, 8, 16, 128) + field
            ).astype(BF)
        copy = pltpu.make_async_copy(
            held_ref.at[pl.ds(first, tile)], result_ref.at[pl.ds(here, tile)], sems.at[step]
        )
        copy.start()
        copies.append(copy)
    for copy in copies:
        copy.wait()


def coarse_kernel(coords_ref, keep_ref, got_ref, coarse_ref, token_ref, held_ref, sems):
    token_ref[...] = jnp.zeros_like(token_ref)
    upper, oy = coords_ref[0] % 2, coords_ref[1] % 2
    there = got_ref[52, 0:16].astype(F32)
    none = jnp.zeros((8, 16, 128), BF)
    for i in range(8):
        rows = jnp.concatenate([got_ref[36 + 2 * i], got_ref[37 + 2 * i]], axis=0)
        rows = rows.reshape(8, 16, 128).astype(F32)
        held_ref[0, i, pl.ds(8 * oy, 8)] = keep_ref[i]
        held_ref[0, i, pl.ds(8 - 8 * oy, 8)] = none
        held_ref[1, i, 0:8] = jnp.where(there == 0, rows, 0.0).astype(BF)
        held_ref[1, i, 8:16] = jnp.where(there == 1, rows, 0.0).astype(BF)
    keep = pltpu.make_async_copy(held_ref.at[0], coarse_ref.at[pl.ds(8 * upper, 8)], sems.at[0])
    got = pltpu.make_async_copy(held_ref.at[1], coarse_ref.at[pl.ds(8 - 8 * upper, 8)], sems.at[1])
    keep.start()
    got.start()
    keep.wait()
    got.wait()


ANY = pl.BlockSpec(memory_space=pl.ANY)
HBM = pl.BlockSpec(memory_space=pltpu.HBM)
TOKEN = jax.ShapeDtypeStruct((8, 128), F32)
sds = jax.ShapeDtypeStruct


def call(kernel, ins, outs, scratch=(), flops=0, moved=1 << 20, limit=8, out=VMEM, **kw):
    return pl.pallas_call(
        kernel,
        in_specs=ins,
        out_specs=[VMEM if shape is TOKEN else out for shape in outs],
        out_shape=outs,
        scratch_shapes=list(scratch),
        cost_estimate=pl.CostEstimate(flops=flops, bytes_accessed=moved, transcendentals=0),
        compiler_params=pltpu.CompilerParams(vmem_limit_bytes=limit << 20),
        **kw,
    )


def prepare_call(cotangent, down, field, conv):
    layer = sds((8, 2, 16, 128), BF)
    return call(
        prepare_kernel, [HBM] * 4,
        [sds((8, 16, 16, 128), BF), sds((512, 256), BF), layer, layer,
         sds((3, 16, 9, 2, 16, 128), BF), sds((3, 3, 512, 256), BF)],
        [pltpu.VMEM((16, 8, 2, 16, 128), BF), pltpu.VMEM((3, 3, 3, 128, 128), BF),
         pltpu.SemaphoreType.DMA((19,))], moved=4 << 20,
    )(cotangent, down, field, conv)


def grad_call(coords, parent, mine, theirs, down, partner, other):
    layers = sds((2, 8, 2, 16, 128), BF)
    return call(
        grad_kernel, [SMEM] * 2 + [VMEM] * 5,
        [sds((16, 8, 2, 16, 128), BF), sds((8, 128, 256), BF), layers, layers],
        [pltpu.VMEM((8, 128, 128), F32)], flops=2 * 2**27, moved=4 << 20,
    )(coords, parent, mine, theirs, down, partner, other)


def inner_call(shifts, weights):
    return call(
        inner_kernel, [VMEM] * 2, [sds((16, 8, 2, 16, 128), BF)],
        flops=2 * 9 * 2048 * 512 * 256, moved=2 << 20, limit=16,
    )(shifts, weights)[0]


def main_call(coords, parent, near, partner, other, inner, down, grads, spread):
    slab = pltpu.VMEM((3, 9, 2, 16, 128), BF)
    return call(
        main_kernel, [SMEM] * 3 + [VMEM] * 8,
        [sds((36, 64, 128), F32), sds((53, 64, 128), BF), sds((8, 8, 16, 128), BF)],
        [slab, slab, pltpu.VMEM((2, 8, 2, 16, 128), BF), pltpu.VMEM((8, 2, 128, 128), F32)],
        flops=2 * 9 * 2048 * 512 * 256, limit=24,
    )(coords, parent, near, partner, other, *inner, down, grads, spread)


def input_call(near, field, partner, other, conv, after, half, base=None):
    ins, values = [SMEM] + [VMEM] * 3 + [HBM, ANY], [near, field, partner, other, conv, after]
    aliases = {}
    if base is not None:
        ins, values, aliases = ins + [ANY], values + [base], {6: 0}
    return call(
        functools.partial(input_kernel, half=half), ins, [sds((16, 8, 2, 16, 128), BF), TOKEN],
        [pltpu.VMEM((3, 10, 9, 2, 16, 128), BF), pltpu.VMEM((3, 3, 256, 512), BF),
         pltpu.VMEM((8, 8, 2, 16, 128), BF), pltpu.VMEM((3, 3, 3, 128, 128), BF),
         pltpu.SemaphoreType.DMA((5,))],
        flops=9 * 2048 * 512 * 256, limit=24, out=ANY, input_output_aliases=aliases,
    )(*values)


def coarse_call(coords, keep, got, after):
    def kernel(coords_ref, keep_ref, got_ref, after_ref, *refs):
        coarse_kernel(coords_ref, keep_ref, got_ref, *refs)

    return call(
        kernel, [SMEM] + [VMEM] * 2 + [ANY], [sds((16, 16, 16, 128), BF), TOKEN],
        [pltpu.VMEM((2, 8, 16, 16, 128), BF), pltpu.SemaphoreType.DMA((2,))], out=ANY,
    )(coords, keep, got, after)


def add_halves(kept_ref, got_ref, total_ref):
    total_ref[...] = (kept_ref[...] + got_ref[0:36].astype(F32)).astype(BF)


def add_sixteen(got_ref, *refs):
    total = got_ref[0].astype(F32)
    for k in range(1, 16):
        total = total + got_ref[k].astype(F32)
    refs[-1][...] = total


def add_in_order(own_ref, *refs):
    y = lax.axis_index("dp")
    total_ref, slots_ref = refs[-2:]
    for k, ref in enumerate((own_ref, *refs[:3])):
        slots_ref[(y - k + 4) % 4] = ref[...]
    total = ((slots_ref[0] + slots_ref[1]) + (slots_ref[2] + slots_ref[3])).astype(BF)
    for k in range(16):
        total_ref[k] = total


def after_call(value, token):
    def kernel(value_ref, token_ref, same_ref):
        pass

    return call(
        kernel, [ANY] * 2, [sds(value.shape, value.dtype)], out=ANY, input_output_aliases={0: 0},
        moved=1024,
    )(value, token)[0]


def write_half(rows_ref, *refs, own):
    conv_ref, down_ref, token_ref, wide_ref, sems = refs[-5:]
    token_ref[...] = jnp.zeros_like(token_ref)
    core = lax.axis_index("core")
    here = pl.ds(pl.multiple_of(64 * (core if own else 1 - core), 64), 64)
    copies = []
    for k, (start, stop) in enumerate(((0, 9), (9, 18), (18, 27), (27, 35))):
        wide_ref[start:stop] = rows_ref[start:stop].astype(F32)
        if start < 27:
            target = conv_ref.at[start:stop, here]
        else:
            target = down_ref.at[:, here]
        copies.append(pltpu.make_async_copy(wide_ref.at[start:stop], target, sems.at[k]))
        copies[-1].start()
    for copy in copies:
        copy.wait()


def write_call(rows, bases=(), own=True):
    return call(
        functools.partial(write_half, own=own), [VMEM] + [ANY] * len(bases),
        [sds((27, 128, 128), F32), sds((8, 128, 128), F32), TOKEN],
        [pltpu.VMEM((36, 64, 128), F32), pltpu.SemaphoreType.DMA((4,))], out=ANY,
        input_output_aliases={1: 0, 2: 1} if bases else {},
    )(rows, *bases)[:2]


def over_core(value):
    return lax.ppermute(value, "core", [(0, 1), (1, 0)])


def over_y(value, by):
    return lax.ppermute(value, "dp", [(i, (i + by) % 4) for i in range(4)])


def over_plane(value):
    return lax.all_to_all(value, ("z", "x"), 0, 0, tiled=True)


def stage(kernel, values, outs, after=(), scratch=()):
    return call(kernel, [VMEM] * len(values) + [ANY] * len(after), outs, scratch)(*values, *after)


def over_other(value):
    pairs = [(i, i + 1) for i in range(1, 31, 2)] + [(i + 1, i) for i in range(1, 31, 2)]
    return lax.ppermute(value, ("z", "x", "core"), pairs)


def local(features, conv_weight, down_weight, coarse_cotangent, brick_coords, neighbours, parents):
    coords, near, parent = brick_coords.reshape(3), neighbours.reshape(26), parents.reshape(1)
    cotangent = coarse_cotangent.reshape(16, 16, 16, 128)
    theirs = over_core(cotangent)
    field = features.reshape(16, 8, 2, 16, 128)
    far = functools.partial(pltpu.with_memory_space_constraint, memory_space=pltpu.HBM)
    mine, down, partner, other, shifts, weights = prepare_call(
        far(cotangent), far(down_weight), far(field), far(conv_weight)
    )
    layers = (partner, other)
    grads, spread, to_partner, to_other = grad_call(far(coords), parent, mine, theirs, down, *layers)
    partner, other = over_core(to_partner), over_other(to_other)
    inner = (shifts, weights, inner_call(shifts, weights))
    kept, sent, keep = main_call(
        coords, parent, near, partner, other, inner, down, grads, spread
    )

    got = over_core(sent)
    own = stage(add_halves, (kept, got), [sds((36, 64, 128), BF)])[0]
    gots = over_plane(own.reshape(16, 144, 128))
    partial_grad, token = input_call(near, grads, partner, other, far(conv_weight), own, 0)
    coarse, token = coarse_call(coords, keep, got, token)
    own = stage(add_sixteen, (gots,), [sds((144, 128), F32)], (token,))[0]
    gots = [over_y(own, k) for k in (1, 2, 3)]
    shares = stage(
        add_in_order, (own, *gots), [sds((16, 144, 128), BF)],
        scratch=[pltpu.VMEM((4, 144, 128), F32)],
    )[0]

    own = over_plane(shares).reshape(36, 64, 128)
    input_grad, token = input_call(near, grads, partner, other, far(conv_weight), shares, 1, partial_grad)
    own = after_call(own, token)
    got = over_core(own)
    halves = write_call(own)
    conv_grad, down_grad = write_call(got, halves, own=False)
    whole = (1, 1, 16, 16, 16, 128)
    return (
        coarse.reshape(whole),
        input_grad.reshape(whole),
        conv_grad.reshape(3, 3, 3, 128, 128),
        down_grad.reshape(2, 2, 2, 128, 128),
    )


def solution(mesh):
    sizes = (mesh.devices.shape[0], 4, 4, 2)
    mesh = jax.sharding.Mesh(mesh.devices.reshape(sizes), ("dp", "z", "x", "core"))
    region = ("z", "x", "core")
    bricks = P("dp", region, None, None, None, None)
    rows = P("dp", region, None)
    return jax.shard_map(
        local,
        mesh=mesh,
        in_specs=(bricks, P(), P(), bricks, rows, rows, P("dp", region)),
        out_specs=(bricks, bricks, P(), P()),
        check_vma=False,
    )
```
